128 devices in a mesh: seq: 64 (over x_lo, z, y, core), tp: 2 (over x_hi).
Axes of the slice: x: 4 (x_hi: 2, x_lo: 2; x = x_hi * 2 + x_lo), y: 4, z: 4, core: 2. Of those that a mesh axis runs over, the one named last changes fastest.
Arguments:
- tokens: bfloat16 [8192, 2048], P('seq'), may hold values from -6 to 6
- doc_lengths: int32 [2, 4], replicated, may hold values from 1 to 4000, as said below
- attn_gain: bfloat16 [2048], P('seq'), may hold values from 0.5 to 1.5
- q_weight: bfloat16 [2048, 2048], P('seq', 'tp'), may hold values from -0.125 to 0.125
- kv_weight: bfloat16 [2048, 256], P('seq'), may hold values from -0.125 to 0.125
- out_weight: bfloat16 [2048, 2048], P('tp', 'seq'), may hold values from -0.5 to 0.5
- ffn_gain: bfloat16 [2048], P('seq'), may hold values from 0.5 to 1.5
- gate_weight: bfloat16 [2048, 5632], P('seq', 'tp'), may hold values from -0.125 to 0.125
- up_weight: bfloat16 [2048, 5632], P('seq', 'tp'), may hold values from -0.125 to 0.125
- down_weight: bfloat16 [5632, 2048], P('tp', 'seq'), may hold values from -0.078125 to 0.078125
- second_queries: bfloat16 [8192, 2048], P('seq', 'tp'), may hold values from -8 to 8
- out_cotangent: bfloat16 [8192, 2048], P('seq'), may hold values from -6 to 6
- second_cotangent: bfloat16 [8192, 2048], P('seq', 'tp'), may hold values from -6 to 6
Outputs:
- result: float32 [8192, 2048], P('seq')
- second_out: float32 [8192, 2048], P('seq', 'tp')
- tokens_grad: float32 [8192, 2048], P('seq')
- attn_gain_grad: float32 [2048], P('seq')
- q_weight_grad: float32 [2048, 2048], P('seq', 'tp')
- kv_weight_grad: float32 [2048, 256], P('seq')
- out_weight_grad: float32 [2048, 2048], P('tp', 'seq')
- ffn_gain_grad: float32 [2048], P('seq')
- gate_weight_grad: float32 [2048, 5632], P('seq', 'tp')
- up_weight_grad: float32 [2048, 5632], P('seq', 'tp')
- down_weight_grad: float32 [5632, 2048], P('tp', 'seq')
- second_queries_grad: float32 [8192, 2048], P('seq', 'tp')
The draws below stay inside these ranges and needn't reach their ends.
Inputs may be any that keep to these rules, and one draw needn't show every extreme that they name: `doc_lengths`: each row sums to 4096. In each row one document, at a place drawn from the seed, has exactly 4096 - 3 * (32) tokens; the other documents of the row together have (3) * (32) tokens, and one of them has exactly 1.
All inputs are finite; a program needn't handle non-finite values.
Results may differ from the reference program's by a relative error of at most 0.018.
Values may be sent and summed in bfloat16 or wider, within the bound.
No kernel may reach another device: no remote copies, remote signals or barrier semaphores. Data moves between devices by JAX's collectives and lax.ppermute only.
A program may use at most 256 MiB of HBM per device.

```python
import math
import jax
import jax.numpy as jnp
from jax import lax

D = 2048
HEADS = 16
HD = 128
FF = 5632
TOK_DEV = 128
NDOCS = 4
SEQLEN = 4096
TOKENS = 8192
SEQS = 2


def doc_row(row_key):
    pick_key, size_key, order_key = jax.random.split(row_key, 3)
    quarter = TOK_DEV // 4
    rest_total = (NDOCS - 1) * quarter
    middle = jax.random.randint(size_key, (), 1, quarter + 1)
    short_count = NDOCS - 3
    others = jnp.concatenate([jnp.ones((short_count,), jnp.int32), jnp.stack([middle, rest_total - short_count - middle]).astype(jnp.int32)])
    others = jax.random.permutation(order_key, others)
    longest = jax.random.randint(pick_key, (), 0, NDOCS)
    places = jnp.arange(NDOCS, dtype=jnp.int32)
    source = jnp.clip(places - (places > longest).astype(jnp.int32), 0, NDOCS - 2)
    picked = jnp.take(others, source)
    return jnp.where(places == longest, SEQLEN - rest_total, picked).astype(jnp.int32)


def draw_doc_lengths(key, part):
    key = jax.random.fold_in(key, 7)
    row_keys = jax.random.split(key, SEQS)
    return jax.vmap(doc_row)(row_keys).astype(jnp.int32)


def block_levels(stream_key, dims, cuts, least, largest):
    level = 1.0
    for dim, parts in cuts:
        draws = jax.random.uniform(jax.random.fold_in(jax.random.fold_in(stream_key, 6), dim), (parts,), jnp.float32, least / len(cuts), largest / len(cuts))
        level = level * jnp.repeat(jnp.exp(draws), dims[dim] // parts).reshape((-1,) + (1,) * (len(dims) - 1 - dim))
    return level


def bell_draw(key, shape, spread, limit, shards=(), kind=jnp.bfloat16):
    values = spread * jax.random.normal(key, shape, jnp.float32)
    if shards:
        values = values * block_levels(key, shape, shards, -0.22, 0.18)
    return jnp.clip(values, -limit, limit).astype(kind)


def setup_inputs(seed: int = 0) -> dict:
    splits = jax.random.split(jax.random.key(seed), 14)
    tokens = bell_draw(splits[0], (TOKENS, D), 1.0, 6.0, ((0, 64),))
    doc_lengths = draw_doc_lengths(jax.random.fold_in(splits[13], 71), 0)
    attn_gain = jnp.clip(1.0 + 0.1 * jax.random.normal(splits[2], (D,), jnp.float32), 0.5, 1.5).astype(jnp.bfloat16)
    q_weight = bell_draw(splits[3], (D, HEADS * HD), D ** -0.5, 0.125, ((0, 64), (1, 2)))
    kv_weight = bell_draw(splits[4], (D, 2 * HD), D ** -0.5, 0.125, ((0, 64),))
    out_weight = bell_draw(splits[5], (HEADS * HD, D), HD ** -0.5, 0.5, ((0, 2), (1, 64)))
    ffn_gain = jnp.clip(1.0 + 0.1 * jax.random.normal(splits[6], (D,), jnp.float32), 0.5, 1.5).astype(jnp.bfloat16)
    gate_weight = bell_draw(splits[7], (D, FF), D ** -0.5, 0.125, ((0, 64), (1, 2)))
    up_weight = bell_draw(splits[8], (D, FF), D ** -0.5, 0.125, ((0, 64), (1, 2)))
    down_weight = bell_draw(splits[9], (FF, D), FF ** -0.5, 0.078125, ((0, 2), (1, 64)))
    second_queries = bell_draw(splits[10], (TOKENS, HEADS * HD), 1.5, 8.0, ((0, 64), (1, 2)))
    out_cotangent = bell_draw(splits[11], (TOKENS, D), 1.0, 6.0, ((0, 64),))
    second_cotangent = bell_draw(splits[12], (TOKENS, HEADS * HD), 1.0, 6.0, ((0, 64), (1, 2)))
    return dict(tokens=tokens, doc_lengths=doc_lengths, attn_gain=attn_gain, q_weight=q_weight, kv_weight=kv_weight, out_weight=out_weight, ffn_gain=ffn_gain, gate_weight=gate_weight, up_weight=up_weight, down_weight=down_weight, second_queries=second_queries, out_cotangent=out_cotangent, second_cotangent=second_cotangent)


@jax.custom_vjp
def low(v):
    return lax.optimization_barrier(v.astype(jnp.bfloat16)).astype(jnp.float32)

@jax.custom_vjp
def low_back(v):
    return v

def low_keep(v):
    return (low(v), None)

def low_pass(kept, grad):
    return (grad,)

def back_keep(v):
    return (v, None)

def back_low(kept, grad):
    return (low(grad),)
low.defvjp(low_keep, low_pass)
low_back.defvjp(back_keep, back_low)
HIGH = lax.Precision.HIGHEST
norm_eps = 1e-05
rope_base = 10000.0
masked_fill = -1e+30

def doc_layout(doc_lengths, first_index, count, seq_len):
    token_index = (first_index + jnp.arange(count, dtype=jnp.int32)).astype(jnp.int32)
    seq_index = (token_index // seq_len).astype(jnp.int32)
    place = (token_index - seq_index * seq_len).astype(jnp.int32)
    seq_count = doc_lengths.shape[0]
    doc_count = doc_lengths.shape[1]
    picked = (seq_index[:, None] == jnp.arange(seq_count, dtype=jnp.int32)[None, :]).astype(jnp.int32)
    row_lengths = lax.optimization_barrier(jnp.sum(picked[:, :, None] * doc_lengths[None, :, :], axis=1)).astype(jnp.int32)
    row_ends = jnp.cumsum(row_lengths, axis=1).astype(jnp.int32)
    passed = (place[:, None] >= row_ends).astype(jnp.int32)
    segment = (seq_index * doc_count + lax.optimization_barrier(jnp.sum(passed, axis=1))).astype(jnp.int32)
    begins = lax.optimization_barrier(jnp.sum(passed * row_lengths, axis=1)).astype(jnp.int32)
    return (segment, (place - begins).astype(jnp.int32))

def rotate(values_in, positions, sign):
    half_dim = values_in.shape[-1] // 2
    freq_index = jnp.arange(half_dim, dtype=jnp.float32)
    inverse_freq = jnp.exp(freq_index * (-2.0 * math.log(rope_base) / values_in.shape[-1]))
    angles = positions.astype(jnp.float32)[:, None] * inverse_freq[None, :]
    shape_out = (angles.shape[0],) + (1,) * (values_in.ndim - 2) + (half_dim,)
    cosine = jnp.cos(angles).reshape(shape_out)
    sine = (sign * jnp.sin(angles)).reshape(shape_out)
    first_half = values_in[..., :half_dim]
    second_half = values_in[..., half_dim:]
    return jnp.concatenate([first_half * cosine - second_half * sine, second_half * cosine + first_half * sine], axis=-1)

def rms_norm(values_in, gain):
    inverse = lax.rsqrt(lax.optimization_barrier(jnp.mean(values_in * values_in, axis=-1, keepdims=True)) + norm_eps)
    return values_in * inverse * gain

def attend(queries, keys, values, segment):
    all_tokens = queries.shape[0]
    head_count = queries.shape[1]
    head_dim = queries.shape[2]
    query_block = min(128, all_tokens)
    block_count = all_tokens // query_block
    key_index = jnp.arange(all_tokens, dtype=jnp.int32)
    score_scale = head_dim ** (-0.5)

    def one_block(block_args):
        block_query, block_segment, block_index = block_args
        scores = jnp.einsum('thd,sd->ths', block_query, keys, precision=HIGH) * score_scale
        scores = low_back(scores)
        allowed = (block_segment[:, None] == segment[None, :]) & (key_index[None, :] <= block_index[:, None])
        allowed = allowed[:, None, :]
        masked = jnp.where(allowed, scores, masked_fill)
        row_top = lax.optimization_barrier(jnp.max(masked, axis=-1, keepdims=True))
        weights = jnp.where(allowed, jnp.exp(masked - row_top), 0.0)
        probs = weights / lax.optimization_barrier(jnp.sum(weights, axis=-1, keepdims=True))
        probs_low = low(probs)
        return jnp.einsum('ths,sd->thd', probs_low, values, precision=HIGH)
    blocks = (queries.reshape(block_count, query_block, head_count, head_dim), segment.reshape(block_count, query_block), key_index.reshape(block_count, query_block))
    mixed = lax.map(jax.checkpoint(one_block), blocks)
    return mixed.reshape(all_tokens, head_count, head_dim)

def forward(inputs, attn_gain, q_weight, kv_weight, out_weight, ffn_gain, gate_weight, up_weight, down_weight, second_queries, segment, positions):
    all_tokens = inputs.shape[0]
    head_dim = kv_weight.shape[1] // 2
    head_count = q_weight.shape[1] // head_dim
    normed = low(rms_norm(inputs, attn_gain))
    queries = low_back(jnp.dot(normed, q_weight, precision=HIGH))
    keyval = jnp.dot(normed, kv_weight, precision=HIGH)
    key_pre = low_back(keyval[:, :head_dim])
    value_rows = low(low_back(keyval[:, head_dim:]))
    query_rot = low(rotate(queries.reshape(all_tokens, head_count, head_dim), positions, 1.0))
    key_rot = low(rotate(key_pre, positions, 1.0))
    both_sets = jnp.concatenate([query_rot, second_queries.reshape(all_tokens, head_count, head_dim)], axis=1)
    mixed = attend(both_sets, key_rot, value_rows, segment)
    attended = low(low_back(mixed[:, :head_count].reshape(all_tokens, head_count * head_dim)))
    second_out = mixed[:, head_count:].reshape(all_tokens, head_count * head_dim)
    branch = low_back(jnp.dot(attended, out_weight, precision=HIGH))
    resid = inputs + branch
    normed2 = low(rms_norm(resid, ffn_gain))
    gate_pre = low_back(jnp.dot(normed2, gate_weight, precision=HIGH))
    up_pre = low_back(jnp.dot(normed2, up_weight, precision=HIGH))
    hidden = low(jax.nn.silu(gate_pre) * up_pre)
    result = resid + jnp.dot(hidden, down_weight, precision=HIGH)
    return (result, second_out)

def reference(tokens, doc_lengths, attn_gain, q_weight, kv_weight, out_weight, ffn_gain, gate_weight, up_weight, down_weight, second_queries, out_cotangent, second_cotangent):
    seq_count = TOKENS // SEQLEN
    group_seqs = math.gcd(seq_count, max(1, 4096 // SEQLEN))
    group_tokens = group_seqs * SEQLEN
    group_count = TOKENS // group_tokens
    weights = [arr.astype(jnp.float32) for arr in (attn_gain, q_weight, kv_weight, out_weight, ffn_gain, gate_weight, up_weight, down_weight)]
    query_width = second_queries.shape[1]

    def one_group(totals, item):
        group_inputs, group_queries, group_cot, group_second_cot, group_index = item
        segment, positions = doc_layout(doc_lengths, group_index * group_tokens, group_tokens, SEQLEN)

        def run(inputs, gain_one, weight_q, weight_kv, weight_out, gain_two, weight_gate, weight_up, weight_down, queries_two):
            return forward(inputs, gain_one, weight_q, weight_kv, weight_out, gain_two, weight_gate, weight_up, weight_down, queries_two, segment, positions)
        outputs, pullback = jax.vjp(run, group_inputs.astype(jnp.float32), *weights, group_queries.astype(jnp.float32))
        grads = pullback((group_cot.astype(jnp.float32), group_second_cot.astype(jnp.float32)))
        new_totals = tuple((total + grad for total, grad in zip(totals, grads[1:9])))
        return (new_totals, (outputs[0], outputs[1], grads[0], grads[9]))
    start_totals = tuple((jnp.zeros_like(weight) for weight in weights))
    group_items = (tokens.reshape(group_count, group_tokens, D), second_queries.reshape(group_count, group_tokens, query_width), out_cotangent.reshape(group_count, group_tokens, D), second_cotangent.reshape(group_count, group_tokens, query_width), jnp.arange(group_count, dtype=jnp.int32))
    totals, stacked = lax.scan(one_group, start_totals, group_items)
    result = stacked[0].reshape(TOKENS, D)
    second_out = stacked[1].reshape(TOKENS, query_width)
    tokens_grad = stacked[2].reshape(TOKENS, D)
    second_queries_grad = stacked[3].reshape(TOKENS, query_width)
    return (result, second_out, tokens_grad, totals[0], totals[1], totals[2], totals[3], totals[4], totals[5], totals[6], totals[7], second_queries_grad)
```

```python
import functools
import math

import jax
import jax.numpy as jnp
from jax import lax
from jax.experimental import pallas as pl
from jax.experimental.pallas import tpu as pltpu
from jax.sharding import Mesh, PartitionSpec as P

norm_eps = 1e-05
rope_base = 10000.0
masked_fill = -1e30
KEY_BLOCK = 1024
BF = jnp.bfloat16
F32 = jnp.float32
MB = 1024 * 1024


def fetch(block, axis, offset):
    n = lax.axis_size(axis)
    return lax.ppermute(block, axis, [((i + offset) % n, i) for i in range(n)])


def hand(block, axis, offset):
    return fetch(block, axis, -offset)


def in_order(first, mine, other, axis):
    return jnp.where(
        first,
        jnp.concatenate([mine, other], axis=axis),
        jnp.concatenate([other, mine], axis=axis),
    )


X, Z, Y = 0, 1, 2


def gather_first(piece):
    both = jnp.stack([piece, fetch(piece, "x", 1)], axis=1)
    width = piece.shape[-1]
    halves = []
    for h, axis in ((0, "z"), (1, "y")):
        mine = both[h].reshape(-1, width)
        halves.append(jnp.concatenate([mine] + [fetch(mine, axis, d) for d in (1, 2, 3)], axis=0))
    return halves


def gather_second(halves):
    by_z, by_y = halves
    zero = [by_z] + [fetch(by_z, "y", d) for d in (1, 2, 3)]
    return zero + [by_y] + [fetch(by_y, "z", d) for d in (1, 2, 3)]


def group_place(pos_ref, group):
    h, y, z, x = group % 2, group // 2 % 4, group // 8 % 4, group // 32
    dx = lax.rem(x - pos_ref[X] + 2, 2)
    dz = lax.rem(z - pos_ref[Z] + 4, 4)
    dy = lax.rem(y - pos_ref[Y] + 4, 4)
    one, two = (dy, dz) if h == 0 else (dz, dy)
    return h * 4 + one, two * 2 + dx


def turned(pos, act):
    toks, feats = act.shape

    def kernel(pos_ref, act_ref, out_ref):
        for block in range(feats // 128):
            part = act_ref[:, block * 128 : (block + 1) * 128].T
            for k in range(4):
                chunk, at = group_place(pos_ref, block * 4 + k)
                out_ref[chunk, at] = part[k * 32 : (k + 1) * 32]

    return pl.pallas_call(
        kernel,
        in_specs=[
            pl.BlockSpec(memory_space=pltpu.SMEM),
            pl.BlockSpec(memory_space=pltpu.VMEM),
        ],
        out_specs=pl.BlockSpec(memory_space=pltpu.VMEM),
        out_shape=jax.ShapeDtypeStruct((8, 8, 32, toks), act.dtype),
        compiler_params=pltpu.CompilerParams(vmem_limit_bytes=16 * MB),
        cost_estimate=pl.CostEstimate(
            flops=0, bytes_accessed=4 * toks * feats, transcendentals=0
        ),
        name="turned",
    )(pos, act).reshape(8, 256, toks)


def turn_back(pos_ref, wide_ref, out_ref):
    for block in range(16):
        groups = [wide_ref[group_place(pos_ref, block * 4 + k)] for k in range(4)]
        rows = jnp.concatenate(groups, axis=0)
        out_ref[:, block * 128 : (block + 1) * 128] = rows.T.astype(out_ref.dtype)


SMEM_SPEC = pl.BlockSpec(memory_space=pltpu.SMEM)
VMEM_SPEC = pl.BlockSpec(memory_space=pltpu.VMEM)


def project(act, chunks, columns, dtypes, flips):
    toks = act.shape[-1]
    width = sum(columns)

    def kernel(act_ref, *refs):
        weights, outs = refs[:8], refs[8:]
        total = jnp.zeros((toks, width), F32)
        for k in range(8):
            total = total + jnp.dot(
                act_ref[k].T, weights[k][:, :width], preferred_element_type=F32
            )
        begin = 0
        for out, w, flip in zip(outs, columns, flips):
            part = total[:, begin : begin + w]
            out[...] = (part.T if flip else part).astype(out.dtype)
            begin += w

    shapes = [(w, toks) if flip else (toks, w) for w, flip in zip(columns, flips)]
    return pl.pallas_call(
        kernel,
        in_specs=[VMEM_SPEC] * 9,
        out_specs=[VMEM_SPEC] * len(columns),
        out_shape=[jax.ShapeDtypeStruct(s, t) for s, t in zip(shapes, dtypes)],
        compiler_params=pltpu.CompilerParams(vmem_limit_bytes=32 * MB),
        cost_estimate=pl.CostEstimate(
            flops=2 * toks * 2048 * width, bytes_accessed=2 * 2048 * (width + toks), transcendentals=0
        ),
        name="project",
    )(act, *chunks)


def unproject(pos, chunks, sides):
    toks = sides[0][0].shape[0 if sides[0][1] else 1]
    count = len(sides)

    def kernel(pos_ref, *refs):
        rights, weights, out_ref, wide = refs[:count], refs[count : count + 8], refs[-2], refs[-1]
        for k in range(8):
            total = None
            begin = 0
            for right, (side, flipped) in zip(rights, sides):
                w = side.shape[1] if flipped else side.shape[0]
                dims = (((1,), (1 if flipped else 0,)), ((), ()))
                part = lax.dot_general(
                    weights[k][:, begin : begin + w], right[...], dims, preferred_element_type=F32
                )
                total = part if total is None else total + part
                begin += w
            wide[k] = total.reshape(8, 32, toks)
        turn_back(pos_ref, wide, out_ref)

    width = chunks[0].shape[1]
    return pl.pallas_call(
        kernel,
        in_specs=[SMEM_SPEC] + [VMEM_SPEC] * (count + 8),
        out_specs=VMEM_SPEC,
        out_shape=jax.ShapeDtypeStruct((toks, 2048), BF),
        scratch_shapes=[pltpu.VMEM((8, 8, 32, toks), F32)],
        compiler_params=pltpu.CompilerParams(vmem_limit_bytes=32 * MB),
        cost_estimate=pl.CostEstimate(
            flops=2 * toks * 2048 * width, bytes_accessed=2 * 2048 * (width + toks), transcendentals=0
        ),
        name="unproject",
    )(pos, *[s for s, f in sides], *chunks)


TILE = 128


def feed_forward(pos, normed2, cot, chunks):
    toks = normed2.shape[-1]
    tiles = chunks[0].shape[1] // (3 * TILE)
    wide_pair = 2 * TILE

    def kernel(pos_ref, normed_ref, cot_ref, *refs):
        weights, grads = refs[:8], refs[8:16]
        ffn_ref, d_norm_ref = refs[16:18]
        normed_rows, cot_rows, pair_weights, down_weights, pair_side, hidden_side, wide = refs[18:]
        j = pl.program_id(0)

        @pl.when(j == 0)
        def _():
            for k in range(8):
                normed_rows[k] = normed_ref[k].T
                cot_rows[k] = cot_ref[k].T

        pre = jnp.zeros((toks, wide_pair), F32)
        d_hidden = jnp.zeros((toks, TILE), F32)
        for k in range(8):
            pre = pre + jnp.dot(
                normed_rows[k], weights[k][:, :wide_pair], preferred_element_type=F32
            )
            d_hidden = d_hidden + jnp.dot(
                cot_rows[k], weights[k][:, wide_pair:], preferred_element_type=F32
            )
        gate, up = pre[:, :TILE], pre[:, TILE:]
        gate_sig = jax.nn.sigmoid(gate)
        gate_act = gate * gate_sig
        hidden = (gate_act * up).astype(BF)
        d_gate = (d_hidden * up * gate_sig * (1.0 + gate * (1.0 - gate_sig))).astype(BF)
        d_up = (d_hidden * gate_act).astype(BF)
        d_pair = jnp.concatenate([d_gate, d_up], axis=1)
        for k in range(8):
            grads[k][:, :wide_pair] = jnp.dot(
                normed_ref[k], d_pair, preferred_element_type=F32
            ).astype(BF)
            grads[k][:, wide_pair:] = jnp.dot(
                cot_ref[k], hidden, preferred_element_type=F32
            ).astype(BF)
        pair_at = pl.ds(pl.multiple_of(j * wide_pair, wide_pair), wide_pair)
        tile_at = pl.ds(pl.multiple_of(j * TILE, TILE), TILE)
        pair_side[:, pair_at] = d_pair
        hidden_side[:, tile_at] = hidden
        for k in range(8):
            pair_weights[k, :, pair_at] = weights[k][:, :wide_pair]
            down_weights[k, :, tile_at] = weights[k][:, wide_pair:]

        @pl.when(j == tiles - 1)
        def _():
            dims = (((1,), (1,)), ((), ()))
            for out_ref, left, right in (
                (d_norm_ref, pair_weights, pair_side),
                (ffn_ref, down_weights, hidden_side),
            ):
                for k in range(8):
                    wide[k] = lax.dot_general(
                        left[k], right[...], dims, preferred_element_type=F32
                    ).reshape(8, 32, toks)
                turn_back(pos_ref, wide, out_ref)

    whole = pl.BlockSpec((8, 256, toks), lambda j: (0, 0, 0))
    tile = pl.BlockSpec((256, 3 * TILE), lambda j: (0, j))
    rows = pl.BlockSpec((toks, 2048), lambda j: (0, 0))
    width = chunks[0].shape[1]
    outs = pl.pallas_call(
        kernel,
        grid=(tiles,),
        in_specs=[SMEM_SPEC, whole, whole] + [tile] * 8,
        out_specs=[tile] * 8 + [rows] * 2,
        out_shape=[jax.ShapeDtypeStruct((256, width), BF)] * 8
        + [jax.ShapeDtypeStruct((toks, 2048), BF)] * 2,
        scratch_shapes=[
            pltpu.VMEM((8, toks, 256), BF),
            pltpu.VMEM((8, toks, 256), BF),
            pltpu.VMEM((8, 256, tiles * wide_pair), BF),
            pltpu.VMEM((8, 256, tiles * TILE), BF),
            pltpu.VMEM((toks, tiles * wide_pair), BF),
            pltpu.VMEM((toks, tiles * TILE), BF),
            pltpu.VMEM((8, 8, 32, toks), F32),
        ],
        compiler_params=pltpu.CompilerParams(vmem_limit_bytes=56 * MB),
        cost_estimate=pl.CostEstimate(
            flops=6 * toks * 2048 * width, bytes_accessed=4 * 2048 * width, transcendentals=toks * width
        ),
        name="feed_forward",
    )(pos, normed2, cot, *chunks)
    return outs[:8], outs[8], outs[9]


def tiled(gate, up, down):
    lead = gate.shape[:-1]
    parts = [w.reshape(lead + (-1, 1, TILE)) for w in (gate, up, down)]
    return jnp.concatenate(parts, axis=-2).reshape(lead + (-1,))


def untiled(columns):
    lead = columns.shape[:-1]
    parts = columns.reshape(lead + (-1, 3, TILE))
    return [parts[..., i, :].reshape(lead + (-1,)) for i in range(3)]


SEND_ORDER = (1, 5, 3, 7, 2, 6, 0, 4)


def weight_chunks(terms, extra=None):
    lefts = []
    for left, right, flipped in terms:
        if not any(left is l for l in lefts):
            lefts.append(left)
    which = [next(i for i, l in enumerate(lefts) if l is left) for left, r, f in terms]
    widths = [r.shape[0] if f else r.shape[1] for l, r, f in terms]
    total = sum(widths) + (extra.shape[-1] if extra is not None else 0)
    operands = lefts + [r for l, r, f in terms] + ([extra] if extra is not None else [])
    count = len(operands)

    def kernel(*refs):
        ins, outs, slots, sem = refs[:count], refs[count : count + 8], refs[-2], refs[-1]
        copies = []
        for step, chunk in enumerate(SEND_ORDER):
            slot = step % 2
            if step >= 2:
                copies[step - 2].wait()
            begin = 0
            for i, (left, right, flipped) in enumerate(terms):
                dims = (((1,), (1 if flipped else 0,)), ((), ()))
                product = lax.dot_general(
                    ins[which[i]][chunk],
                    ins[len(lefts) + i][...],
                    dims,
                    preferred_element_type=F32,
                )
                slots[slot, :, begin : begin + widths[i]] = product.astype(BF)
                begin += widths[i]
            if extra is not None:
                slots[slot, :, begin:total] = ins[-1][chunk]
            copy = pltpu.make_async_copy(slots.at[slot], outs[chunk], sem.at[slot])
            copy.start()
            copies.append(copy)
        copies[-2].wait()
        copies[-1].wait()

    vmem = pl.BlockSpec(memory_space=pltpu.VMEM)
    flops = 2 * 2048 * 256 * total
    return pl.pallas_call(
        kernel,
        in_specs=[vmem] * count,
        out_specs=[pl.BlockSpec(memory_space=pl.ANY)] * 8,
        out_shape=[jax.ShapeDtypeStruct((256, total), BF)] * 8,
        scratch_shapes=[pltpu.VMEM((2, 256, total), BF), pltpu.SemaphoreType.DMA((2,))],
        compiler_params=pltpu.CompilerParams(vmem_limit_bytes=40 * MB),
        cost_estimate=pl.CostEstimate(
            flops=flops, bytes_accessed=2 * 2048 * total, transcendentals=0
        ),
        name="weight_chunks",
    )(*operands)


def summed(parts):
    total = parts[0].astype(F32)
    for part in parts[1:]:
        total = total + part.astype(F32)
    return total


def scatter_first(chunks):
    got = []
    for h, axis in ((0, "y"), (1, "z")):
        own = chunks[4 * h]
        got.append([own] + [hand(chunks[4 * h + d], axis, d) for d in (1, 2, 3)])
    return got


def scatter_second(got):
    width = got[0][0].shape[-1]
    shares = []
    for h, axis in ((0, "z"), (1, "y")):
        blocks = []
        for d in range(4):
            blocks.append(summed([g[d * 64 : (d + 1) * 64] for g in got[h]]).astype(BF))
        shares.append(
            [blocks[0]] + [hand(blocks[d], axis, d) for d in (1, 2, 3)]
        )
    keep = jnp.stack([summed([b[:32] for b in share]) for share in shares])
    give = jnp.stack([summed([b[32:] for b in share]).astype(BF) for share in shares])
    return keep + fetch(give, "x", 1).astype(F32)


def halves_of_rows(first, both):
    mine = jnp.where(first, both[0], both[1])
    give = jnp.where(first, both[1], both[0])
    return mine, fetch(give, "c", 1)


def allowed_keys(begin, count, info):
    shape = (count, info.shape[1])
    key_place = begin + lax.broadcasted_iota(jnp.int32, shape, 0)
    return (key_place <= info[0:1, :]) & (key_place >= info[1:2, :])


def attend_kernel(bounds, info_ref, qt_ref, k_ref, vt_ref, ot_ref, lse_ref, *, first_set, scale):
    units, head_dim, rows = qt_ref.shape
    at = jnp.where(pl.program_id(0) * units >= first_set, 2, 0)
    info = info_ref[0]

    def step(j, carry):
        begin = pl.multiple_of(j * KEY_BLOCK, KEY_BLOCK)
        keys = k_ref[pl.ds(begin, KEY_BLOCK), :]
        values = vt_ref[:, pl.ds(begin, KEY_BLOCK)]
        allowed = allowed_keys(begin, KEY_BLOCK, info)
        out = []
        for u in range(units):
            top, mass, acc = carry[u]
            scores = jnp.dot(keys, qt_ref[u], preferred_element_type=F32)
            scores = jnp.where(allowed, scores, masked_fill)
            new_top = jnp.maximum(top, jnp.max(scores, axis=0, keepdims=True))
            weights = jnp.exp2((scores - new_top) * scale)
            shrink = jnp.exp2((top - new_top) * scale)
            mass = mass * shrink + jnp.sum(weights, axis=0, keepdims=True)
            acc = acc * shrink + jnp.dot(
                values, weights.astype(BF), preferred_element_type=F32
            )
            out.append((new_top, mass, acc))
        return tuple(out)

    start = (
        jnp.full((1, rows), masked_fill, F32),
        jnp.zeros((1, rows), F32),
        jnp.zeros((head_dim, rows), F32),
    )
    done = lax.fori_loop(bounds[at], bounds[at + 1], step, (start,) * units)
    for u in range(units):
        top, mass, acc = done[u]
        ot_ref[u] = acc / mass
        lse_ref[u] = top * scale + jnp.log2(mass)


def attend(bounds, info, qt, keys, values_t, scale):
    units = 2
    blocks, head_dim, rows = qt.shape
    count = keys.shape[0]
    first_set = blocks // 2
    block = pl.BlockSpec((units, head_dim, rows), lambda i, b: (i, 0, 0))
    return pl.pallas_call(
        functools.partial(attend_kernel, first_set=first_set, scale=scale),
        grid_spec=pltpu.PrefetchScalarGridSpec(
            num_scalar_prefetch=1,
            grid=(blocks // units,),
            in_specs=[
                pl.BlockSpec((1, 2, rows), lambda i, b: (i * units // first_set, 0, 0)),
                block,
                pl.BlockSpec((count, head_dim), lambda i, b: (0, 0)),
                pl.BlockSpec((head_dim, count), lambda i, b: (0, 0)),
            ],
            out_specs=[block, pl.BlockSpec((units, 1, rows), lambda i, b: (i, 0, 0))],
        ),
        out_shape=[
            jax.ShapeDtypeStruct((blocks, head_dim, rows), F32),
            jax.ShapeDtypeStruct((blocks, 1, rows), F32),
        ],
        compiler_params=pltpu.CompilerParams(vmem_limit_bytes=48 * MB),
        cost_estimate=pl.CostEstimate(
            flops=8 * blocks * rows * count * head_dim,
            bytes_accessed=blocks * rows * head_dim * 6 + count * head_dim * 4,
            transcendentals=blocks * rows * count,
        ),
        name="attend",
    )(bounds, info, qt, keys, values_t)


def attend_back_kernel(
    bounds, info_ref, qt_ref, dot_ref, ot_ref, lse_ref, k_ref, kt_ref, v_ref, dqt_ref, dk_ref, dv_ref,
    *, first_set, scale,
):
    units, head_dim, rows = qt_ref.shape

    @pl.when(pl.program_id(0) == 0)
    def _():
        dk_ref[...] = jnp.zeros_like(dk_ref)
        dv_ref[...] = jnp.zeros_like(dv_ref)

    at = jnp.where(pl.program_id(0) * units >= first_set, 2, 0)
    info = info_ref[0]
    queries = [qt_ref[u].T for u in range(units)]
    d_outs = [dot_ref[u].T for u in range(units)]
    deltas = [
        jnp.sum(dot_ref[u].astype(F32) * ot_ref[u], axis=0, keepdims=True) for u in range(units)
    ]

    def step(j, carry):
        begin = pl.multiple_of(j * KEY_BLOCK, KEY_BLOCK)
        part = pl.ds(begin, KEY_BLOCK)
        allowed = allowed_keys(begin, KEY_BLOCK, info)
        out = []
        d_keys = d_values = None
        for u in range(units):
            scores = jnp.dot(k_ref[part, :], qt_ref[u], preferred_element_type=F32)
            d_probs = jnp.dot(v_ref[part, :], dot_ref[u], preferred_element_type=F32)
            probs = jnp.where(allowed, jnp.exp2(scores * scale - lse_ref[u]), 0.0)
            d_scores = (probs * (d_probs - deltas[u])).astype(BF)
            for_keys = jnp.dot(d_scores, queries[u], preferred_element_type=F32)
            for_values = jnp.dot(probs.astype(BF), d_outs[u], preferred_element_type=F32)
            d_keys = for_keys if u == 0 else d_keys + for_keys
            d_values = for_values if u == 0 else d_values + for_values
            out.append(
                carry[u] + jnp.dot(kt_ref[:, part], d_scores, preferred_element_type=F32)
            )
        dk_ref[part, :] += d_keys
        dv_ref[part, :] += d_values
        return tuple(out)

    start = jnp.zeros((head_dim, rows), F32)
    done = lax.fori_loop(bounds[at], bounds[at + 1], step, (start,) * units)
    for u in range(units):
        dqt_ref[u] = done[u]


def attend_back(bounds, info, qt, d_out_t, out_t, lse, keys, keys_t, values, scale):
    units = 2
    blocks, head_dim, rows = qt.shape
    count = keys.shape[0]
    first_set = blocks // 2
    block = pl.BlockSpec((units, head_dim, rows), lambda i, b: (i, 0, 0))
    whole = pl.BlockSpec((count, head_dim), lambda i, b: (0, 0))
    return pl.pallas_call(
        functools.partial(attend_back_kernel, first_set=first_set, scale=scale),
        grid_spec=pltpu.PrefetchScalarGridSpec(
            num_scalar_prefetch=1,
            grid=(blocks // units,),
            in_specs=[
                pl.BlockSpec((1, 2, rows), lambda i, b: (i * units // first_set, 0, 0)),
                block,
                block,
                block,
                pl.BlockSpec((units, 1, rows), lambda i, b: (i, 0, 0)),
                whole,
                pl.BlockSpec((head_dim, count), lambda i, b: (0, 0)),
                whole,
            ],
            out_specs=[block, whole, whole],
        ),
        out_shape=[jax.ShapeDtypeStruct((blocks, head_dim, rows), F32)]
        + [jax.ShapeDtypeStruct((count, head_dim), F32)] * 2,
        compiler_params=pltpu.CompilerParams(vmem_limit_bytes=56 * MB),
        cost_estimate=pl.CostEstimate(
            flops=10 * blocks * rows * count * head_dim,
            bytes_accessed=blocks * rows * head_dim * 12 + count * head_dim * 14,
            transcendentals=blocks * rows * count,
        ),
        name="attend_back",
    )(bounds, info, qt, d_out_t, out_t, lse, keys, keys_t, values)


def doc_starts(lengths, places):
    ends = jnp.cumsum(lengths)
    passed = (places[:, None] >= ends[None, :]).astype(jnp.int32)
    return jnp.sum(passed * lengths[None, :], axis=1)


def rotate_rows(values, cosine, sine):
    half = values.shape[-1] // 2
    one, two = values[..., :half], values[..., half:]
    return jnp.concatenate([one * cosine - two * sine, two * cosine + one * sine], axis=-1)


def rotate_columns(values, cosine, sine):
    half = values.shape[1] // 2
    one, two = values[:, :half], values[:, half:]
    return jnp.concatenate([one * cosine - two * sine, two * cosine + one * sine], axis=1)


def head_blocks(array):
    toks = array.shape[0]
    turned_rows = array.T.reshape(-1, 2, 128, toks)
    return jnp.transpose(turned_rows, (0, 2, 1, 3)).reshape(-1, 128, 2 * toks)


def head_blocks_back(blocks):
    count, head_dim, wide = blocks.shape
    rows = jnp.transpose(blocks.reshape(count, head_dim, 2, wide // 2), (0, 2, 1, 3))
    return rows.reshape(-1, wide // 2).T


def on_device(
    tokens, doc_lengths, attn_gain, q_weight, kv_weight, out_weight, ffn_gain,
    gate_weight, up_weight, down_weight, second_queries, out_cotangent, second_cotangent,
):
    x, z, y, c = (lax.axis_index(a) for a in ("x", "z", "y", "c"))
    first = c == 0
    pos = jnp.stack([x, z, y, c]).astype(jnp.int32)
    toks, width = tokens.shape
    head_dim = kv_weight.shape[1] // 2
    score_scale = head_dim ** (-0.5)
    scale = score_scale * math.log2(math.e)
    rows = q_weight.shape[0]

    def split(weights):
        mine = jnp.concatenate([jnp.where(first, a, b) for a, b in weights], axis=1)
        give = jnp.concatenate([jnp.where(first, b, a) for a, b in weights], axis=1)
        other = fetch(give, "c", 1)
        return jnp.where(first, jnp.stack([mine, other]), jnp.stack([other, mine]))

    def halved(w):
        return w[:, : w.shape[1] // 2], w[:, w.shape[1] // 2 :]

    n_q, n_kv = q_weight.shape[1] // 2, head_dim
    n_out, n_ffn = out_weight.shape[0] // 2, down_weight.shape[0] // 2
    gains = jnp.stack([attn_gain, ffn_gain], axis=1)
    gains = jnp.pad(gains, ((0, 0), (0, 126)))
    one = split([halved(q_weight), halved(kv_weight), (gains, gains)])
    two = split([halved(out_weight.T)])
    ffn_weights = [halved(w) for w in (gate_weight, up_weight, down_weight.T)]
    three = split([tuple(tiled(*[w[i] for w in ffn_weights]) for i in range(2))])

    one_halves = gather_first(one)
    attn_chunks = gather_second(one_halves)
    two_halves = gather_first(two)
    three_halves = gather_first(three)
    out_chunks = gather_second(two_halves)
    ffn_chunks = gather_second(three_halves)

    gain_cols = jnp.stack([w[:, n_q + n_kv : n_q + n_kv + 2] for w in attn_chunks])
    gain_cols = gain_cols.reshape(2, 4, 4, 2, 32, 2)
    here = lambda a, i, n, axis: jnp.take(a, (jnp.arange(n) - i) % n, axis=axis)
    gain_cols = jnp.stack(
        [
            jnp.transpose(here(here(here(gain_cols[0], y, 4, 0), z, 4, 1), x, 2, 2), (2, 1, 0, 3, 4)),
            jnp.transpose(here(here(here(gain_cols[1], z, 4, 0), y, 4, 1), x, 2, 2), (2, 0, 1, 3, 4)),
        ],
        axis=3,
    )
    gain_rows = gain_cols.reshape(-1, 2).T.astype(F32)
    gain_one, gain_two = gain_rows[0:1], gain_rows[1:2]

    def pair_up(own):
        return in_order(first, own, fetch(own, "c", 1), 0)

    def reduce_rows(partial):
        low = partial
        mine = jnp.where(first, low[:toks], low[toks:])
        give = jnp.where(first, low[toks:], low[:toks])
        core_sum = mine.astype(F32) + fetch(give, "c", 1).astype(F32)
        send = core_sum.astype(BF)
        return send.astype(F32) + fetch(send, "t", 1).astype(F32), core_sum

    chip = z * 4 + y
    pair_places = chip * (2 * toks) + jnp.arange(2 * toks, dtype=jnp.int32)
    lengths = jnp.where(x == 0, doc_lengths[0], doc_lengths[1])
    pair_starts = doc_starts(lengths, pair_places)
    positions = (pair_places - pair_starts).astype(F32)
    own_places = jnp.where(first, pair_places[:toks], pair_places[toks:])
    own_starts = jnp.where(first, pair_starts[:toks], pair_starts[toks:])
    info = jnp.stack(
        [
            jnp.stack([pair_places, pair_starts]),
            jnp.stack([jnp.tile(own_places, 2), jnp.tile(own_starts, 2)]),
        ]
    )
    bounds = jnp.stack(
        [
            pair_starts[0] // KEY_BLOCK,
            pair_places[-1] // KEY_BLOCK + 1,
            own_starts[0] // KEY_BLOCK,
            own_places[-1] // KEY_BLOCK + 1,
        ]
    ).astype(jnp.int32)
    inverse_freq = jnp.exp(
        jnp.arange(head_dim // 2, dtype=F32) * (-2.0 * math.log(rope_base) / head_dim)
    )
    angles_t = inverse_freq[:, None] * positions[None, :]
    cos_t, sin_t = jnp.cos(angles_t), jnp.sin(angles_t)
    cos_r, sin_r = cos_t.T, sin_t.T

    inputs = tokens.astype(F32)
    inv_attn = lax.rsqrt(jnp.mean(inputs * inputs, axis=-1, keepdims=True) + norm_eps)
    normed = pair_up((inputs * inv_attn * gain_one).astype(BF))
    normed_t = turned(pos, normed)
    queries_t, keyval = project(normed_t, attn_chunks, (n_q, n_kv), (F32, F32), (True, False))
    query_rot = rotate_columns(queries_t.reshape(-1, head_dim, 2 * toks), cos_t, sin_t).astype(BF)
    kv_own = jnp.where(first, rotate_rows(keyval, cos_r, sin_r), keyval).astype(BF)
    roll = lambda blocks, i: jnp.take(jnp.stack(blocks), (jnp.arange(4) - i) % 4, axis=0)
    kv_z = roll([kv_own] + [fetch(kv_own, "z", d) for d in (1, 2, 3)], z)
    kv_all = roll([kv_z] + [fetch(kv_z, "y", d) for d in (1, 2, 3)], y)
    kv_all = jnp.swapaxes(kv_all, 0, 1).reshape(-1, head_dim)
    kv_other = fetch(kv_all, "c", 1)
    keys = jnp.where(first, kv_all, kv_other)
    values = jnp.where(first, kv_other, kv_all)
    keys_t, values_t = keys.T, values.T
    query_t = jnp.concatenate([query_rot, head_blocks(second_queries)], axis=0)
    out_t, lse = attend(bounds, info, query_t, keys, values_t, scale)
    n_first = query_rot.shape[0]
    second_out = head_blocks_back(out_t[n_first:])
    attended_t = out_t[:n_first].reshape(-1, 2 * toks).astype(BF)

    branch, unused = reduce_rows(unproject(pos, out_chunks, [(attended_t, False)]))
    resid = inputs + branch
    inv_ffn = lax.rsqrt(jnp.mean(resid * resid, axis=-1, keepdims=True) + norm_eps)
    normed2 = pair_up((resid * inv_ffn * gain_two).astype(BF))
    cot = pair_up(out_cotangent)
    ffn_grads, ffn_part, d_norm2_part = feed_forward(
        pos, turned(pos, normed2), turned(pos, cot), ffn_chunks
    )
    ffn_got = scatter_first(ffn_grads)
    d_normed2, unused = reduce_rows(d_norm2_part)
    ffn_sum, unused = reduce_rows(ffn_part)
    result = resid + ffn_sum

    scaled_two = gain_two * d_normed2
    ffn_gain_part = jnp.sum(d_normed2 * resid * inv_ffn, axis=0)
    d_resid = (
        out_cotangent.astype(F32)
        + inv_ffn * scaled_two
        - resid * inv_ffn**3 * jnp.mean(scaled_two * resid, axis=-1, keepdims=True)
    )
    d_branch = pair_up(d_resid.astype(BF))

    d_branch_t = turned(pos, d_branch)
    (d_attended_t,) = project(d_branch_t, out_chunks, (n_out,), (BF,), (True,))
    d_out_t = jnp.concatenate(
        [d_attended_t.reshape(-1, head_dim, 2 * toks), head_blocks(second_cotangent)], axis=0
    )
    out_got = scatter_first(weight_chunks([(d_branch_t, attended_t, True)]))
    d_query_t, d_keys, d_values = attend_back(
        bounds, info, query_t, d_out_t, out_t, lse, keys, keys_t, values, scale
    )
    d_query_t = d_query_t * score_scale
    second_queries_grad = head_blocks_back(d_query_t[n_first:])
    d_queries_t = rotate_columns(d_query_t[:n_first], cos_t, -sin_t).reshape(-1, 2 * toks).astype(BF)

    d_keys = d_keys * score_scale
    kv_mine = jnp.where(first, d_keys, d_values)
    kv_give = jnp.where(first, d_values, d_keys).astype(BF)
    kv_chip = (kv_mine + fetch(kv_give, "c", 1).astype(F32)).reshape(4, 4, 2 * toks, head_dim)

    def pick(array, index):
        return lax.dynamic_index_in_dim(array, lax.rem(index, 4), 0, keepdims=False)

    kv_sum = summed(
        [pick(kv_chip, z)] + [hand(pick(kv_chip, z + d).astype(BF), "z", d) for d in (1, 2, 3)]
    )
    kv_sum = summed(
        [pick(kv_sum, y)] + [hand(pick(kv_sum, y + d).astype(BF), "y", d) for d in (1, 2, 3)]
    )
    d_keyval = jnp.where(first, rotate_rows(kv_sum, cos_r, -sin_r), kv_sum).astype(BF)
    d_norm_part = unproject(pos, attn_chunks, [(d_queries_t, False), (d_keyval, True)])
    d_normed, d_norm_core = reduce_rows(d_norm_part)
    attn_gain_part = jnp.sum(d_norm_core * inputs * inv_attn, axis=0)

    gain_parts = jnp.stack([attn_gain_part, 0.5 * ffn_gain_part]).reshape(2, 2, 4, 4, 2, 32)
    take = lambda a, i, n, axis: jnp.take(a, (i + jnp.arange(n)) % n, axis=axis)
    gain_parts = take(take(take(gain_parts, x, 2, 1), z, 4, 2), y, 4, 3)
    gain_chunks = jnp.stack(
        [
            jnp.transpose(gain_parts[:, :, :, :, 0], (3, 2, 1, 4, 0)),
            jnp.transpose(gain_parts[:, :, :, :, 1], (2, 3, 1, 4, 0)),
        ]
    ).reshape(8, 256, 2)
    gain_chunks = jnp.pad(gain_chunks, ((0, 0), (0, 0), (0, 126))).astype(BF)
    attn_got = scatter_first(
        weight_chunks(
            [(normed_t, d_queries_t, True), (normed_t, d_keyval, False)],
            gain_chunks,
        )
    )
    scaled_one = gain_one * d_normed
    tokens_grad = (
        d_resid
        + inv_attn * scaled_one
        - inputs * inv_attn**3 * jnp.mean(scaled_one * inputs, axis=-1, keepdims=True)
    )

    def whole_rows(got, widths):
        mine, other = halves_of_rows(first, scatter_second(got))
        shares = []
        begin = 0
        for w in widths:
            part = slice(begin, begin + w)
            shares.append((mine[:, part], other[:, part]))
            begin += w
        return shares

    (ffn_s,) = whole_rows(ffn_got, (3 * n_ffn,))
    gate_s, up_s, down_s = zip(*[untiled(side) for side in ffn_s])
    (out_s,) = whole_rows(out_got, (n_out,))
    q_s, kv_s, gain_s = whole_rows(attn_got, (n_q, n_kv, 128))
    joined = lambda s: in_order(first, s[0], s[1], 1)
    kv_gain = jnp.concatenate([joined(kv_s), gain_s[0] + gain_s[1]], axis=1)
    kv_gain = kv_gain + fetch(kv_gain, "t", 1)
    return (
        result,
        second_out,
        tokens_grad,
        kv_gain[:, 2 * n_kv],
        joined(q_s),
        kv_gain[:, : 2 * n_kv],
        joined(out_s).T,
        kv_gain[:, 2 * n_kv + 1],
        joined(gate_s),
        joined(up_s),
        joined(down_s).T,
        second_queries_grad,
    )


def solution(mesh):
    fine = Mesh(mesh.devices.reshape(2, 4, 4, 2, 2), ("x", "z", "y", "c", "t"))
    seq = ("x", "z", "y", "c")
    rows, both, turned_both = P(seq, None), P(seq, "t"), P("t", seq)
    in_specs = (
        rows, P(), P(seq), both, rows, turned_both, P(seq), both, both, turned_both, both, rows, both,
    )
    out_specs = (
        rows, both, rows, P(seq), both, rows, turned_both, P(seq), both, both, turned_both, both,
    )
    return jax.shard_map(
        on_device, mesh=fine, in_specs=in_specs, out_specs=out_specs, check_vma=False
    )
```

```python
import functools
import math

import jax
import jax.numpy as jnp
from jax import lax
from jax.experimental import pallas as pl
from jax.experimental.pallas import tpu as pltpu
from jax.sharding import Mesh, PartitionSpec as P

norm_eps = 1e-05
rope_base = 10000.0
masked_fill = -1e30
KEY_BLOCK = 1024
BF = jnp.bfloat16
F32 = jnp.float32
MB = 1024 * 1024


def fetch(block, axis, offset):
    n = lax.axis_size(axis)
    return lax.ppermute(block, axis, [((i + offset) % n, i) for i in range(n)])


def hand(block, axis, offset):
    return fetch(block, axis, -offset)


def in_order(first, mine, other, axis):
    return jnp.where(
        first,
        jnp.concatenate([mine, other], axis=axis),
        jnp.concatenate([other, mine], axis=axis),
    )


X, Z, Y, CORE = 0, 1, 2, 3


def near_blocks(pair):
    return [fetch(block, axis, d) for block, axis in pair for d in (1, 3)]


def far_blocks(pair, near):
    out = []
    for i, (block, axis) in enumerate(pair):
        after, before = near[2 * i : 2 * i + 2]
        half = block.shape[0] // 2
        far = (fetch(after[:half], axis, 1), fetch(before[half:], axis, 3))
        out.append([block, after, far, before])
    return out[0] + out[1]


def across_x(mine, other):
    rows = mine.shape[0]
    got = fetch(jnp.concatenate([mine, other], axis=0), "x", 1)
    return [
        jnp.concatenate([mine, got[:rows]], axis=0),
        jnp.concatenate([other, got[rows:]], axis=0),
    ]


def first_blocks(pieces):
    return [
        [piece] + [fetch(piece, axis, d) for d in (1, 2, 3)] for piece, axis in zip(pieces, ("z", "y"))
    ]


def joined(blocks, begin, width):
    rows = blocks[0].shape[0]

    def kernel(*refs):
        ins, out, sem = refs[:-2], refs[-2], refs[-1]
        copies = [
            pltpu.make_async_copy(
                ref.at[:, pl.ds(begin, width)], out.at[pl.ds(i * rows, rows)], sem.at[i]
            )
            for i, ref in enumerate(ins)
        ]
        for copy in copies:
            copy.start()
        for copy in copies:
            copy.wait()

    count = len(blocks)
    return call(
        kernel,
        "joined",
        [ANY_SPEC] * count,
        VMEM_SPEC,
        jax.ShapeDtypeStruct((count * rows, width), BF),
        [pltpu.SemaphoreType.DMA((count,))],
    )(*blocks)


def second_pair(halves):
    return [(halves[0], "y"), (halves[1], "z")]


def place_in_chunks(pos_ref, x, z, y, dh):
    dx = lax.rem(x - pos_ref[X] + 2, 2)
    dz = lax.rem(z - pos_ref[Z] + 4, 4)
    dy = lax.rem(y - pos_ref[Y] + 4, 4)
    own = dh == 0
    return dh * 4 + jnp.where(own, dy, dz), jnp.where(own, dz, dy) * 2 + dx


def group_place(pos_ref, group):
    h, y, z, x = group % 2, group // 2 % 4, group // 8 % 4, group // 32
    return place_in_chunks(pos_ref, x, z, y, lax.rem(h + pos_ref[CORE], 2))


SMEM_SPEC = pl.BlockSpec(memory_space=pltpu.SMEM)
VMEM_SPEC = pl.BlockSpec(memory_space=pltpu.VMEM)
ANY_SPEC = pl.BlockSpec(memory_space=pl.ANY)
SMALL = pl.CostEstimate(flops=1024, bytes_accessed=1024, transcendentals=0)


def call(kernel, name, in_specs, out_specs, out_shape, scratch=(), limit=24, grid=None, **more):
    return pl.pallas_call(
        kernel,
        grid=grid or (1,),
        in_specs=in_specs,
        out_specs=out_specs,
        out_shape=out_shape,
        scratch_shapes=scratch,
        compiler_params=pltpu.CompilerParams(vmem_limit_bytes=limit * MB),
        cost_estimate=SMALL,
        name=name,
        **more,
    )


def tie(*arrays):
    return list(lax.optimization_barrier(arrays))


def both_cores(pos_ref, own, other):
    first = pos_ref[CORE] == 0
    return jnp.concatenate(
        [jnp.where(first, own, other), jnp.where(first, other, own)], axis=0
    )


def turn(pos_ref, act_ref, out_ref):
    for block in range(16):
        part = act_ref[:, block * 128 : (block + 1) * 128].T
        for k in range(4):
            out_ref[group_place(pos_ref, block * 4 + k)] = part[k * 32 : (k + 1) * 32]


def turned(pos, own, other):
    toks, feats = own.shape

    def kernel(pos_ref, own_ref, other_ref, out_ref, act):
        act[...] = both_cores(pos_ref, own_ref[...], other_ref[...])
        turn(pos_ref, act, out_ref)

    return call(
        kernel,
        "turned",
        [SMEM_SPEC, VMEM_SPEC, VMEM_SPEC],
        VMEM_SPEC,
        jax.ShapeDtypeStruct((8, 8, 32, 2 * toks), own.dtype),
        [pltpu.VMEM((2 * toks, feats), own.dtype)],
    )(pos, own, other).reshape(8, 256, 2 * toks)


def normed_rows(pos, own, other, chunks, width, at):
    toks, feats = own.shape

    def kernel(pos_ref, own_ref, other_ref, *refs):
        sides, gains, (out_ref, gain_ref, side_ref, wide, act) = refs[:8], refs[8:16], refs[16:]
        for k in range(8):
            wide[k] = gains[k][...].astype(F32).reshape(8, 32, 128)
        for block in range(feats // 128):
            groups = [wide[group_place(pos_ref, block * 4 + k)] for k in range(4)]
            gain_ref[:, block * 128 : (block + 1) * 128] = jnp.concatenate(groups, axis=0).T[:8]
        rows = both_cores(pos_ref, own_ref[...], other_ref[...]).astype(F32)
        inverse = lax.rsqrt(jnp.mean(rows * rows, axis=-1, keepdims=True) + norm_eps)
        act[...] = (rows * inverse * gain_ref[0:1, :]).astype(BF)
        turn(pos_ref, act, out_ref)
        total = jnp.zeros((2 * toks, width), F32)
        for k in range(8):
            turned_rows = out_ref[k].reshape(256, 2 * toks)
            total = total + jnp.dot(turned_rows.T, sides[k][...], preferred_element_type=F32)
        side_ref[...] = total

    specs = [pl.BlockSpec((256, w), lambda i, b=b: (0, b)) for w, b in ((width, at), (128, at + 1))]
    out, gains, side = call(
        kernel,
        "normed_rows",
        [SMEM_SPEC] + [VMEM_SPEC] * 2 + [specs[0]] * 8 + [specs[1]] * 8,
        [VMEM_SPEC] * 3,
        [
            jax.ShapeDtypeStruct((8, 8, 32, 2 * toks), BF),
            jax.ShapeDtypeStruct((8, feats), F32),
            jax.ShapeDtypeStruct((2 * toks, width), F32),
        ],
        [pltpu.VMEM((8, 8, 32, 128), F32), pltpu.VMEM((2 * toks, feats), BF)],
    )(pos, own, other, *chunks, *chunks)
    return out.reshape(8, 256, 2 * toks), gains, side


def turn_back(pos_ref, wide_ref, own_ref, other_ref):
    first = pos_ref[CORE] == 0
    half = wide_ref.shape[-1] // 2
    for block in range(16):
        groups = [wide_ref[group_place(pos_ref, block * 4 + k)] for k in range(4)]
        rows = jnp.concatenate(groups, axis=0).T.astype(own_ref.dtype)
        at = slice(block * 128, (block + 1) * 128)
        own_ref[:, at] = jnp.where(first, rows[:half], rows[half:])
        other_ref[:, at] = jnp.where(first, rows[half:], rows[:half])


def project(act, chunks, width, at, kind):
    toks = act.shape[-1]

    def kernel(act_ref, *refs):
        weights, out = refs[:8], refs[8]
        total = jnp.zeros((toks, width), F32)
        for k in range(8):
            total = total + jnp.dot(
                act_ref[k].T, weights[k][...], preferred_element_type=F32
            )
        out[...] = total.T.astype(kind)

    return call(
        kernel,
        "project",
        [VMEM_SPEC] + [pl.BlockSpec((256, width), lambda i: (0, at))] * 8,
        VMEM_SPEC,
        jax.ShapeDtypeStruct((width, toks), kind),
    )(act, *chunks)


def unproject(pos, sides):
    count = len(sides)
    toks = sides[0][2].shape[0 if sides[0][3] else 1]
    operands, specs, starts = [], [], []
    for chunks, at, side, flipped in sides:
        width = side.shape[1 if flipped else 0]
        starts.append(len(operands))
        if isinstance(chunks, list):
            operands += chunks
            specs += [pl.BlockSpec((256, width), lambda i, at=at: (0, at))] * 8
        else:
            operands.append(chunks)
            specs.append(VMEM_SPEC)

    def kernel(pos_ref, *refs):
        rights, weights = refs[:count], refs[count : count + len(operands)]
        own_ref, other_ref, wide = refs[count + len(operands) :]
        for k in range(8):
            total = None
            for i, (chunks, at, side, flipped) in enumerate(sides):
                begin = starts[i]
                left = weights[begin + k][...] if isinstance(chunks, list) else weights[begin][k]
                dims = (((1,), (1 if flipped else 0,)), ((), ()))
                part = lax.dot_general(left, rights[i][...], dims, preferred_element_type=F32)
                total = part if total is None else total + part
            wide[k] = total.reshape(8, 32, toks)
        turn_back(pos_ref, wide, own_ref, other_ref)

    return call(
        kernel,
        "unproject",
        [SMEM_SPEC] + [VMEM_SPEC] * count + specs,
        [VMEM_SPEC] * 2,
        [jax.ShapeDtypeStruct((toks // 2, 2048), BF)] * 2,
        [pltpu.VMEM((8, 8, 32, toks), F32)],
    )(pos, *[side[2] for side in sides], *operands)


TILE = 128
PART_ROWS = (256, 256, 128, 128, 256) * 2


def halves_joined(parts):
    out = []
    for i in (0, 5):
        out += [(parts[i],), (parts[i + 1],), (parts[i + 2], parts[i + 3]), (parts[i + 4],)]
    return out


def feed_forward(pos, normed2, cot, chunks, sums=()):
    toks = normed2.shape[-1]
    width = chunks[0].shape[1]
    tiles = width // (3 * TILE)
    wide_pair = 2 * TILE
    arrays = [a for chunk in chunks for a in (chunk if isinstance(chunk, tuple) else (chunk,))]
    count = len(arrays)

    def kernel(pos_ref, normed_ref, cot_ref, *refs):
        loose, refs = refs[:count], refs[count:]
        added, refs = refs[: len(sums)], refs[len(sums) :]
        parts, refs = refs[:10], refs[10:]
        grads = halves_joined(parts)
        d_norm_refs, ffn_refs = refs[:2], refs[2:4]
        normed_rows, cot_rows, pair_weights, down_weights, pair_side, hidden_side, wide = refs[4:]
        weights, used = [], 0
        for chunk in chunks:
            parts = len(chunk) if isinstance(chunk, tuple) else 1
            got = [ref[...] for ref in loose[used : used + parts]]
            weights.append(jnp.concatenate(got, axis=0) if parts > 1 else got[0])
            used += parts
        j = pl.program_id(0)

        @pl.when(j == 0)
        def _():
            for k in range(8):
                normed_rows[k] = normed_ref[k].T
                cot_rows[k] = cot_ref[k].T

        pre = jnp.zeros((toks, wide_pair), F32)
        d_hidden = jnp.zeros((toks, TILE), F32)
        for k in range(8):
            pre = pre + jnp.dot(
                normed_rows[k], weights[k][:, :wide_pair], preferred_element_type=F32
            )
            d_hidden = d_hidden + jnp.dot(
                cot_rows[k], weights[k][:, wide_pair:], preferred_element_type=F32
            )
        gate, up = pre[:, :TILE], pre[:, TILE:]
        gate_sig = jax.nn.sigmoid(gate)
        gate_act = gate * gate_sig
        hidden = (gate_act * up).astype(BF)
        d_gate = (d_hidden * up * gate_sig * (1.0 + gate * (1.0 - gate_sig))).astype(BF)
        d_up = (d_hidden * gate_act).astype(BF)
        d_pair = jnp.concatenate([d_gate, d_up], axis=1)
        for k in range(8):
            pair_grad = jnp.dot(normed_ref[k], d_pair, preferred_element_type=F32).astype(BF)
            down_grad = jnp.dot(cot_ref[k], hidden, preferred_element_type=F32).astype(BF)
            begin = 0
            for ref in grads[k]:
                at = slice(begin, begin + ref.shape[0])
                ref[:, :wide_pair] = pair_grad[at]
                ref[:, wide_pair:] = down_grad[at]
                begin += ref.shape[0]
        pair_at = pl.ds(pl.multiple_of(j * wide_pair, wide_pair), wide_pair)
        tile_at = pl.ds(pl.multiple_of(j * TILE, TILE), TILE)
        pair_side[:, pair_at] = d_pair
        hidden_side[:, tile_at] = hidden
        for k in range(8):
            pair_weights[k, :, pair_at] = weights[k][:, :wide_pair]
            down_weights[k, :, tile_at] = weights[k][:, wide_pair:]

        @pl.when(j == tiles - 1)
        def _():
            dims = (((1,), (1,)), ((), ()))
            for out_refs, left, right in (
                (d_norm_refs, pair_weights, pair_side),
                (ffn_refs, down_weights, hidden_side),
            ):
                for k in range(8):
                    wide[k] = lax.dot_general(
                        left[k], right[...], dims, preferred_element_type=F32
                    ).reshape(8, 32, toks)
                turn_back(pos_ref, wide, *out_refs)
            for out_ref, more_ref in zip(d_norm_refs + ffn_refs, added):
                out_ref[...] = (out_ref[...].astype(F32) + more_ref[...].astype(F32)).astype(BF)

    whole = pl.BlockSpec((8, 256, toks), lambda j: (0, 0, 0))
    tiles_in = [pl.BlockSpec((a.shape[0], 3 * TILE), lambda j: (0, j)) for a in arrays]
    rows = pl.BlockSpec((toks // 2, 2048), lambda j: (0, 0))
    outs = call(
        kernel,
        "feed_forward",
        [SMEM_SPEC, whole, whole] + tiles_in + [rows] * len(sums),
        [pl.BlockSpec((r, 3 * TILE), lambda j: (0, j)) for r in PART_ROWS] + [rows] * 4,
        [jax.ShapeDtypeStruct((r, width), BF) for r in PART_ROWS]
        + [jax.ShapeDtypeStruct((toks // 2, 2048), BF)] * 4,
        [
            pltpu.VMEM((8, toks, 256), BF),
            pltpu.VMEM((8, toks, 256), BF),
            pltpu.VMEM((8, 256, tiles * wide_pair), BF),
            pltpu.VMEM((8, 256, tiles * TILE), BF),
            pltpu.VMEM((toks, tiles * wide_pair), BF),
            pltpu.VMEM((toks, tiles * TILE), BF),
            pltpu.VMEM((8, 8, 32, toks), F32),
        ],
        limit=58,
        grid=(tiles,),
    )(pos, normed2, cot, *arrays, *sums)
    return halves_joined(outs[:10]), outs[10:]


SEND_ORDER = (2, 6, 1, 5, 3, 7, 0, 4)


def weight_chunks(terms):
    widths = [r.shape[0] if f else r.shape[1] for l, r, f in terms]
    total = sum(widths)
    operands = [l for l, r, f in terms] + [r for l, r, f in terms]
    count = len(operands)

    def kernel(*refs):
        ins, outs = refs[:count], halves_joined(refs[count : count + 10])
        slots, sem = refs[-2:]
        pending = {}
        for step, chunk in enumerate(SEND_ORDER):
            slot = step % 2
            for copy in pending.get(slot, ()):
                copy.wait()
            begin = 0
            for i, (left, right, flipped) in enumerate(terms):
                dims = (((1,), (1 if flipped else 0,)), ((), ()))
                product = lax.dot_general(
                    ins[i][chunk], ins[len(terms) + i][...], dims, preferred_element_type=F32
                )
                slots[slot, :, begin : begin + widths[i]] = product.astype(BF)
                begin += widths[i]
            copies, at = [], 0
            for part, out in enumerate(outs[chunk]):
                rows = out.shape[0]
                copies.append(
                    pltpu.make_async_copy(
                        slots.at[slot, pl.ds(at, rows)], out, sem.at[slot, part]
                    )
                )
                at += rows
            for copy in copies:
                copy.start()
            pending[slot] = copies
        for copies in pending.values():
            for copy in copies:
                copy.wait()

    outs = call(
        kernel,
        "weight_chunks",
        [VMEM_SPEC] * count,
        [ANY_SPEC] * 10,
        [jax.ShapeDtypeStruct((r, total), BF) for r in PART_ROWS],
        [pltpu.VMEM((2, 256, total), BF), pltpu.SemaphoreType.DMA((2, 2))],
    )(*operands)
    return halves_joined(outs)


def summed(parts):
    total = parts[0].astype(F32)
    for part in parts[1:]:
        total = total + part.astype(F32)
    return total


def add_half(chunk, half, at):
    rows, width = half.shape
    tile = next((t for t in (1152, 640) if width % t == 0), width)

    def kernel(chunk_ref, half_ref, out_ref):
        out_ref[...] = (chunk_ref[...].astype(F32) + half_ref[...].astype(F32)).astype(BF)

    there = pl.BlockSpec((rows, tile), lambda i: (at, i))
    return call(
        kernel,
        "add_half",
        [there, pl.BlockSpec((rows, tile), lambda i: (0, i))],
        there,
        jax.ShapeDtypeStruct(chunk.shape, BF),
        grid=(width // tile,),
        input_output_aliases={0: 0},
    )(chunk, half)


def scatter_first(chunks):
    far = []
    for h, axis in ((0, "y"), (1, "z")):
        upper, lower = chunks[4 * h + 2]
        far += [hand(upper, axis, 1), hand(lower, axis, 3)]
    far = tie(*far)
    got = []
    for h, axis in ((0, "y"), (1, "z")):
        own, one, three = (chunks[4 * h + d][0] for d in (0, 1, 3))
        one, three = add_half(one, far[2 * h], 0), add_half(three, far[2 * h + 1], 1)
        got.append([own, hand(one, axis, 1), hand(three, axis, 3)])
    return got


def scatter_second(pieces):
    def part(h, begin, end):
        sums = [summed([g[begin:end] for g in got[h]]) for got in pieces]
        return sums[0] if len(sums) == 1 else jnp.concatenate(sums, axis=1)

    axes = ((0, "z"), (1, "y"))
    far = [part(h, begin, begin + 32).astype(BF) for h, axis in axes for begin in (128, 160)]
    own = [part(h, 0, 64).astype(BF) for h, axis in axes]
    one = [part(h, 64, 128) for h, axis in axes]
    three = [part(h, 192, 256) for h, axis in axes]
    got = []
    for h, axis in axes:
        got += [hand(far[2 * h], axis, 1), hand(far[2 * h + 1], axis, 3)]
    got = tie(*got)
    keep, give = [], []
    for h, axis in axes:
        upper, lower = got[2 * h], got[2 * h + 1]
        after = jnp.concatenate([one[h][:32] + upper.astype(F32), one[h][32:]], axis=0).astype(BF)
        before = jnp.concatenate([three[h][:32], three[h][32:] + lower.astype(F32)], axis=0).astype(BF)
        share = summed([own[h], hand(after, axis, 1), hand(before, axis, 3)])
        keep.append(share[:32])
        give.append(share[32:].astype(BF))
    got = fetch(jnp.concatenate(give, axis=0), "x", 1).astype(F32)
    return keep[0] + got[:32], keep[1] + got[32:]


def prepared(pos, q, out_t, kv, gate, up, down_t, gains):
    rows = q.shape[0]
    hidden = gate.shape[1] // 2
    attn_width = (q.shape[1] + out_t.shape[1] + kv.shape[1]) // 2 + 128

    def kernel(pos_ref, q_ref, out_t_ref, kv_ref, gate_ref, up_ref, down_ref, *refs):
        gain_refs, (attn_mine, attn_give, ffn_mine, ffn_give) = refs[:2], refs[2:]
        first = pos_ref[CORE] == 0

        def put(mine_ref, give_ref, to, source, at, width):
            half = source.shape[1] // 2
            one, two = source[:, at : at + width], source[:, half + at : half + at + width]
            mine_ref[:, to : to + width] = jnp.where(first, one, two)
            give_ref[:, to : to + width] = jnp.where(first, two, one)

        begin = 0
        for ref in (q_ref, out_t_ref, kv_ref):
            width = ref.shape[1] // 2
            put(attn_mine, attn_give, begin, ref, 0, width)
            begin += width
        same = lax.broadcasted_iota(jnp.int32, (rows, rows), 0) == lax.broadcasted_iota(
            jnp.int32, (rows, rows), 1
        )
        lane = lax.broadcasted_iota(jnp.int32, (rows, 128), 1)
        block = jnp.zeros((rows, 128), F32)
        for i, ref in enumerate(gain_refs):
            column = jnp.sum(jnp.where(same, ref[...].astype(F32), 0.0), axis=1, keepdims=True)
            block = jnp.where(lane == i, column, block)
        attn_mine[:, begin:] = block.astype(BF)
        attn_give[:, begin:] = block.astype(BF)
        for t in range(hidden // TILE):
            for i, ref in enumerate((gate_ref, up_ref, down_ref)):
                put(ffn_mine, ffn_give, (3 * t + i) * TILE, ref, t * TILE, TILE)

    return call(
        kernel,
        "prepared",
        [SMEM_SPEC] + [VMEM_SPEC] * 8,
        [VMEM_SPEC] * 4,
        [jax.ShapeDtypeStruct((rows, attn_width), BF)] * 2
        + [jax.ShapeDtypeStruct((rows, 3 * hidden), BF)] * 2,
        limit=60,
    )(pos, q, out_t, kv, gate, up, down_t, *[g.reshape(1, -1) for g in gains])


def unpacked(pos, mine, other, layout):
    rows = mine.shape[0]
    halves = [sum(w for b, w in pieces) for pieces in layout]

    def kernel(pos_ref, mine_ref, other_ref, *outs):
        first = pos_ref[CORE] == 0
        for out, half, pieces in zip(outs, halves, layout):
            to = 0
            for begin, width in pieces:
                one, two = mine_ref[:, begin : begin + width], other_ref[:, begin : begin + width]
                out[:, to : to + width] = jnp.where(first, one, two)
                out[:, half + to : half + to + width] = jnp.where(first, two, one)
                to += width

    return call(
        kernel,
        "unpacked",
        [SMEM_SPEC] + [VMEM_SPEC] * 2,
        [VMEM_SPEC] * len(layout),
        [jax.ShapeDtypeStruct((rows, 2 * half), F32) for half in halves],
    )(pos, mine, other)


def arranged(pos, mine, other):
    count, head_dim = mine.shape
    block = 1024

    def kernel(pos_ref, mine_ref, other_ref, k_ref, v_ref, kt_ref, vt_ref):
        first = pos_ref[CORE] == 0
        one, two = mine_ref[...], other_ref[...]
        keys, values = jnp.where(first, one, two), jnp.where(first, two, one)
        k_ref[...] = keys
        v_ref[...] = values
        kt_ref[...] = keys.T
        vt_ref[...] = values.T

    rows = pl.BlockSpec((block, head_dim), lambda i: (i, 0))
    columns = pl.BlockSpec((head_dim, block), lambda i: (0, i))
    natural = jax.ShapeDtypeStruct((count, head_dim), BF)
    across = jax.ShapeDtypeStruct((head_dim, count), BF)
    return call(
        kernel,
        "arranged",
        [SMEM_SPEC, rows, rows],
        [rows, rows, columns, columns],
        [natural, natural, across, across],
        grid=(count // block,),
    )(pos, mine, other)


def key_gradients(pos, act, d_keyval, tokens, d_own, d_other, ffn_gain):
    toks, width = d_keyval.shape

    def kernel(pos_ref, act_ref, side_ref, tokens_ref, own_ref, other_ref, ffn_ref, out_ref, wide):
        for k in range(8):
            product = jnp.dot(act_ref[k], side_ref[...], preferred_element_type=F32)
            wide[k] = product.reshape(8, 32, width)
        rows = tokens_ref[...].astype(F32)
        inverse = lax.rsqrt(jnp.mean(rows * rows, axis=-1, keepdims=True) + norm_eps)
        d_normed = own_ref[...].astype(F32) + other_ref[...].astype(F32)
        attn_gain = jnp.sum(d_normed * rows * inverse, axis=0, keepdims=True)
        gains = jnp.concatenate(
            [attn_gain, 0.5 * ffn_ref[...], jnp.zeros((126, rows.shape[1]), F32)], axis=0
        )
        for block in range(16):
            groups = [wide[group_place(pos_ref, block * 4 + k)] for k in range(4)]
            at = slice(block * 128, (block + 1) * 128)
            out_ref[at, :width] = jnp.concatenate(groups, axis=0).astype(BF)
            out_ref[at, width:] = gains[:, at].T.astype(BF)

    return call(
        kernel,
        "key_gradients",
        [SMEM_SPEC] + [VMEM_SPEC] * 6,
        VMEM_SPEC,
        jax.ShapeDtypeStruct((2048, width + 128), BF),
        [pltpu.VMEM((8, 8, 32, width), F32)],
    )(pos, act, d_keyval, tokens, d_own, d_other, ffn_gain)


def allowed_keys(begin, count, places, starts):
    shape = (count, places.shape[1])
    key_place = begin + lax.broadcasted_iota(jnp.int32, shape, 0)
    return (key_place <= places) & (key_place >= starts)


def row_places(pos_ref, docs_ref, own, rows):
    half = rows // 2
    base = (pos_ref[Z] * 4 + pos_ref[Y]) * rows + jnp.where(own, pos_ref[CORE] * half, 0)
    lane = lax.broadcasted_iota(jnp.int32, (1, rows), 1)
    places = base + jnp.where(own, lax.rem(lane, half), lane)
    end = start = jnp.int32(0)
    starts = jnp.zeros((1, rows), jnp.int32)
    for j in range(docs_ref.shape[1]):
        length = docs_ref[pos_ref[X], j]
        end = end + length
        start = start + jnp.where(base >= end, length, 0)
        starts = starts + jnp.where(places >= end, length, 0)
    last = base + jnp.where(own, half, rows) - 1
    return places, starts, lax.div(start, KEY_BLOCK), lax.div(last, KEY_BLOCK) + 1


def attend_kernel(pos_ref, docs_ref, qt_ref, k_ref, vt_ref, ot_ref, lse_ref, *, first_set, scale):
    units, head_dim, rows = qt_ref.shape
    own = pl.program_id(0) * units >= first_set
    places, starts, low, high = row_places(pos_ref, docs_ref, own, rows)

    def step(j, carry):
        begin = pl.multiple_of(j * KEY_BLOCK, KEY_BLOCK)
        keys = k_ref[pl.ds(begin, KEY_BLOCK), :]
        values = vt_ref[:, pl.ds(begin, KEY_BLOCK)]
        allowed = allowed_keys(begin, KEY_BLOCK, places, starts)
        out = []
        for u in range(units):
            top, mass, acc = carry[u]
            scores = jnp.dot(keys, qt_ref[u], preferred_element_type=F32)
            scores = jnp.where(allowed, scores, masked_fill)
            new_top = jnp.maximum(top, jnp.max(scores, axis=0, keepdims=True))
            weights = jnp.exp2((scores - new_top) * scale)
            shrink = jnp.exp2((top - new_top) * scale)
            mass = mass * shrink + jnp.sum(weights, axis=0, keepdims=True)
            acc = acc * shrink + jnp.dot(
                values, weights.astype(BF), preferred_element_type=F32
            )
            out.append((new_top, mass, acc))
        return tuple(out)

    start = (
        jnp.full((1, rows), masked_fill, F32),
        jnp.zeros((1, rows), F32),
        jnp.zeros((head_dim, rows), F32),
    )
    done = lax.fori_loop(low, high, step, (start,) * units)
    for u in range(units):
        top, mass, acc = done[u]
        ot_ref[u] = acc / mass
        lse_ref[u] = top * scale + jnp.log2(mass)


def attend(pos, docs, qt, keys, values_t, scale):
    units = 2
    blocks, head_dim, rows = qt.shape
    count = keys.shape[0]
    first_set = blocks // 2
    block = pl.BlockSpec((units, head_dim, rows), lambda i, p, d: (i, 0, 0))
    return pl.pallas_call(
        functools.partial(attend_kernel, first_set=first_set, scale=scale),
        grid_spec=pltpu.PrefetchScalarGridSpec(
            num_scalar_prefetch=2,
            grid=(blocks // units,),
            in_specs=[
                block,
                pl.BlockSpec((count, head_dim), lambda i, p, d: (0, 0)),
                pl.BlockSpec((head_dim, count), lambda i, p, d: (0, 0)),
            ],
            out_specs=[block, pl.BlockSpec((units, 1, rows), lambda i, p, d: (i, 0, 0))],
        ),
        out_shape=[
            jax.ShapeDtypeStruct((blocks, head_dim, rows), F32),
            jax.ShapeDtypeStruct((blocks, 1, rows), F32),
        ],
        compiler_params=pltpu.CompilerParams(vmem_limit_bytes=28 * MB),
        cost_estimate=SMALL,
        name="attend",
    )(pos, docs, qt, keys, values_t)


def attend_back_kernel(
    pos_ref, docs_ref, qt_ref, dot_ref, ot_ref, lse_ref, k_ref, kt_ref, v_ref,
    dqt_ref, mine_ref, give_ref, dk_ref, dv_ref, *, first_set, scale, score_scale,
):
    units, head_dim, rows = qt_ref.shape

    @pl.when(pl.program_id(0) == 0)
    def _():
        dk_ref[...] = jnp.zeros_like(dk_ref)
        dv_ref[...] = jnp.zeros_like(dv_ref)

    own = pl.program_id(0) * units >= first_set
    places, starts, low, high = row_places(pos_ref, docs_ref, own, rows)
    queries = [qt_ref[u].T for u in range(units)]
    d_outs = [dot_ref[u].T for u in range(units)]
    deltas = [
        jnp.sum(dot_ref[u].astype(F32) * ot_ref[u], axis=0, keepdims=True) for u in range(units)
    ]

    def step(j, carry):
        begin = pl.multiple_of(j * KEY_BLOCK, KEY_BLOCK)
        part = pl.ds(begin, KEY_BLOCK)
        allowed = allowed_keys(begin, KEY_BLOCK, places, starts)
        out = []
        d_keys = d_values = None
        for u in range(units):
            scores = jnp.dot(k_ref[part, :], qt_ref[u], preferred_element_type=F32)
            d_probs = jnp.dot(v_ref[part, :], dot_ref[u], preferred_element_type=F32)
            probs = jnp.where(allowed, jnp.exp2(scores * scale - lse_ref[u]), 0.0)
            d_scores = (probs * (d_probs - deltas[u])).astype(BF)
            for_keys = jnp.dot(d_scores, queries[u], preferred_element_type=F32)
            for_values = jnp.dot(probs.astype(BF), d_outs[u], preferred_element_type=F32)
            d_keys = for_keys if u == 0 else d_keys + for_keys
            d_values = for_values if u == 0 else d_values + for_values
            out.append(
                carry[u] + jnp.dot(kt_ref[:, part], d_scores, preferred_element_type=F32)
            )
        dk_ref[part, :] += d_keys
        dv_ref[part, :] += d_values
        return tuple(out)

    start = jnp.zeros((head_dim, rows), F32)
    done = lax.fori_loop(low, high, step, (start,) * units)
    for u in range(units):
        dqt_ref[u] = done[u] * score_scale

    @pl.when(pl.program_id(0) == pl.num_programs(0) - 1)
    def _():
        first = pos_ref[CORE] == 0
        d_keys, d_values = dk_ref[...] * score_scale, dv_ref[...]
        mine_ref[...] = jnp.where(first, d_keys, d_values)
        give_ref[...] = jnp.where(first, d_values, d_keys).astype(BF)


def attend_back(pos, docs, qt, d_out_t, out_t, lse, keys, keys_t, values, scale, score_scale):
    units = 2
    blocks, head_dim, rows = qt.shape
    count = keys.shape[0]
    first_set = blocks // 2
    block = pl.BlockSpec((units, head_dim, rows), lambda i, p, d: (i, 0, 0))
    whole = pl.BlockSpec((count, head_dim), lambda i, p, d: (0, 0))
    return pl.pallas_call(
        functools.partial(
            attend_back_kernel, first_set=first_set, scale=scale, score_scale=score_scale
        ),
        grid_spec=pltpu.PrefetchScalarGridSpec(
            num_scalar_prefetch=2,
            grid=(blocks // units,),
            in_specs=[
                block,
                block,
                block,
                pl.BlockSpec((units, 1, rows), lambda i, p, d: (i, 0, 0)),
                whole,
                pl.BlockSpec((head_dim, count), lambda i, p, d: (0, 0)),
                whole,
            ],
            out_specs=[block, whole, whole],
            scratch_shapes=[pltpu.VMEM((count, head_dim), F32)] * 2,
        ),
        out_shape=[
            jax.ShapeDtypeStruct((blocks, head_dim, rows), F32),
            jax.ShapeDtypeStruct((count, head_dim), F32),
            jax.ShapeDtypeStruct((count, head_dim), BF),
        ],
        compiler_params=pltpu.CompilerParams(vmem_limit_bytes=44 * MB),
        cost_estimate=SMALL,
        name="attend_back",
    )(pos, docs, qt, d_out_t, out_t, lse, keys, keys_t, values)


def doc_starts(lengths, places):
    ends = jnp.cumsum(lengths)
    passed = (places[:, None] >= ends[None, :]).astype(jnp.int32)
    return jnp.sum(passed * lengths[None, :], axis=1)


def rotate_rows(values, cosine, sine):
    half = values.shape[-1] // 2
    one, two = values[..., :half], values[..., half:]
    return jnp.concatenate([one * cosine - two * sine, two * cosine + one * sine], axis=-1)


def rotate_columns(values, cosine, sine):
    half = values.shape[1] // 2
    one, two = values[:, :half], values[:, half:]
    return jnp.concatenate([one * cosine - two * sine, two * cosine + one * sine], axis=1)


def head_blocks(array):
    toks, width = array.shape
    count = width // 256

    def kernel(array_ref, out_ref):
        for b in range(count):
            for i in range(2):
                at = (2 * b + i) * 128
                out_ref[b, :, i * toks : (i + 1) * toks] = array_ref[:, at : at + 128].T

    shape = jax.ShapeDtypeStruct((count, 128, 2 * toks), array.dtype)
    return call(kernel, "head_blocks", [VMEM_SPEC], VMEM_SPEC, shape)(array)


def head_blocks_back(blocks, begin):
    total, head_dim, wide = blocks.shape
    count, toks = total - begin, wide // 2

    def kernel(blocks_ref, out_ref):
        for b in range(count):
            for i in range(2):
                at = (2 * b + i) * 128
                out_ref[:, at : at + 128] = blocks_ref[b, :, i * toks : (i + 1) * toks].T

    shape = jax.ShapeDtypeStruct((toks, count * 256), blocks.dtype)
    spec = pl.BlockSpec((count, head_dim, wide), lambda i: (begin // count, 0, 0))
    return call(kernel, "head_blocks_back", [spec], VMEM_SPEC, shape)(blocks)


def on_device(
    tokens, doc_lengths, attn_gain, q_weight, kv_weight, out_weight, ffn_gain,
    gate_weight, up_weight, down_weight, second_queries, out_cotangent, second_cotangent,
):
    x, z, y, c = (lax.axis_index(a) for a in ("x", "z", "y", "c"))
    first = c == 0
    pos = jnp.stack([x, z, y, c]).astype(jnp.int32)
    toks, width = tokens.shape
    head_dim = kv_weight.shape[1] // 2
    score_scale = head_dim ** (-0.5)
    scale = score_scale * math.log2(math.e)
    rows = q_weight.shape[0]

    def swap(own):
        return fetch(own, "c", 1)

    n_q, n_kv = q_weight.shape[1] // 2, head_dim
    n_out, n_ffn = out_weight.shape[0] // 2, down_weight.shape[0] // 2
    n_attn = n_q + n_out
    at_out, at_kv = n_q // n_out, n_attn // n_kv
    attn_mine, attn_give, ffn_mine, ffn_give = prepared(
        pos, q_weight, out_weight.T, kv_weight, gate_weight, up_weight, down_weight.T,
        (attn_gain, ffn_gain),
    )
    attn_other, ffn_other, tokens_other, cot_other = tie(
        swap(attn_give), swap(ffn_give), swap(tokens), swap(out_cotangent)
    )
    attn_rows = across_x(attn_mine, attn_other)
    ffn_rows = across_x(ffn_mine, ffn_other)
    attn_pair = second_pair([jnp.concatenate(b, axis=0) for b in first_blocks(attn_rows)])
    attn_chunks = far_blocks(attn_pair, tie(*near_blocks(attn_pair)))
    attn_chunks = [jnp.concatenate(w, axis=0) if isinstance(w, tuple) else w for w in attn_chunks]
    def over_tp(rows):
        send = rows.astype(BF)
        return send.astype(F32) + fetch(send, "t", 1).astype(F32)

    def reduce_rows(own, other):
        return over_tp(own.astype(F32) + swap(other).astype(F32))

    places = (z * 4 + y) * (2 * toks) + jnp.arange(2 * toks, dtype=jnp.int32)
    starts = doc_starts(jnp.where(x == 0, doc_lengths[0], doc_lengths[1]), places)
    positions = (places - starts).astype(F32)
    inverse_freq = jnp.exp(
        jnp.arange(head_dim // 2, dtype=F32) * (-2.0 * math.log(rope_base) / head_dim)
    )
    angles_t = inverse_freq[:, None] * positions[None, :]
    cos_t, sin_t = jnp.cos(angles_t), jnp.sin(angles_t)

    inputs = tokens.astype(F32)
    inv_attn = lax.rsqrt(jnp.mean(inputs * inputs, axis=-1, keepdims=True) + norm_eps)
    second_t, second_cot_t = head_blocks(second_queries), head_blocks(second_cotangent)
    cot_t = turned(pos, out_cotangent, cot_other)
    cos_r, sin_r = cos_t.T, sin_t.T
    normed_t, gain_rows, keyval = normed_rows(pos, tokens, tokens_other, attn_chunks, n_kv, at_kv)
    gain_one, gain_two = gain_rows[0:1], gain_rows[1:2]
    kv_own = jnp.where(first, rotate_rows(keyval, cos_r, sin_r), keyval).astype(BF)
    kv_sent, *ffn_rows = tie(
        jnp.broadcast_to(kv_own[None], (16,) + kv_own.shape), *ffn_rows
    )
    kv_all = lax.all_to_all(kv_sent, ("z", "y"), 0, 0).reshape(-1, head_dim)
    ffn_blocks = first_blocks(ffn_rows)
    kv_all, *blocks = tie(kv_all, *ffn_blocks[0], *ffn_blocks[1])
    ffn_blocks = blocks[:4], blocks[4:]
    ffn_pair = second_pair([joined(blocks, 0, 3 * n_ffn) for blocks in ffn_blocks])
    ffn_near = near_blocks(ffn_pair)
    kv_all, second_t, second_cot_t, cot_t, *unused = tie(
        kv_all, second_t, second_cot_t, cot_t, *[half for half, axis in ffn_pair]
    )
    queries_t = project(normed_t, attn_chunks, n_q, 0, F32)
    query_rot = rotate_columns(queries_t.reshape(-1, head_dim, 2 * toks), cos_t, sin_t).astype(BF)
    keys, values, keys_t, values_t = arranged(pos, kv_all, swap(kv_all))
    query_t = jnp.concatenate([query_rot, second_t], axis=0)
    out_t, lse = attend(pos, doc_lengths, query_t, keys, values_t, scale)
    out_t, lse, *ffn_near = tie(out_t, lse, *ffn_near)
    ffn_chunks = far_blocks(ffn_pair, ffn_near)
    n_first = query_rot.shape[0]
    second_out = head_blocks_back(out_t, n_first)
    attended_t = out_t[:n_first].reshape(-1, 2 * toks).astype(BF)

    branch = reduce_rows(*unproject(pos, [(attn_chunks, at_out, attended_t, False)]))
    resid = inputs + branch
    inv_ffn = lax.rsqrt(jnp.mean(resid * resid, axis=-1, keepdims=True) + norm_eps)
    normed2 = (resid * inv_ffn * gain_two).astype(BF)
    normed2_t = turned(pos, normed2, swap(normed2))
    grads, sums = feed_forward(pos, normed2_t, cot_t, ffn_chunks)
    ffn_got = scatter_first(grads)
    d_norm2_part, ffn_part = sums[:2], sums[2:]
    d_normed2 = reduce_rows(*d_norm2_part)

    scaled_two = gain_two * d_normed2
    ffn_gain_part = jnp.sum(d_normed2 * resid * inv_ffn, axis=0)
    d_resid = (
        out_cotangent.astype(F32)
        + inv_ffn * scaled_two
        - resid * inv_ffn**3 * jnp.mean(scaled_two * resid, axis=-1, keepdims=True)
    )
    d_branch = d_resid.astype(BF)

    d_branch_t = turned(pos, d_branch, swap(d_branch))
    d_attended_t = project(d_branch_t, attn_chunks, n_out, at_out, BF)
    d_out_t = jnp.concatenate(
        [d_attended_t.reshape(-1, head_dim, 2 * toks), second_cot_t], axis=0
    )
    d_query_t, kv_mine, kv_give = attend_back(
        pos, doc_lengths, query_t, d_out_t, out_t, lse, keys, keys_t, values, scale, score_scale
    )
    kv_give, d_query_t, *ffn_part = tie(kv_give, d_query_t, *ffn_part)
    kv_other = swap(kv_give)
    second_queries_grad = head_blocks_back(d_query_t, n_first)
    d_queries_t = rotate_columns(d_query_t[:n_first], cos_t, -sin_t).reshape(-1, 2 * toks).astype(BF)

    attn_grads = weight_chunks([(normed_t, d_queries_t, True), (d_branch_t, attended_t, True)])
    terms = [term for half in ffn_got for term in half]
    grads = [part for chunk in attn_grads for part in chunk]
    kv_other, *rest = tie(kv_other, *terms, *grads)
    ffn_got, grads = [rest[:3], rest[3:6]], rest[6:]
    attn_got = scatter_first(halves_joined(grads))
    kv_chip = (kv_mine + kv_other.astype(F32)).astype(BF).reshape(16, 2 * toks, head_dim)
    kv_parts = lax.all_to_all(kv_chip, ("z", "y"), 0, 0)
    kv_sum = jnp.sum(kv_parts.astype(F32), axis=0)
    ffn_sum = reduce_rows(*ffn_part)
    result = resid + ffn_sum
    d_keyval = jnp.where(first, rotate_rows(kv_sum, cos_r, -sin_r), kv_sum).astype(BF)
    d_norm_part = unproject(
        pos, [(attn_chunks, 0, d_queries_t, False), (attn_chunks, at_kv, d_keyval, True)]
    )
    d_norm_other = swap(d_norm_part[1])
    d_normed = over_tp(d_norm_part[0].astype(F32) + d_norm_other.astype(F32))
    kv_grads = key_gradients(
        pos, normed_t, d_keyval, tokens, d_norm_part[0], d_norm_other, ffn_gain_part[None]
    )
    got = [g for pieces in (attn_got, ffn_got) for half in pieces for g in half]
    kv_grads, *got = tie(kv_grads, *got)
    pieces = [[got[6 * i : 6 * i + 3], got[6 * i + 3 : 6 * i + 6]] for i in range(2)]
    share, share_give = scatter_second(pieces)
    kv_got = lax.all_to_all(kv_grads.reshape(32, 2, rows, -1), ("x", "z", "y"), 0, 0)
    kv_share = jnp.sum(kv_got.astype(F32), axis=0)
    scaled_one = gain_one * d_normed
    tokens_grad = (
        d_resid
        + inv_attn * scaled_one
        - inputs * inv_attn**3 * jnp.mean(scaled_one * inputs, axis=-1, keepdims=True)
    )

    share_other = swap(share_give)
    tiles = [(n_attn + t * 3 * TILE, TILE) for t in range(n_ffn // TILE)]
    q_grad, out_grad_t, gate_grad, up_grad, down_grad_t = unpacked(
        pos,
        share,
        share_other,
        [[(0, n_q)], [(n_q, n_out)]] + [[(b + i * TILE, w) for b, w in tiles] for i in range(3)],
    )
    kv_mine, kv_give = (jnp.where(first, kv_share[i], kv_share[1 - i]) for i in (0, 1))
    kv_other = swap(kv_give)
    kv_gain = jnp.concatenate(
        [
            in_order(first, kv_mine[:, :n_kv], kv_other[:, :n_kv], 1),
            kv_mine[:, n_kv:] + kv_other[:, n_kv:],
        ],
        axis=1,
    )
    kv_gain = kv_gain + fetch(kv_gain, "t", 1)
    return (
        result,
        second_out,
        tokens_grad,
        kv_gain[:, 2 * n_kv],
        q_grad,
        kv_gain[:, : 2 * n_kv],
        out_grad_t.T,
        kv_gain[:, 2 * n_kv + 1],
        gate_grad,
        up_grad,
        down_grad_t.T,
        second_queries_grad,
    )


def solution(mesh):
    fine = Mesh(mesh.devices.reshape(2, 4, 4, 2, 2), ("x", "z", "y", "c", "t"))
    seq = ("x", "z", "y", "c")
    rows, both, turned_both = P(seq, None), P(seq, "t"), P("t", seq)
    in_specs = (
        rows, P(), P(seq), both, rows, turned_both, P(seq), both, both, turned_both, both, rows, both,
    )
    out_specs = (
        rows, both, rows, P(seq), both, rows, turned_both, P(seq), both, both, turned_both, both,
    )
    return jax.shard_map(
        on_device, mesh=fine, in_specs=in_specs, out_specs=out_specs, check_vma=False
    )
```

```python
import functools
import math

import jax
import jax.numpy as jnp
from jax import lax
from jax.experimental import pallas as pl
from jax.experimental.pallas import tpu as pltpu
from jax.sharding import Mesh, PartitionSpec as P

norm_eps = 1e-05
rope_base = 10000.0
masked_fill = -1e30
KEY_BLOCK = 1024
BF = jnp.bfloat16
F32 = jnp.float32
MB = 1024 * 1024


def fetch(block, axis, offset):
    n = lax.axis_size(axis)
    return lax.ppermute(block, axis, [((i + offset) % n, i) for i in range(n)])


def hand(block, axis, offset):
    return fetch(block, axis, -offset)


def in_order(first, mine, other, axis):
    return jnp.where(
        first,
        jnp.concatenate([mine, other], axis=axis),
        jnp.concatenate([other, mine], axis=axis),
    )


X, Z, Y, CORE = 0, 1, 2, 3


def near_blocks(pair):
    return [fetch(block, axis, d) for block, axis in pair for d in (1, 3)]


def far_blocks(pair, near):
    out = []
    for i, (block, axis) in enumerate(pair):
        after, before = near[2 * i : 2 * i + 2]
        half = block.shape[0] // 2
        far = (fetch(after[:half], axis, 1), fetch(before[half:], axis, 3))
        out.append([block, after, far, before])
    return out[0] + out[1]


def across_x(mine, other):
    rows = mine.shape[0]
    got = fetch(jnp.concatenate([mine, other], axis=0), "x", 1)
    return [
        jnp.concatenate([mine, got[:rows]], axis=0),
        jnp.concatenate([other, got[rows:]], axis=0),
    ]


def first_blocks(pieces):
    return [
        [piece] + [fetch(piece, axis, d) for d in (1, 2, 3)] for piece, axis in zip(pieces, ("z", "y"))
    ]


def second_pair(halves):
    return [(halves[0], "y"), (halves[1], "z")]


def place_in_chunks(pos_ref, x, z, y, dh):
    dx = lax.rem(x - pos_ref[X] + 2, 2)
    dz = lax.rem(z - pos_ref[Z] + 4, 4)
    dy = lax.rem(y - pos_ref[Y] + 4, 4)
    own = dh == 0
    return dh * 4 + jnp.where(own, dy, dz), jnp.where(own, dz, dy) * 2 + dx


def group_place(pos_ref, group):
    h, y, z, x = group % 2, group // 2 % 4, group // 8 % 4, group // 32
    return place_in_chunks(pos_ref, x, z, y, lax.rem(h + pos_ref[CORE], 2))


def whole_place(pos_ref, group):
    h, y, z, x = group % 2, group // 2 % 4, group // 8 % 4, group // 32
    dx = lax.rem(x - pos_ref[X] + 2, 2)
    return (z * 4 + y) * 4 + dx * 2 + lax.rem(h + pos_ref[CORE], 2)


SMEM_SPEC = pl.BlockSpec(memory_space=pltpu.SMEM)
VMEM_SPEC = pl.BlockSpec(memory_space=pltpu.VMEM)
ANY_SPEC = pl.BlockSpec(memory_space=pl.ANY)
SMALL = pl.CostEstimate(flops=1024, bytes_accessed=1024, transcendentals=0)


def call(kernel, name, in_specs, out_specs, out_shape, scratch=(), limit=24, grid=None, **more):
    return pl.pallas_call(
        kernel,
        grid=grid or (1,),
        in_specs=in_specs,
        out_specs=out_specs,
        out_shape=out_shape,
        scratch_shapes=scratch,
        compiler_params=pltpu.CompilerParams(vmem_limit_bytes=limit * MB),
        cost_estimate=SMALL,
        name=name,
        **more,
    )


def tie(*arrays):
    return list(lax.optimization_barrier(arrays))


def both_cores(pos_ref, own, other):
    first = pos_ref[CORE] == 0
    return jnp.concatenate(
        [jnp.where(first, own, other), jnp.where(first, other, own)], axis=0
    )


def turn(pos_ref, act_ref, out_ref, place=group_place):
    for block in range(16):
        part = act_ref[:, block * 128 : (block + 1) * 128].T
        for k in range(4):
            out_ref[place(pos_ref, block * 4 + k)] = part[k * 32 : (k + 1) * 32]


def turned(pos, own, other, whole=False):
    toks, feats = own.shape
    shape = (64, 32, 2 * toks) if whole else (8, 8, 32, 2 * toks)

    def kernel(pos_ref, own_ref, other_ref, out_ref, act):
        act[...] = both_cores(pos_ref, own_ref[...], other_ref[...])
        turn(pos_ref, act, out_ref, whole_place if whole else group_place)

    out = call(
        kernel,
        "turned",
        [SMEM_SPEC, VMEM_SPEC, VMEM_SPEC],
        VMEM_SPEC,
        jax.ShapeDtypeStruct(shape, own.dtype),
        [pltpu.VMEM((2 * toks, feats), own.dtype)],
    )(pos, own, other)
    return out.reshape((2048, 2 * toks) if whole else (8, 256, 2 * toks))


def normed_rows(pos, own, other, chunks, width, at):
    toks, feats = own.shape

    def kernel(pos_ref, own_ref, other_ref, *refs):
        sides, gains, (out_ref, gain_ref, side_ref, wide, act) = refs[:8], refs[8:16], refs[16:]
        for k in range(8):
            wide[k] = gains[k][...].astype(F32).reshape(8, 32, 128)
        for block in range(feats // 128):
            groups = [wide[group_place(pos_ref, block * 4 + k)] for k in range(4)]
            gain_ref[:, block * 128 : (block + 1) * 128] = jnp.concatenate(groups, axis=0).T[:8]
        rows = both_cores(pos_ref, own_ref[...], other_ref[...]).astype(F32)
        inverse = lax.rsqrt(jnp.mean(rows * rows, axis=-1, keepdims=True) + norm_eps)
        act[...] = (rows * inverse * gain_ref[0:1, :]).astype(BF)
        turn(pos_ref, act, out_ref)
        total = jnp.zeros((2 * toks, width), F32)
        for k in range(8):
            turned_rows = out_ref[k].reshape(256, 2 * toks)
            total = total + jnp.dot(turned_rows.T, sides[k][...], preferred_element_type=F32)
        side_ref[...] = total

    specs = [pl.BlockSpec((256, w), lambda i, b=b: (0, b)) for w, b in ((width, at), (128, at + 1))]
    out, gains, side = call(
        kernel,
        "normed_rows",
        [SMEM_SPEC] + [VMEM_SPEC] * 2 + [specs[0]] * 8 + [specs[1]] * 8,
        [VMEM_SPEC] * 3,
        [
            jax.ShapeDtypeStruct((8, 8, 32, 2 * toks), BF),
            jax.ShapeDtypeStruct((8, feats), F32),
            jax.ShapeDtypeStruct((2 * toks, width), F32),
        ],
        [pltpu.VMEM((8, 8, 32, 128), F32), pltpu.VMEM((2 * toks, feats), BF)],
    )(pos, own, other, *chunks, *chunks)
    return out.reshape(8, 256, 2 * toks), gains, side


def turn_back(pos_ref, wide_ref, own_ref, other_ref, place=group_place):
    first = pos_ref[CORE] == 0
    half = wide_ref.shape[-1] // 2
    for block in range(16):
        groups = [wide_ref[place(pos_ref, block * 4 + k)] for k in range(4)]
        rows = jnp.concatenate(groups, axis=0).T.astype(own_ref.dtype)
        at = slice(block * 128, (block + 1) * 128)
        own_ref[:, at] = jnp.where(first, rows[:half], rows[half:])
        other_ref[:, at] = jnp.where(first, rows[half:], rows[:half])


def project(act, chunks, width, at, kind):
    toks = act.shape[-1]

    def kernel(act_ref, *refs):
        weights, out = refs[:8], refs[8]
        total = jnp.zeros((toks, width), F32)
        for k in range(8):
            total = total + jnp.dot(
                act_ref[k].T, weights[k][...], preferred_element_type=F32
            )
        out[...] = total.T.astype(kind)

    return call(
        kernel,
        "project",
        [VMEM_SPEC] + [pl.BlockSpec((256, width), lambda i: (0, at))] * 8,
        VMEM_SPEC,
        jax.ShapeDtypeStruct((width, toks), kind),
    )(act, *chunks)


def unproject(pos, sides):
    count = len(sides)
    toks = sides[0][2].shape[0 if sides[0][3] else 1]
    operands, specs, starts = [], [], []
    for chunks, at, side, flipped in sides:
        width = side.shape[1 if flipped else 0]
        starts.append(len(operands))
        if isinstance(chunks, list):
            operands += chunks
            specs += [pl.BlockSpec((256, width), lambda i, at=at: (0, at))] * 8
        else:
            operands.append(chunks)
            specs.append(VMEM_SPEC)

    def kernel(pos_ref, *refs):
        rights, weights = refs[:count], refs[count : count + len(operands)]
        own_ref, other_ref, wide = refs[count + len(operands) :]
        for k in range(8):
            total = None
            for i, (chunks, at, side, flipped) in enumerate(sides):
                begin = starts[i]
                left = weights[begin + k][...] if isinstance(chunks, list) else weights[begin][k]
                dims = (((1,), (1 if flipped else 0,)), ((), ()))
                part = lax.dot_general(left, rights[i][...], dims, preferred_element_type=F32)
                total = part if total is None else total + part
            wide[k] = total.reshape(8, 32, toks)
        turn_back(pos_ref, wide, own_ref, other_ref)

    return call(
        kernel,
        "unproject",
        [SMEM_SPEC] + [VMEM_SPEC] * count + specs,
        [VMEM_SPEC] * 2,
        [jax.ShapeDtypeStruct((toks // 2, 2048), BF)] * 2,
        [pltpu.VMEM((8, 8, 32, toks), F32)],
    )(pos, *[side[2] for side in sides], *operands)


TILE = 256


def tile_columns(hidden):
    return [(3 * at, at, min(TILE, hidden - at)) for at in range(0, hidden, TILE)]


def feed_forward(pos, normed2, cot, weights):
    toks = normed2.shape[1]
    width = weights.shape[1]
    hidden_units = width // 3
    tiles = tile_columns(hidden_units)

    def kernel(pos_ref, normed_ref, cot_ref, w_ref, grad_ref, *refs):
        d_norm_refs, ffn_refs = refs[:2], refs[2:4]
        normed_rows, cot_rows, pair_weights, down_weights, pair_side, hidden_side, wide = refs[4:]
        j = pl.program_id(0)

        @pl.when(j == 0)
        def _():
            for k in range(8):
                at = slice(k * 256, (k + 1) * 256)
                normed_rows[:, at] = normed_ref[at, :].T
                cot_rows[:, at] = cot_ref[at, :].T

        def tile_step(t, begin):
            pre = jnp.dot(normed_rows[...], w_ref[:, : 2 * t], preferred_element_type=F32)
            d_hidden = jnp.dot(
                cot_rows[...], w_ref[:, 2 * t : 3 * t], preferred_element_type=F32
            )
            gate, up = pre[:, :t], pre[:, t:]
            gate_sig = jax.nn.sigmoid(gate)
            gate_act = gate * gate_sig
            hidden = (gate_act * up).astype(BF)
            d_gate = (d_hidden * up * gate_sig * (1.0 + gate * (1.0 - gate_sig))).astype(BF)
            d_up = (d_hidden * gate_act).astype(BF)
            d_pair = jnp.concatenate([d_gate, d_up], axis=1)
            grad_ref[:, : 2 * t] = jnp.dot(
                normed_ref[...], d_pair, preferred_element_type=F32
            ).astype(BF)
            grad_ref[:, 2 * t : 3 * t] = jnp.dot(
                cot_ref[...], hidden, preferred_element_type=F32
            ).astype(BF)
            pair_at, down_at = pl.ds(2 * begin, 2 * t), pl.ds(begin, t)
            pair_side[:, pair_at] = d_pair
            hidden_side[:, down_at] = hidden
            pair_weights[:, pair_at] = w_ref[:, : 2 * t]
            down_weights[:, down_at] = w_ref[:, 2 * t : 3 * t]

        last = tiles[-1]

        @pl.when(j < len(tiles) - 1)
        def _():
            tile_step(TILE, pl.multiple_of(j * TILE, TILE))

        @pl.when(j == len(tiles) - 1)
        def _():
            tile_step(last[2], last[1])
            dims = (((1,), (1,)), ((), ()))
            for out_refs, left, right in (
                (d_norm_refs, pair_weights, pair_side),
                (ffn_refs, down_weights, hidden_side),
            ):
                wide[...] = lax.dot_general(
                    left[...], right[...], dims, preferred_element_type=F32
                ).reshape(64, 32, toks)
                turn_back(pos_ref, wide, *out_refs, whole_place)

    whole = pl.BlockSpec((2048, toks), lambda j: (0, 0))
    tile = pl.BlockSpec((2048, 3 * TILE), lambda j: (0, j))
    rows = pl.BlockSpec((toks // 2, 2048), lambda j: (0, 0))
    outs = call(
        kernel,
        "feed_forward",
        [SMEM_SPEC, whole, whole, tile],
        [tile] + [rows] * 4,
        [jax.ShapeDtypeStruct((2048, width), BF)]
        + [jax.ShapeDtypeStruct((toks // 2, 2048), BF)] * 4,
        [
            pltpu.VMEM((toks, 2048), BF),
            pltpu.VMEM((toks, 2048), BF),
            pltpu.VMEM((2048, 2 * hidden_units), BF),
            pltpu.VMEM((2048, hidden_units), BF),
            pltpu.VMEM((toks, 2 * hidden_units), BF),
            pltpu.VMEM((toks, hidden_units), BF),
            pltpu.VMEM((64, 32, toks), F32),
        ],
        limit=60,
        grid=(len(tiles),),
    )(pos, normed2, cot, weights)
    return outs[0], outs[1:3], outs[3:5]


SEND_ORDER = (1, 5, 3, 7, 2, 6, 0, 4)


def weight_chunks(terms):
    widths = [r.shape[0] if f else r.shape[1] for l, r, f in terms]
    total = sum(widths)
    operands = [l for l, r, f in terms] + [r for l, r, f in terms]
    count = len(operands)

    def kernel(*refs):
        ins, outs = refs[:count], refs[count : count + 8]
        slots, sem = refs[-2:]
        copies = []
        for step, chunk in enumerate(SEND_ORDER):
            slot = step % 2
            if step >= 2:
                copies[step - 2].wait()
            begin = 0
            for i, (left, right, flipped) in enumerate(terms):
                dims = (((1,), (1 if flipped else 0,)), ((), ()))
                product = lax.dot_general(
                    ins[i][chunk], ins[len(terms) + i][...], dims, preferred_element_type=F32
                )
                slots[slot, :, begin : begin + widths[i]] = product.astype(BF)
                begin += widths[i]
            copies.append(pltpu.make_async_copy(slots.at[slot], outs[chunk], sem.at[slot]))
            copies[step].start()
        copies[-2].wait()
        copies[-1].wait()

    return call(
        kernel,
        "weight_chunks",
        [VMEM_SPEC] * count,
        [ANY_SPEC] * 8,
        [jax.ShapeDtypeStruct((256, total), BF)] * 8,
        [pltpu.VMEM((2, 256, total), BF), pltpu.SemaphoreType.DMA((2,))],
    )(*operands)


def summed(parts):
    total = parts[0].astype(F32)
    for part in parts[1:]:
        total = total + part.astype(F32)
    return total


def scatter_first(chunks):
    first = []
    for h, axis in ((0, "y"), (1, "z")):
        first += [chunks[4 * h]] + [hand(chunks[4 * h + d], axis, d) for d in (1, 2, 3)]
    return first


def scatter_second(first, beside):
    second = []
    for terms, axis in ((first[:4], "z"), (first[4:], "y")):
        parts = [summed([t[d * 64 : (d + 1) * 64] for t in terms]).astype(BF) for d in range(4)]
        second.append([parts[0]] + [hand(parts[d], axis, d) for d in (1, 2, 3)])
    shares = [summed(terms) for terms in second]
    give = jnp.concatenate([share[32:].astype(BF) for share in shares], axis=0)
    give, beside = tie(give, beside)
    got = fetch(give, "x", 1).astype(F32)
    return shares[0][:32] + got[:32], shares[1][:32] + got[32:], beside


def prepared(pos, q, out_t, kv, gate, up, down_t, gains):
    rows = q.shape[0]
    hidden = gate.shape[1] // 2
    attn_width = (q.shape[1] + out_t.shape[1] + kv.shape[1]) // 2 + 128

    def kernel(pos_ref, q_ref, out_t_ref, kv_ref, gate_ref, up_ref, down_ref, *refs):
        gain_refs, (attn_mine, attn_give, ffn_mine, ffn_give) = refs[:2], refs[2:]
        first = pos_ref[CORE] == 0

        def put(mine_ref, give_ref, to, source, at, width):
            half = source.shape[1] // 2
            one, two = source[:, at : at + width], source[:, half + at : half + at + width]
            mine_ref[:, to : to + width] = jnp.where(first, one, two)
            give_ref[:, to : to + width] = jnp.where(first, two, one)

        begin = 0
        for ref in (q_ref, out_t_ref, kv_ref):
            width = ref.shape[1] // 2
            put(attn_mine, attn_give, begin, ref, 0, width)
            begin += width
        same = lax.broadcasted_iota(jnp.int32, (rows, rows), 0) == lax.broadcasted_iota(
            jnp.int32, (rows, rows), 1
        )
        lane = lax.broadcasted_iota(jnp.int32, (rows, 128), 1)
        block = jnp.zeros((rows, 128), F32)
        for i, ref in enumerate(gain_refs):
            column = jnp.sum(jnp.where(same, ref[...].astype(F32), 0.0), axis=1, keepdims=True)
            block = jnp.where(lane == i, column, block)
        attn_mine[:, begin:] = block.astype(BF)
        attn_give[:, begin:] = block.astype(BF)
        for begin, unit, width in tile_columns(hidden):
            for i, ref in enumerate((gate_ref, up_ref, down_ref)):
                put(ffn_mine, ffn_give, begin + i * width, ref, unit, width)

    return call(
        kernel,
        "prepared",
        [SMEM_SPEC] + [VMEM_SPEC] * 8,
        [VMEM_SPEC] * 4,
        [jax.ShapeDtypeStruct((rows, attn_width), BF)] * 2
        + [jax.ShapeDtypeStruct((rows, 3 * hidden), BF)] * 2,
        limit=60,
    )(pos, q, out_t, kv, gate, up, down_t, *[g.reshape(1, -1) for g in gains])


def unpacked(pos, mine, other, layout):
    rows = mine.shape[0]
    halves = [sum(w for b, w in pieces) for pieces in layout]

    def kernel(pos_ref, mine_ref, other_ref, *outs):
        first = pos_ref[CORE] == 0
        for out, half, pieces in zip(outs, halves, layout):
            to = 0
            for begin, width in pieces:
                one, two = mine_ref[:, begin : begin + width], other_ref[:, begin : begin + width]
                out[:, to : to + width] = jnp.where(first, one, two)
                out[:, half + to : half + to + width] = jnp.where(first, two, one)
                to += width

    return call(
        kernel,
        "unpacked",
        [SMEM_SPEC] + [VMEM_SPEC] * 2,
        [VMEM_SPEC] * len(layout),
        [jax.ShapeDtypeStruct((rows, 2 * half), F32) for half in halves],
    )(pos, mine, other)


def arranged(pos, mine, other):
    count, head_dim = mine.shape
    block = 1024

    def kernel(pos_ref, mine_ref, other_ref, k_ref, v_ref, kt_ref, vt_ref):
        first = pos_ref[CORE] == 0
        one, two = mine_ref[...], other_ref[...]
        keys, values = jnp.where(first, one, two), jnp.where(first, two, one)
        k_ref[...] = keys
        v_ref[...] = values
        kt_ref[...] = keys.T
        vt_ref[...] = values.T

    rows = pl.BlockSpec((block, head_dim), lambda i: (i, 0))
    columns = pl.BlockSpec((head_dim, block), lambda i: (0, i))
    natural = jax.ShapeDtypeStruct((count, head_dim), BF)
    across = jax.ShapeDtypeStruct((head_dim, count), BF)
    return call(
        kernel,
        "arranged",
        [SMEM_SPEC, rows, rows],
        [rows, rows, columns, columns],
        [natural, natural, across, across],
        grid=(count // block,),
    )(pos, mine, other)


def key_gradients(pos, act, d_keyval, tokens, d_own, d_other, ffn_gain):
    toks, width = d_keyval.shape

    def kernel(pos_ref, act_ref, side_ref, tokens_ref, own_ref, other_ref, ffn_ref, out_ref, wide):
        for k in range(8):
            product = jnp.dot(act_ref[k], side_ref[...], preferred_element_type=F32)
            wide[k] = product.reshape(8, 32, width)
        rows = tokens_ref[...].astype(F32)
        inverse = lax.rsqrt(jnp.mean(rows * rows, axis=-1, keepdims=True) + norm_eps)
        d_normed = own_ref[...].astype(F32) + other_ref[...].astype(F32)
        attn_gain = jnp.sum(d_normed * rows * inverse, axis=0, keepdims=True)
        gains = jnp.concatenate(
            [attn_gain, 0.5 * ffn_ref[...], jnp.zeros((126, rows.shape[1]), F32)], axis=0
        )
        for block in range(16):
            groups = [wide[group_place(pos_ref, block * 4 + k)] for k in range(4)]
            at = slice(block * 128, (block + 1) * 128)
            out_ref[at, :width] = jnp.concatenate(groups, axis=0).astype(BF)
            out_ref[at, width:] = gains[:, at].T.astype(BF)

    return call(
        kernel,
        "key_gradients",
        [SMEM_SPEC] + [VMEM_SPEC] * 6,
        VMEM_SPEC,
        jax.ShapeDtypeStruct((2048, width + 128), BF),
        [pltpu.VMEM((8, 8, 32, width), F32)],
    )(pos, act, d_keyval, tokens, d_own, d_other, ffn_gain)


def allowed_keys(begin, count, places, starts):
    shape = (count, places.shape[1])
    key_place = begin + lax.broadcasted_iota(jnp.int32, shape, 0)
    return (key_place <= places) & (key_place >= starts)


def row_places(pos_ref, docs_ref, own, rows):
    half = rows // 2
    base = (pos_ref[Z] * 4 + pos_ref[Y]) * rows + jnp.where(own, pos_ref[CORE] * half, 0)
    lane = lax.broadcasted_iota(jnp.int32, (1, rows), 1)
    places = base + jnp.where(own, lax.rem(lane, half), lane)
    end = start = jnp.int32(0)
    starts = jnp.zeros((1, rows), jnp.int32)
    for j in range(docs_ref.shape[1]):
        length = docs_ref[pos_ref[X], j]
        end = end + length
        start = start + jnp.where(base >= end, length, 0)
        starts = starts + jnp.where(places >= end, length, 0)
    last = base + jnp.where(own, half, rows) - 1
    return places, starts, lax.div(start, KEY_BLOCK), lax.div(last, KEY_BLOCK) + 1


def attend_kernel(pos_ref, docs_ref, qt_ref, k_ref, vt_ref, ot_ref, lse_ref, *, first_set, scale):
    units, head_dim, rows = qt_ref.shape
    own = pl.program_id(0) * units >= first_set
    places, starts, low, high = row_places(pos_ref, docs_ref, own, rows)

    def step(j, carry):
        begin = pl.multiple_of(j * KEY_BLOCK, KEY_BLOCK)
        keys = k_ref[pl.ds(begin, KEY_BLOCK), :]
        values = vt_ref[:, pl.ds(begin, KEY_BLOCK)]
        allowed = allowed_keys(begin, KEY_BLOCK, places, starts)
        out = []
        for u in range(units):
            top, mass, acc = carry[u]
            scores = jnp.dot(keys, qt_ref[u], preferred_element_type=F32)
            scores = jnp.where(allowed, scores, masked_fill)
            new_top = jnp.maximum(top, jnp.max(scores, axis=0, keepdims=True))
            weights = jnp.exp2((scores - new_top) * scale)
            shrink = jnp.exp2((top - new_top) * scale)
            mass = mass * shrink + jnp.sum(weights, axis=0, keepdims=True)
            acc = acc * shrink + jnp.dot(
                values, weights.astype(BF), preferred_element_type=F32
            )
            out.append((new_top, mass, acc))
        return tuple(out)

    start = (
        jnp.full((1, rows), masked_fill, F32),
        jnp.zeros((1, rows), F32),
        jnp.zeros((head_dim, rows), F32),
    )
    done = lax.fori_loop(low, high, step, (start,) * units)
    for u in range(units):
        top, mass, acc = done[u]
        ot_ref[u] = acc / mass
        lse_ref[u] = top * scale + jnp.log2(mass)


def attend(pos, docs, qt, keys, values_t, scale):
    units = 2
    blocks, head_dim, rows = qt.shape
    count = keys.shape[0]
    first_set = blocks // 2
    block = pl.BlockSpec((units, head_dim, rows), lambda i, p, d: (i, 0, 0))
    return pl.pallas_call(
        functools.partial(attend_kernel, first_set=first_set, scale=scale),
        grid_spec=pltpu.PrefetchScalarGridSpec(
            num_scalar_prefetch=2,
            grid=(blocks // units,),
            in_specs=[
                block,
                pl.BlockSpec((count, head_dim), lambda i, p, d: (0, 0)),
                pl.BlockSpec((head_dim, count), lambda i, p, d: (0, 0)),
            ],
            out_specs=[block, pl.BlockSpec((units, 1, rows), lambda i, p, d: (i, 0, 0))],
        ),
        out_shape=[
            jax.ShapeDtypeStruct((blocks, head_dim, rows), F32),
            jax.ShapeDtypeStruct((blocks, 1, rows), F32),
        ],
        compiler_params=pltpu.CompilerParams(vmem_limit_bytes=28 * MB),
        cost_estimate=SMALL,
        name="attend",
    )(pos, docs, qt, keys, values_t)


def attend_back_kernel(
    pos_ref, docs_ref, qt_ref, dot_ref, ot_ref, lse_ref, k_ref, kt_ref, v_ref,
    dqt_ref, mine_ref, give_ref, dk_ref, dv_ref, *, first_set, scale, score_scale,
):
    units, head_dim, rows = qt_ref.shape

    @pl.when(pl.program_id(0) == 0)
    def _():
        dk_ref[...] = jnp.zeros_like(dk_ref)
        dv_ref[...] = jnp.zeros_like(dv_ref)

    own = pl.program_id(0) * units >= first_set
    places, starts, low, high = row_places(pos_ref, docs_ref, own, rows)
    queries = [qt_ref[u].T for u in range(units)]
    d_outs = [dot_ref[u].T for u in range(units)]
    deltas = [
        jnp.sum(dot_ref[u].astype(F32) * ot_ref[u], axis=0, keepdims=True) for u in range(units)
    ]

    def step(j, carry):
        begin = pl.multiple_of(j * KEY_BLOCK, KEY_BLOCK)
        part = pl.ds(begin, KEY_BLOCK)
        allowed = allowed_keys(begin, KEY_BLOCK, places, starts)
        out = []
        d_keys = d_values = None
        for u in range(units):
            scores = jnp.dot(k_ref[part, :], qt_ref[u], preferred_element_type=F32)
            d_probs = jnp.dot(v_ref[part, :], dot_ref[u], preferred_element_type=F32)
            probs = jnp.where(allowed, jnp.exp2(scores * scale - lse_ref[u]), 0.0)
            d_scores = (probs * (d_probs - deltas[u])).astype(BF)
            for_keys = jnp.dot(d_scores, queries[u], preferred_element_type=F32)
            for_values = jnp.dot(probs.astype(BF), d_outs[u], preferred_element_type=F32)
            d_keys = for_keys if u == 0 else d_keys + for_keys
            d_values = for_values if u == 0 else d_values + for_values
            out.append(
                carry[u] + jnp.dot(kt_ref[:, part], d_scores, preferred_element_type=F32)
            )
        dk_ref[part, :] += d_keys
        dv_ref[part, :] += d_values
        return tuple(out)

    start = jnp.zeros((head_dim, rows), F32)
    done = lax.fori_loop(low, high, step, (start,) * units)
    for u in range(units):
        dqt_ref[u] = done[u] * score_scale

    @pl.when(pl.program_id(0) == pl.num_programs(0) - 1)
    def _():
        first = pos_ref[CORE] == 0
        d_keys, d_values = dk_ref[...] * score_scale, dv_ref[...]
        mine_ref[...] = jnp.where(first, d_keys, d_values)
        give_ref[...] = jnp.where(first, d_values, d_keys).astype(BF)


def attend_back(pos, docs, qt, d_out_t, out_t, lse, keys, keys_t, values, scale, score_scale):
    units = 2
    blocks, head_dim, rows = qt.shape
    count = keys.shape[0]
    first_set = blocks // 2
    block = pl.BlockSpec((units, head_dim, rows), lambda i, p, d: (i, 0, 0))
    whole = pl.BlockSpec((count, head_dim), lambda i, p, d: (0, 0))
    return pl.pallas_call(
        functools.partial(
            attend_back_kernel, first_set=first_set, scale=scale, score_scale=score_scale
        ),
        grid_spec=pltpu.PrefetchScalarGridSpec(
            num_scalar_prefetch=2,
            grid=(blocks // units,),
            in_specs=[
                block,
                block,
                block,
                pl.BlockSpec((units, 1, rows), lambda i, p, d: (i, 0, 0)),
                whole,
                pl.BlockSpec((head_dim, count), lambda i, p, d: (0, 0)),
                whole,
            ],
            out_specs=[block, whole, whole],
            scratch_shapes=[pltpu.VMEM((count, head_dim), F32)] * 2,
        ),
        out_shape=[
            jax.ShapeDtypeStruct((blocks, head_dim, rows), F32),
            jax.ShapeDtypeStruct((count, head_dim), F32),
            jax.ShapeDtypeStruct((count, head_dim), BF),
        ],
        compiler_params=pltpu.CompilerParams(vmem_limit_bytes=44 * MB),
        cost_estimate=SMALL,
        name="attend_back",
    )(pos, docs, qt, d_out_t, out_t, lse, keys, keys_t, values)


def doc_starts(lengths, places):
    ends = jnp.cumsum(lengths)
    passed = (places[:, None] >= ends[None, :]).astype(jnp.int32)
    return jnp.sum(passed * lengths[None, :], axis=1)


def rotate_rows(values, cosine, sine):
    half = values.shape[-1] // 2
    one, two = values[..., :half], values[..., half:]
    return jnp.concatenate([one * cosine - two * sine, two * cosine + one * sine], axis=-1)


def rotate_columns(values, cosine, sine):
    half = values.shape[1] // 2
    one, two = values[:, :half], values[:, half:]
    return jnp.concatenate([one * cosine - two * sine, two * cosine + one * sine], axis=1)


def head_blocks(array):
    toks, width = array.shape
    count = width // 256

    def kernel(array_ref, out_ref):
        for b in range(count):
            for i in range(2):
                at = (2 * b + i) * 128
                out_ref[b, :, i * toks : (i + 1) * toks] = array_ref[:, at : at + 128].T

    shape = jax.ShapeDtypeStruct((count, 128, 2 * toks), array.dtype)
    return call(kernel, "head_blocks", [VMEM_SPEC], VMEM_SPEC, shape)(array)


def head_blocks_back(blocks, begin):
    total, head_dim, wide = blocks.shape
    count, toks = total - begin, wide // 2

    def kernel(blocks_ref, out_ref):
        for b in range(count):
            for i in range(2):
                at = (2 * b + i) * 128
                out_ref[:, at : at + 128] = blocks_ref[b, :, i * toks : (i + 1) * toks].T

    shape = jax.ShapeDtypeStruct((toks, count * 256), blocks.dtype)
    spec = pl.BlockSpec((count, head_dim, wide), lambda i: (begin // count, 0, 0))
    return call(kernel, "head_blocks_back", [spec], VMEM_SPEC, shape)(blocks)


def on_device(
    tokens, doc_lengths, attn_gain, q_weight, kv_weight, out_weight, ffn_gain,
    gate_weight, up_weight, down_weight, second_queries, out_cotangent, second_cotangent,
):
    x, z, y, c = (lax.axis_index(a) for a in ("x", "z", "y", "c"))
    first = c == 0
    pos = jnp.stack([x, z, y, c]).astype(jnp.int32)
    toks, width = tokens.shape
    head_dim = kv_weight.shape[1] // 2
    score_scale = head_dim ** (-0.5)
    scale = score_scale * math.log2(math.e)
    rows = q_weight.shape[0]

    def swap(own):
        return fetch(own, "c", 1)

    n_q, n_kv = q_weight.shape[1] // 2, head_dim
    n_out, n_ffn = out_weight.shape[0] // 2, down_weight.shape[0] // 2
    n_attn = n_q + n_out
    at_out, at_kv = n_q // n_out, n_attn // n_kv
    attn_mine, attn_give, ffn_mine, ffn_give = prepared(
        pos, q_weight, out_weight.T, kv_weight, gate_weight, up_weight, down_weight.T,
        (attn_gain, ffn_gain),
    )
    attn_other, ffn_other, tokens_other, cot_other = tie(
        swap(attn_give), swap(ffn_give), swap(tokens), swap(out_cotangent)
    )
    *attn_rows, ffn_mine, ffn_other = tie(*across_x(attn_mine, attn_other), ffn_mine, ffn_other)
    ffn_both = jnp.concatenate([ffn_mine, ffn_other], axis=0)
    blocks = first_blocks(attn_rows)
    ffn_got, *blocks = tie(fetch(ffn_both, "x", 1), *blocks[0], *blocks[1])
    ffn_rows = jnp.concatenate([ffn_both, ffn_got], axis=0)
    ffn_whole = lax.all_gather(ffn_rows, ("z", "y"), axis=0, tiled=True)
    attn_pair = second_pair([jnp.concatenate(b, axis=0) for b in (blocks[:4], blocks[4:])])
    attn_chunks = far_blocks(attn_pair, tie(*near_blocks(attn_pair)))
    attn_chunks = [jnp.concatenate(w, axis=0) if isinstance(w, tuple) else w for w in attn_chunks]
    def over_tp(rows):
        send = rows.astype(BF)
        return send.astype(F32) + fetch(send, "t", 1).astype(F32)

    def reduce_rows(own, other):
        return over_tp(own.astype(F32) + swap(other).astype(F32))

    places = (z * 4 + y) * (2 * toks) + jnp.arange(2 * toks, dtype=jnp.int32)
    starts = doc_starts(jnp.where(x == 0, doc_lengths[0], doc_lengths[1]), places)
    positions = (places - starts).astype(F32)
    inverse_freq = jnp.exp(
        jnp.arange(head_dim // 2, dtype=F32) * (-2.0 * math.log(rope_base) / head_dim)
    )
    angles_t = inverse_freq[:, None] * positions[None, :]
    cos_t, sin_t = jnp.cos(angles_t), jnp.sin(angles_t)

    inputs = tokens.astype(F32)
    inv_attn = lax.rsqrt(jnp.mean(inputs * inputs, axis=-1, keepdims=True) + norm_eps)
    second_t, second_cot_t = head_blocks(second_queries), head_blocks(second_cotangent)
    cot_t = turned(pos, out_cotangent, cot_other, whole=True)
    cos_r, sin_r = cos_t.T, sin_t.T
    normed_t, gain_rows, keyval = normed_rows(pos, tokens, tokens_other, attn_chunks, n_kv, at_kv)
    gain_one, gain_two = gain_rows[0:1], gain_rows[1:2]
    kv_own = jnp.where(first, rotate_rows(keyval, cos_r, sin_r), keyval).astype(BF)
    kv_sent = jnp.broadcast_to(kv_own[None], (16,) + kv_own.shape)
    kv_all = lax.all_to_all(kv_sent, ("z", "y"), 0, 0).reshape(-1, head_dim)
    queries_t = project(normed_t, attn_chunks, n_q, 0, F32)
    query_rot = rotate_columns(queries_t.reshape(-1, head_dim, 2 * toks), cos_t, sin_t).astype(BF)
    keys, values, keys_t, values_t = arranged(pos, kv_all, swap(kv_all))
    query_t = jnp.concatenate([query_rot, second_t], axis=0)
    out_t, lse = attend(pos, doc_lengths, query_t, keys, values_t, scale)
    n_first = query_rot.shape[0]
    second_out = head_blocks_back(out_t, n_first)
    attended_t = out_t[:n_first].reshape(-1, 2 * toks).astype(BF)

    branch = reduce_rows(*unproject(pos, [(attn_chunks, at_out, attended_t, False)]))
    resid = inputs + branch
    inv_ffn = lax.rsqrt(jnp.mean(resid * resid, axis=-1, keepdims=True) + norm_eps)
    normed2 = (resid * inv_ffn * gain_two).astype(BF)
    normed2_t = turned(pos, normed2, swap(normed2), whole=True)
    ffn_grads, d_norm2_part, ffn_part = feed_forward(pos, normed2_t, cot_t, ffn_whole)
    ffn_share = lax.psum_scatter(ffn_grads, ("z", "y"), scatter_dimension=0, tiled=True)
    d_normed2 = reduce_rows(*d_norm2_part)

    scaled_two = gain_two * d_normed2
    ffn_gain_part = jnp.sum(d_normed2 * resid * inv_ffn, axis=0)
    d_resid = (
        out_cotangent.astype(F32)
        + inv_ffn * scaled_two
        - resid * inv_ffn**3 * jnp.mean(scaled_two * resid, axis=-1, keepdims=True)
    )
    d_branch = d_resid.astype(BF)

    d_branch_t = turned(pos, d_branch, swap(d_branch))
    d_attended_t = project(d_branch_t, attn_chunks, n_out, at_out, BF)
    d_out_t = jnp.concatenate(
        [d_attended_t.reshape(-1, head_dim, 2 * toks), second_cot_t], axis=0
    )
    d_query_t, kv_mine, kv_give = attend_back(
        pos, doc_lengths, query_t, d_out_t, out_t, lse, keys, keys_t, values, scale, score_scale
    )
    kv_give, d_query_t, *ffn_part = tie(kv_give, d_query_t, *ffn_part)
    ffn_sum = reduce_rows(*ffn_part)
    kv_other = swap(kv_give)
    second_queries_grad = head_blocks_back(d_query_t, n_first)
    d_queries_t = rotate_columns(d_query_t[:n_first], cos_t, -sin_t).reshape(-1, 2 * toks).astype(BF)

    attn_grads = weight_chunks([(normed_t, d_queries_t, True), (d_branch_t, attended_t, True)])
    kv_chip = (kv_mine + kv_other.astype(F32)).astype(BF).reshape(16, 2 * toks, head_dim)
    kv_chip, *attn_grads = tie(kv_chip, *attn_grads)
    kv_parts = lax.all_to_all(kv_chip, ("z", "y"), 0, 0)
    kv_parts, ffn_sum = tie(kv_parts, ffn_sum)
    kv_sum = jnp.sum(kv_parts.astype(F32), axis=0)
    result = resid + ffn_sum
    d_keyval = jnp.where(first, rotate_rows(kv_sum, cos_r, -sin_r), kv_sum).astype(BF)
    d_norm_part = unproject(
        pos, [(attn_chunks, 0, d_queries_t, False), (attn_chunks, at_kv, d_keyval, True)]
    )
    d_norm_other = swap(d_norm_part[1])
    d_normed = over_tp(d_norm_part[0].astype(F32) + d_norm_other.astype(F32))
    kv_grads = key_gradients(
        pos, normed_t, d_keyval, tokens, d_norm_part[0], d_norm_other, ffn_gain_part[None]
    )
    kv_got = lax.all_to_all(kv_grads.reshape(32, 2, rows, -1), ("x", "z", "y"), 0, 0)
    kv_got, *attn_terms = tie(kv_got, *scatter_first(attn_grads))
    ffn_got = fetch(ffn_share[64:], "x", 1)
    attn_share, attn_give, ffn_got = scatter_second(attn_terms, ffn_got)
    ffn_sums = ffn_share[:64].astype(F32) + ffn_got.astype(F32)
    kv_share = jnp.sum(kv_got.astype(F32), axis=0)
    scaled_one = gain_one * d_normed
    tokens_grad = (
        d_resid
        + inv_attn * scaled_one
        - inputs * inv_attn**3 * jnp.mean(scaled_one * inputs, axis=-1, keepdims=True)
    )

    gate_grad, up_grad, down_grad_t = unpacked(
        pos,
        ffn_sums[:32],
        swap(ffn_sums[32:]),
        [[(b + i * w, w) for b, unit, w in tile_columns(n_ffn)] for i in range(3)],
    )
    q_grad, out_grad_t = unpacked(pos, attn_share, swap(attn_give), [[(0, n_q)], [(n_q, n_out)]])
    kv_mine, kv_give = (jnp.where(first, kv_share[i], kv_share[1 - i]) for i in (0, 1))
    kv_other = swap(kv_give)
    kv_gain = jnp.concatenate(
        [
            in_order(first, kv_mine[:, :n_kv], kv_other[:, :n_kv], 1),
            kv_mine[:, n_kv:] + kv_other[:, n_kv:],
        ],
        axis=1,
    )
    kv_gain = kv_gain + fetch(kv_gain, "t", 1)
    return (
        result,
        second_out,
        tokens_grad,
        kv_gain[:, 2 * n_kv],
        q_grad,
        kv_gain[:, : 2 * n_kv],
        out_grad_t.T,
        kv_gain[:, 2 * n_kv + 1],
        gate_grad,
        up_grad,
        down_grad_t.T,
        second_queries_grad,
    )


def solution(mesh):
    fine = Mesh(mesh.devices.reshape(2, 4, 4, 2, 2), ("x", "z", "y", "c", "t"))
    seq = ("x", "z", "y", "c")
    rows, both, turned_both = P(seq, None), P(seq, "t"), P("t", seq)
    in_specs = (
        rows, P(), P(seq), both, rows, turned_both, P(seq), both, both, turned_both, both, rows, both,
    )
    out_specs = (
        rows, both, rows, P(seq), both, rows, turned_both, P(seq), both, both, turned_both, both,
    )
    return jax.shard_map(
        on_device, mesh=fine, in_specs=in_specs, out_specs=out_specs, check_vma=False
    )
```

```python
import functools
import math

import jax
import jax.numpy as jnp
from jax import lax
from jax.experimental import pallas as pl
from jax.experimental.pallas import tpu as pltpu
from jax.sharding import Mesh, PartitionSpec as P

norm_eps = 1e-05
rope_base = 10000.0
masked_fill = -1e30
KEY_BLOCK = 1024
BF = jnp.bfloat16
F32 = jnp.float32
MB = 1024 * 1024


def fetch(block, axis, offset):
    n = lax.axis_size(axis)
    return lax.ppermute(block, axis, [((i + offset) % n, i) for i in range(n)])


def hand(block, axis, offset):
    return fetch(block, axis, -offset)


def in_order(first, mine, other, axis):
    return jnp.where(
        first,
        jnp.concatenate([mine, other], axis=axis),
        jnp.concatenate([other, mine], axis=axis),
    )


X, Z, Y, CORE = 0, 1, 2, 3


def near_blocks(pair):
    return [fetch(block, axis, d) for block, axis in pair for d in (1, 3)]


def far_blocks(pair, near):
    out = []
    for i, (block, axis) in enumerate(pair):
        after, before = near[2 * i : 2 * i + 2]
        half = block.shape[0] // 2
        far = (fetch(after[:half], axis, 1), fetch(before[half:], axis, 3))
        out.append([block, after, far, before])
    return out[0] + out[1]


def across_x(mine, other):
    rows = mine.shape[0]
    got = fetch(jnp.concatenate([mine, other], axis=0), "x", 1)
    return [
        jnp.concatenate([mine, got[:rows]], axis=0),
        jnp.concatenate([other, got[rows:]], axis=0),
    ]


def first_blocks(pieces):
    return [
        [piece] + [fetch(piece, axis, d) for d in (1, 2, 3)] for piece, axis in zip(pieces, ("z", "y"))
    ]


def second_pair(halves):
    return [(halves[0], "y"), (halves[1], "z")]


def place_in_chunks(pos_ref, x, z, y, dh):
    dx = lax.rem(x - pos_ref[X] + 2, 2)
    dz = lax.rem(z - pos_ref[Z] + 4, 4)
    dy = lax.rem(y - pos_ref[Y] + 4, 4)
    own = dh == 0
    return dh * 4 + jnp.where(own, dy, dz), jnp.where(own, dz, dy) * 2 + dx


def group_place(pos_ref, group):
    h, y, z, x = group % 2, group // 2 % 4, group // 8 % 4, group // 32
    return place_in_chunks(pos_ref, x, z, y, lax.rem(h + pos_ref[CORE], 2))


def whole_place(pos_ref, group):
    h, y, z, x = group % 2, group // 2 % 4, group // 8 % 4, group // 32
    dx = lax.rem(x - pos_ref[X] + 2, 2)
    return (z * 4 + y) * 4 + dx * 2 + lax.rem(h + pos_ref[CORE], 2)


SMEM_SPEC = pl.BlockSpec(memory_space=pltpu.SMEM)
VMEM_SPEC = pl.BlockSpec(memory_space=pltpu.VMEM)
ANY_SPEC = pl.BlockSpec(memory_space=pl.ANY)
SMALL = pl.CostEstimate(flops=1024, bytes_accessed=1024, transcendentals=0)


def call(kernel, name, in_specs, out_specs, out_shape, scratch=(), limit=24, grid=None, **more):
    return pl.pallas_call(
        kernel,
        grid=grid or (1,),
        in_specs=in_specs,
        out_specs=out_specs,
        out_shape=out_shape,
        scratch_shapes=scratch,
        compiler_params=pltpu.CompilerParams(vmem_limit_bytes=limit * MB),
        cost_estimate=SMALL,
        name=name,
        **more,
    )


def tie(*arrays):
    return list(lax.optimization_barrier(arrays))


def both_cores(pos_ref, own, other):
    first = pos_ref[CORE] == 0
    return jnp.concatenate(
        [jnp.where(first, own, other), jnp.where(first, other, own)], axis=0
    )


def turn(pos_ref, act_ref, out_ref, place=group_place):
    for block in range(16):
        part = act_ref[:, block * 128 : (block + 1) * 128].T
        for k in range(4):
            out_ref[place(pos_ref, block * 4 + k)] = part[k * 32 : (k + 1) * 32]


def turned(pos, own, other, whole=False):
    toks, feats = own.shape
    shape = (64, 32, 2 * toks) if whole else (8, 8, 32, 2 * toks)

    def kernel(pos_ref, own_ref, other_ref, out_ref, act):
        act[...] = both_cores(pos_ref, own_ref[...], other_ref[...])
        turn(pos_ref, act, out_ref, whole_place if whole else group_place)

    out = call(
        kernel,
        "turned",
        [SMEM_SPEC, VMEM_SPEC, VMEM_SPEC],
        VMEM_SPEC,
        jax.ShapeDtypeStruct(shape, own.dtype),
        [pltpu.VMEM((2 * toks, feats), own.dtype)],
    )(pos, own, other)
    return out.reshape((2048, 2 * toks) if whole else (8, 256, 2 * toks))


def normed_rows(pos, own, other, chunks, width, at):
    toks, feats = own.shape

    def kernel(pos_ref, own_ref, other_ref, *refs):
        sides, gains, (out_ref, gain_ref, side_ref, wide, act) = refs[:8], refs[8:16], refs[16:]
        for k in range(8):
            wide[k] = gains[k][...].astype(F32).reshape(8, 32, 128)
        for block in range(feats // 128):
            groups = [wide[group_place(pos_ref, block * 4 + k)] for k in range(4)]
            gain_ref[:, block * 128 : (block + 1) * 128] = jnp.concatenate(groups, axis=0).T[:8]
        rows = both_cores(pos_ref, own_ref[...], other_ref[...]).astype(F32)
        inverse = lax.rsqrt(jnp.mean(rows * rows, axis=-1, keepdims=True) + norm_eps)
        act[...] = (rows * inverse * gain_ref[0:1, :]).astype(BF)
        turn(pos_ref, act, out_ref)
        total = jnp.zeros((2 * toks, width), F32)
        for k in range(8):
            turned_rows = out_ref[k].reshape(256, 2 * toks)
            total = total + jnp.dot(turned_rows.T, sides[k][...], preferred_element_type=F32)
        side_ref[...] = total

    specs = [pl.BlockSpec((256, w), lambda i, b=b: (0, b)) for w, b in ((width, at), (128, at + 1))]
    out, gains, side = call(
        kernel,
        "normed_rows",
        [SMEM_SPEC] + [VMEM_SPEC] * 2 + [specs[0]] * 8 + [specs[1]] * 8,
        [VMEM_SPEC] * 3,
        [
            jax.ShapeDtypeStruct((8, 8, 32, 2 * toks), BF),
            jax.ShapeDtypeStruct((8, feats), F32),
            jax.ShapeDtypeStruct((2 * toks, width), F32),
        ],
        [pltpu.VMEM((8, 8, 32, 128), F32), pltpu.VMEM((2 * toks, feats), BF)],
    )(pos, own, other, *chunks, *chunks)
    return out.reshape(8, 256, 2 * toks), gains, side


def turn_back(pos_ref, wide_ref, own_ref, other_ref, place=group_place):
    first = pos_ref[CORE] == 0
    half = wide_ref.shape[-1] // 2
    for block in range(16):
        groups = [wide_ref[place(pos_ref, block * 4 + k)] for k in range(4)]
        rows = jnp.concatenate(groups, axis=0).T.astype(own_ref.dtype)
        at = slice(block * 128, (block + 1) * 128)
        own_ref[:, at] = jnp.where(first, rows[:half], rows[half:])
        other_ref[:, at] = jnp.where(first, rows[half:], rows[:half])


def project(act, chunks, width, at, kind):
    toks = act.shape[-1]

    def kernel(act_ref, *refs):
        weights, out = refs[:8], refs[8]
        total = jnp.zeros((toks, width), F32)
        for k in range(8):
            total = total + jnp.dot(
                act_ref[k].T, weights[k][...], preferred_element_type=F32
            )
        out[...] = total.T.astype(kind)

    return call(
        kernel,
        "project",
        [VMEM_SPEC] + [pl.BlockSpec((256, width), lambda i: (0, at))] * 8,
        VMEM_SPEC,
        jax.ShapeDtypeStruct((width, toks), kind),
    )(act, *chunks)


def unproject(pos, sides):
    count = len(sides)
    toks = sides[0][2].shape[0 if sides[0][3] else 1]
    operands, specs, starts = [], [], []
    for chunks, at, side, flipped in sides:
        width = side.shape[1 if flipped else 0]
        starts.append(len(operands))
        if isinstance(chunks, list):
            operands += chunks
            specs += [pl.BlockSpec((256, width), lambda i, at=at: (0, at))] * 8
        else:
            operands.append(chunks)
            specs.append(VMEM_SPEC)

    def kernel(pos_ref, *refs):
        rights, weights = refs[:count], refs[count : count + len(operands)]
        own_ref, other_ref, wide = refs[count + len(operands) :]
        for k in range(8):
            total = None
            for i, (chunks, at, side, flipped) in enumerate(sides):
                begin = starts[i]
                left = weights[begin + k][...] if isinstance(chunks, list) else weights[begin][k]
                dims = (((1,), (1 if flipped else 0,)), ((), ()))
                part = lax.dot_general(left, rights[i][...], dims, preferred_element_type=F32)
                total = part if total is None else total + part
            wide[k] = total.reshape(8, 32, toks)
        turn_back(pos_ref, wide, own_ref, other_ref)

    return call(
        kernel,
        "unproject",
        [SMEM_SPEC] + [VMEM_SPEC] * count + specs,
        [VMEM_SPEC] * 2,
        [jax.ShapeDtypeStruct((toks // 2, 2048), BF)] * 2,
        [pltpu.VMEM((8, 8, 32, toks), F32)],
    )(pos, *[side[2] for side in sides], *operands)


TILE = 256


def tile_columns(hidden):
    return [(3 * at, at, min(TILE, hidden - at)) for at in range(0, hidden, TILE)]


def feed_forward(pos, normed2, cot, weights):
    toks = normed2.shape[1]
    width = weights.shape[1]
    hidden_units = width // 3
    tiles = tile_columns(hidden_units)

    def kernel(pos_ref, normed_ref, cot_ref, w_ref, grad_ref, *refs):
        d_norm_refs, ffn_refs = refs[:2], refs[2:4]
        normed_rows, cot_rows, pair_weights, down_weights, pair_side, hidden_side, wide = refs[4:]
        j = pl.program_id(0)

        @pl.when(j == 0)
        def _():
            for k in range(8):
                at = slice(k * 256, (k + 1) * 256)
                normed_rows[:, at] = normed_ref[at, :].T
                cot_rows[:, at] = cot_ref[at, :].T

        def tile_step(t, begin):
            pre = jnp.dot(normed_rows[...], w_ref[:, : 2 * t], preferred_element_type=F32)
            d_hidden = jnp.dot(
                cot_rows[...], w_ref[:, 2 * t : 3 * t], preferred_element_type=F32
            )
            gate, up = pre[:, :t], pre[:, t:]
            gate_sig = jax.nn.sigmoid(gate)
            gate_act = gate * gate_sig
            hidden = (gate_act * up).astype(BF)
            d_gate = (d_hidden * up * gate_sig * (1.0 + gate * (1.0 - gate_sig))).astype(BF)
            d_up = (d_hidden * gate_act).astype(BF)
            d_pair = jnp.concatenate([d_gate, d_up], axis=1)
            grad_ref[:, : 2 * t] = jnp.dot(
                normed_ref[...], d_pair, preferred_element_type=F32
            ).astype(BF)
            grad_ref[:, 2 * t : 3 * t] = jnp.dot(
                cot_ref[...], hidden, preferred_element_type=F32
            ).astype(BF)
            pair_at, down_at = pl.ds(2 * begin, 2 * t), pl.ds(begin, t)
            pair_side[:, pair_at] = d_pair
            hidden_side[:, down_at] = hidden
            pair_weights[:, pair_at] = w_ref[:, : 2 * t]
            down_weights[:, down_at] = w_ref[:, 2 * t : 3 * t]

        last = tiles[-1]

        @pl.when(j < len(tiles) - 1)
        def _():
            tile_step(TILE, pl.multiple_of(j * TILE, TILE))

        @pl.when(j == len(tiles) - 1)
        def _():
            tile_step(last[2], last[1])
            dims = (((1,), (1,)), ((), ()))
            for out_refs, left, right in (
                (d_norm_refs, pair_weights, pair_side),
                (ffn_refs, down_weights, hidden_side),
            ):
                wide[...] = lax.dot_general(
                    left[...], right[...], dims, preferred_element_type=F32
                ).reshape(64, 32, toks)
                turn_back(pos_ref, wide, *out_refs, whole_place)

    whole = pl.BlockSpec((2048, toks), lambda j: (0, 0))
    tile = pl.BlockSpec((2048, 3 * TILE), lambda j: (0, j))
    rows = pl.BlockSpec((toks // 2, 2048), lambda j: (0, 0))
    outs = call(
        kernel,
        "feed_forward",
        [SMEM_SPEC, whole, whole, tile],
        [tile] + [rows] * 4,
        [jax.ShapeDtypeStruct((2048, width), BF)]
        + [jax.ShapeDtypeStruct((toks // 2, 2048), BF)] * 4,
        [
            pltpu.VMEM((toks, 2048), BF),
            pltpu.VMEM((toks, 2048), BF),
            pltpu.VMEM((2048, 2 * hidden_units), BF),
            pltpu.VMEM((2048, hidden_units), BF),
            pltpu.VMEM((toks, 2 * hidden_units), BF),
            pltpu.VMEM((toks, hidden_units), BF),
            pltpu.VMEM((64, 32, toks), F32),
        ],
        limit=60,
        grid=(len(tiles),),
    )(pos, normed2, cot, weights)
    return outs[0], outs[1:3], outs[3:5]


SEND_ORDER = (1, 5, 3, 7, 2, 6, 0, 4)


def weight_chunks(terms):
    widths = [r.shape[0] if f else r.shape[1] for l, r, f in terms]
    total = sum(widths)
    operands = [l for l, r, f in terms] + [r for l, r, f in terms]
    count = len(operands)

    def kernel(*refs):
        ins, outs = refs[:count], refs[count : count + 8]
        slots, sem = refs[-2:]
        copies = []
        for step, chunk in enumerate(SEND_ORDER):
            slot = step % 2
            if step >= 2:
                copies[step - 2].wait()
            begin = 0
            for i, (left, right, flipped) in enumerate(terms):
                dims = (((1,), (1 if flipped else 0,)), ((), ()))
                product = lax.dot_general(
                    ins[i][chunk], ins[len(terms) + i][...], dims, preferred_element_type=F32
                )
                slots[slot, :, begin : begin + widths[i]] = product.astype(BF)
                begin += widths[i]
            copies.append(pltpu.make_async_copy(slots.at[slot], outs[chunk], sem.at[slot]))
            copies[step].start()
        copies[-2].wait()
        copies[-1].wait()

    return call(
        kernel,
        "weight_chunks",
        [VMEM_SPEC] * count,
        [ANY_SPEC] * 8,
        [jax.ShapeDtypeStruct((256, total), BF)] * 8,
        [pltpu.VMEM((2, 256, total), BF), pltpu.SemaphoreType.DMA((2,))],
    )(*operands)


def summed(parts):
    total = parts[0].astype(F32)
    for part in parts[1:]:
        total = total + part.astype(F32)
    return total


def scatter_first(chunks):
    first = []
    for h, axis in ((0, "y"), (1, "z")):
        first += [chunks[4 * h]] + [hand(chunks[4 * h + d], axis, d) for d in (1, 2, 3)]
    return first


def scatter_second(first, beside):
    second = []
    for terms, axis in ((first[:4], "z"), (first[4:], "y")):
        parts = [summed([t[d * 64 : (d + 1) * 64] for t in terms]).astype(BF) for d in range(4)]
        second.append([parts[0]] + [hand(parts[d], axis, d) for d in (1, 2, 3)])
    shares = [summed(terms) for terms in second]
    give = jnp.concatenate([share[32:].astype(BF) for share in shares], axis=0)
    give, beside = tie(give, beside)
    got = fetch(give, "x", 1).astype(F32)
    return shares[0][:32] + got[:32], shares[1][:32] + got[32:], beside


def prepared(pos, q, out_t, kv, gate, up, down_t, gains):
    rows = q.shape[0]
    hidden = gate.shape[1] // 2
    attn_width = (q.shape[1] + out_t.shape[1] + kv.shape[1]) // 2 + 128

    def kernel(pos_ref, q_ref, out_t_ref, kv_ref, gate_ref, up_ref, down_ref, *refs):
        gain_refs, (attn_mine, attn_give, ffn_mine, ffn_give) = refs[:2], refs[2:]
        first = pos_ref[CORE] == 0

        def put(mine_ref, give_ref, to, source, at, width):
            half = source.shape[1] // 2
            one, two = source[:, at : at + width], source[:, half + at : half + at + width]
            mine_ref[:, to : to + width] = jnp.where(first, one, two)
            give_ref[:, to : to + width] = jnp.where(first, two, one)

        begin = 0
        for ref in (q_ref, out_t_ref, kv_ref):
            width = ref.shape[1] // 2
            put(attn_mine, attn_give, begin, ref, 0, width)
            begin += width
        same = lax.broadcasted_iota(jnp.int32, (rows, rows), 0) == lax.broadcasted_iota(
            jnp.int32, (rows, rows), 1
        )
        lane = lax.broadcasted_iota(jnp.int32, (rows, 128), 1)
        block = jnp.zeros((rows, 128), F32)
        for i, ref in enumerate(gain_refs):
            column = jnp.sum(jnp.where(same, ref[...].astype(F32), 0.0), axis=1, keepdims=True)
            block = jnp.where(lane == i, column, block)
        attn_mine[:, begin:] = block.astype(BF)
        attn_give[:, begin:] = block.astype(BF)
        for begin, unit, width in tile_columns(hidden):
            for i, ref in enumerate((gate_ref, up_ref, down_ref)):
                put(ffn_mine, ffn_give, begin + i * width, ref, unit, width)

    return call(
        kernel,
        "prepared",
        [SMEM_SPEC] + [VMEM_SPEC] * 8,
        [VMEM_SPEC] * 4,
        [jax.ShapeDtypeStruct((rows, attn_width), BF)] * 2
        + [jax.ShapeDtypeStruct((rows, 3 * hidden), BF)] * 2,
        limit=60,
    )(pos, q, out_t, kv, gate, up, down_t, *[g.reshape(1, -1) for g in gains])


def unpacked(pos, mine, other, layout):
    rows = mine.shape[0]
    halves = [sum(w for b, w in pieces) for pieces in layout]

    def kernel(pos_ref, mine_ref, other_ref, *outs):
        first = pos_ref[CORE] == 0
        for out, half, pieces in zip(outs, halves, layout):
            to = 0
            for begin, width in pieces:
                one, two = mine_ref[:, begin : begin + width], other_ref[:, begin : begin + width]
                out[:, to : to + width] = jnp.where(first, one, two)
                out[:, half + to : half + to + width] = jnp.where(first, two, one)
                to += width

    return call(
        kernel,
        "unpacked",
        [SMEM_SPEC] + [VMEM_SPEC] * 2,
        [VMEM_SPEC] * len(layout),
        [jax.ShapeDtypeStruct((rows, 2 * half), F32) for half in halves],
    )(pos, mine, other)


def arranged(pos, mine, other):
    count, head_dim = mine.shape
    block = 1024

    def kernel(pos_ref, mine_ref, other_ref, k_ref, v_ref, kt_ref, vt_ref):
        first = pos_ref[CORE] == 0
        one, two = mine_ref[...], other_ref[...]
        keys, values = jnp.where(first, one, two), jnp.where(first, two, one)
        k_ref[...] = keys
        v_ref[...] = values
        kt_ref[...] = keys.T
        vt_ref[...] = values.T

    rows = pl.BlockSpec((block, head_dim), lambda i: (i, 0))
    columns = pl.BlockSpec((head_dim, block), lambda i: (0, i))
    natural = jax.ShapeDtypeStruct((count, head_dim), BF)
    across = jax.ShapeDtypeStruct((head_dim, count), BF)
    return call(
        kernel,
        "arranged",
        [SMEM_SPEC, rows, rows],
        [rows, rows, columns, columns],
        [natural, natural, across, across],
        grid=(count // block,),
    )(pos, mine, other)


def key_gradients(pos, act, d_keyval, tokens, d_own, d_other, ffn_gain):
    toks, width = d_keyval.shape

    def kernel(pos_ref, act_ref, side_ref, tokens_ref, own_ref, other_ref, ffn_ref, out_ref, wide):
        for k in range(8):
            product = jnp.dot(act_ref[k], side_ref[...], preferred_element_type=F32)
            wide[k] = product.reshape(8, 32, width)
        rows = tokens_ref[...].astype(F32)
        inverse = lax.rsqrt(jnp.mean(rows * rows, axis=-1, keepdims=True) + norm_eps)
        d_normed = own_ref[...].astype(F32) + other_ref[...].astype(F32)
        attn_gain = jnp.sum(d_normed * rows * inverse, axis=0, keepdims=True)
        gains = jnp.concatenate(
            [attn_gain, 0.5 * ffn_ref[...], jnp.zeros((126, rows.shape[1]), F32)], axis=0
        )
        for block in range(16):
            groups = [wide[group_place(pos_ref, block * 4 + k)] for k in range(4)]
            at = slice(block * 128, (block + 1) * 128)
            out_ref[at, :width] = jnp.concatenate(groups, axis=0).astype(BF)
            out_ref[at, width:] = gains[:, at].T.astype(BF)

    return call(
        kernel,
        "key_gradients",
        [SMEM_SPEC] + [VMEM_SPEC] * 6,
        VMEM_SPEC,
        jax.ShapeDtypeStruct((2048, width + 128), BF),
        [pltpu.VMEM((8, 8, 32, width), F32)],
    )(pos, act, d_keyval, tokens, d_own, d_other, ffn_gain)


def allowed_keys(begin, count, places, starts):
    shape = (count, places.shape[1])
    key_place = begin + lax.broadcasted_iota(jnp.int32, shape, 0)
    return (key_place <= places) & (key_place >= starts)


def row_places(pos_ref, docs_ref, own, rows, key_block=KEY_BLOCK):
    half = rows // 2
    base = (pos_ref[Z] * 4 + pos_ref[Y]) * rows + jnp.where(own, pos_ref[CORE] * half, 0)
    lane = lax.broadcasted_iota(jnp.int32, (1, rows), 1)
    places = base + jnp.where(own, lax.rem(lane, half), lane)
    end = start = jnp.int32(0)
    starts = jnp.zeros((1, rows), jnp.int32)
    for j in range(docs_ref.shape[1]):
        length = docs_ref[pos_ref[X], j]
        end = end + length
        start = start + jnp.where(base >= end, length, 0)
        starts = starts + jnp.where(places >= end, length, 0)
    last = base + jnp.where(own, half, rows) - 1
    return places, starts, lax.div(start, key_block), lax.div(last, key_block) + 1


def attend_kernel(
    pos_ref, docs_ref, qt_ref, k_ref, vt_ref, ot_ref, lse_ref, *, first_set, scale, key_block
):
    units, head_dim, rows = qt_ref.shape
    own = pl.program_id(0) * units >= first_set
    places, starts, low, high = row_places(pos_ref, docs_ref, own, rows, key_block)

    def step(j, carry):
        begin = pl.multiple_of(j * key_block, key_block)
        keys = k_ref[pl.ds(begin, key_block), :]
        values = vt_ref[:, pl.ds(begin, key_block)]
        allowed = allowed_keys(begin, key_block, places, starts)
        out = []
        for u in range(units):
            top, mass, acc = carry[u]
            scores = jnp.dot(keys, qt_ref[u], preferred_element_type=F32)
            scores = jnp.where(allowed, scores, masked_fill)
            new_top = jnp.maximum(top, jnp.max(scores, axis=0, keepdims=True))
            weights = jnp.exp2((scores - new_top) * scale)
            shrink = jnp.exp2((top - new_top) * scale)
            mass = mass * shrink + jnp.sum(weights, axis=0, keepdims=True)
            acc = acc * shrink + jnp.dot(
                values, weights.astype(BF), preferred_element_type=F32
            )
            out.append((new_top, mass, acc))
        return tuple(out)

    start = (
        jnp.full((1, rows), masked_fill, F32),
        jnp.zeros((1, rows), F32),
        jnp.zeros((head_dim, rows), F32),
    )
    done = lax.fori_loop(low, high, step, (start,) * units)
    for u in range(units):
        top, mass, acc = done[u]
        ot_ref[u] = acc / mass
        lse_ref[u] = top * scale + jnp.log2(mass)


def attend(pos, docs, qt, keys, values_t, scale):
    units = 1
    blocks, head_dim, rows = qt.shape
    count = keys.shape[0]
    first_set = blocks // 2
    block = pl.BlockSpec((units, head_dim, rows), lambda i, p, d: (i, 0, 0))
    return pl.pallas_call(
        functools.partial(
            attend_kernel, first_set=first_set, scale=scale, key_block=2 * KEY_BLOCK
        ),
        grid_spec=pltpu.PrefetchScalarGridSpec(
            num_scalar_prefetch=2,
            grid=(blocks // units,),
            in_specs=[
                block,
                pl.BlockSpec((count, head_dim), lambda i, p, d: (0, 0)),
                pl.BlockSpec((head_dim, count), lambda i, p, d: (0, 0)),
            ],
            out_specs=[block, pl.BlockSpec((units, 1, rows), lambda i, p, d: (i, 0, 0))],
        ),
        out_shape=[
            jax.ShapeDtypeStruct((blocks, head_dim, rows), F32),
            jax.ShapeDtypeStruct((blocks, 1, rows), F32),
        ],
        compiler_params=pltpu.CompilerParams(vmem_limit_bytes=32 * MB),
        cost_estimate=SMALL,
        name="attend",
    )(pos, docs, qt, keys, values_t)


def attend_back_kernel(
    pos_ref, docs_ref, qt_ref, dot_ref, ot_ref, lse_ref, k_ref, kt_ref, v_ref,
    dqt_ref, mine_ref, give_ref, dk_ref, dv_ref, *, first_set, scale, score_scale,
):
    units, head_dim, rows = qt_ref.shape

    @pl.when(pl.program_id(0) == 0)
    def _():
        dk_ref[...] = jnp.zeros_like(dk_ref)
        dv_ref[...] = jnp.zeros_like(dv_ref)

    own = pl.program_id(0) * units >= first_set
    places, starts, low, high = row_places(pos_ref, docs_ref, own, rows)
    queries = [qt_ref[u].T for u in range(units)]
    d_outs = [dot_ref[u].T for u in range(units)]
    deltas = [
        jnp.sum(dot_ref[u].astype(F32) * ot_ref[u], axis=0, keepdims=True) for u in range(units)
    ]

    def step(j, carry):
        begin = pl.multiple_of(j * KEY_BLOCK, KEY_BLOCK)
        part = pl.ds(begin, KEY_BLOCK)
        allowed = allowed_keys(begin, KEY_BLOCK, places, starts)
        out = []
        d_keys = d_values = None
        for u in range(units):
            scores = jnp.dot(k_ref[part, :], qt_ref[u], preferred_element_type=F32)
            d_probs = jnp.dot(v_ref[part, :], dot_ref[u], preferred_element_type=F32)
            probs = jnp.where(allowed, jnp.exp2(scores * scale - lse_ref[u]), 0.0)
            d_scores = (probs * (d_probs - deltas[u])).astype(BF)
            for_keys = jnp.dot(d_scores, queries[u], preferred_element_type=F32)
            for_values = jnp.dot(probs.astype(BF), d_outs[u], preferred_element_type=F32)
            d_keys = for_keys if u == 0 else d_keys + for_keys
            d_values = for_values if u == 0 else d_values + for_values
            out.append(
                carry[u] + jnp.dot(kt_ref[:, part], d_scores, preferred_element_type=F32)
            )
        dk_ref[part, :] += d_keys
        dv_ref[part, :] += d_values
        return tuple(out)

    start = jnp.zeros((head_dim, rows), F32)
    done = lax.fori_loop(low, high, step, (start,) * units)
    for u in range(units):
        dqt_ref[u] = done[u] * score_scale

    @pl.when(pl.program_id(0) == pl.num_programs(0) - 1)
    def _():
        first = pos_ref[CORE] == 0
        d_keys, d_values = dk_ref[...] * score_scale, dv_ref[...]
        mine_ref[...] = jnp.where(first, d_keys, d_values)
        give_ref[...] = jnp.where(first, d_values, d_keys).astype(BF)


def attend_back(pos, docs, qt, d_out_t, out_t, lse, keys, keys_t, values, scale, score_scale):
    units = 2
    blocks, head_dim, rows = qt.shape
    count = keys.shape[0]
    first_set = blocks // 2
    block = pl.BlockSpec((units, head_dim, rows), lambda i, p, d: (i, 0, 0))
    whole = pl.BlockSpec((count, head_dim), lambda i, p, d: (0, 0))
    return pl.pallas_call(
        functools.partial(
            attend_back_kernel, first_set=first_set, scale=scale, score_scale=score_scale
        ),
        grid_spec=pltpu.PrefetchScalarGridSpec(
            num_scalar_prefetch=2,
            grid=(blocks // units,),
            in_specs=[
                block,
                block,
                block,
                pl.BlockSpec((units, 1, rows), lambda i, p, d: (i, 0, 0)),
                whole,
                pl.BlockSpec((head_dim, count), lambda i, p, d: (0, 0)),
                whole,
            ],
            out_specs=[block, whole, whole],
            scratch_shapes=[pltpu.VMEM((count, head_dim), F32)] * 2,
        ),
        out_shape=[
            jax.ShapeDtypeStruct((blocks, head_dim, rows), F32),
            jax.ShapeDtypeStruct((count, head_dim), F32),
            jax.ShapeDtypeStruct((count, head_dim), BF),
        ],
        compiler_params=pltpu.CompilerParams(vmem_limit_bytes=44 * MB),
        cost_estimate=SMALL,
        name="attend_back",
    )(pos, docs, qt, d_out_t, out_t, lse, keys, keys_t, values)


def doc_starts(lengths, places):
    ends = jnp.cumsum(lengths)
    passed = (places[:, None] >= ends[None, :]).astype(jnp.int32)
    return jnp.sum(passed * lengths[None, :], axis=1)


def rotate_rows(values, cosine, sine):
    half = values.shape[-1] // 2
    one, two = values[..., :half], values[..., half:]
    return jnp.concatenate([one * cosine - two * sine, two * cosine + one * sine], axis=-1)


def rotate_columns(values, cosine, sine):
    half = values.shape[1] // 2
    one, two = values[:, :half], values[:, half:]
    return jnp.concatenate([one * cosine - two * sine, two * cosine + one * sine], axis=1)


def head_blocks(array):
    toks, width = array.shape
    count = width // 256

    def kernel(array_ref, out_ref):
        for b in range(count):
            for i in range(2):
                at = (2 * b + i) * 128
                out_ref[b, :, i * toks : (i + 1) * toks] = array_ref[:, at : at + 128].T

    shape = jax.ShapeDtypeStruct((count, 128, 2 * toks), array.dtype)
    return call(kernel, "head_blocks", [VMEM_SPEC], VMEM_SPEC, shape)(array)


def head_blocks_back(blocks, begin):
    total, head_dim, wide = blocks.shape
    count, toks = total - begin, wide // 2

    def kernel(blocks_ref, out_ref):
        for b in range(count):
            for i in range(2):
                at = (2 * b + i) * 128
                out_ref[:, at : at + 128] = blocks_ref[b, :, i * toks : (i + 1) * toks].T

    shape = jax.ShapeDtypeStruct((toks, count * 256), blocks.dtype)
    spec = pl.BlockSpec((count, head_dim, wide), lambda i: (begin // count, 0, 0))
    return call(kernel, "head_blocks_back", [spec], VMEM_SPEC, shape)(blocks)


def on_device(
    tokens, doc_lengths, attn_gain, q_weight, kv_weight, out_weight, ffn_gain,
    gate_weight, up_weight, down_weight, second_queries, out_cotangent, second_cotangent,
):
    x, z, y, c = (lax.axis_index(a) for a in ("x", "z", "y", "c"))
    first = c == 0
    pos = jnp.stack([x, z, y, c]).astype(jnp.int32)
    toks, width = tokens.shape
    head_dim = kv_weight.shape[1] // 2
    score_scale = head_dim ** (-0.5)
    scale = score_scale * math.log2(math.e)
    rows = q_weight.shape[0]

    def swap(own):
        return fetch(own, "c", 1)

    n_q, n_kv = q_weight.shape[1] // 2, head_dim
    n_out, n_ffn = out_weight.shape[0] // 2, down_weight.shape[0] // 2
    n_attn = n_q + n_out
    at_out, at_kv = n_q // n_out, n_attn // n_kv
    attn_mine, attn_give, ffn_mine, ffn_give = prepared(
        pos, q_weight, out_weight.T, kv_weight, gate_weight, up_weight, down_weight.T,
        (attn_gain, ffn_gain),
    )
    attn_other, ffn_other, tokens_other, cot_other = tie(
        swap(attn_give), swap(ffn_give), swap(tokens), swap(out_cotangent)
    )
    attn_rows = across_x(attn_mine, attn_other)
    ffn_both = jnp.concatenate([ffn_mine, ffn_other], axis=0)
    blocks = first_blocks(attn_rows)
    ffn_got, *blocks = tie(fetch(ffn_both, "x", 1), *blocks[0], *blocks[1])
    ffn_rows = jnp.concatenate([ffn_both, ffn_got], axis=0)
    ffn_whole = lax.all_gather(ffn_rows, ("z", "y"), axis=0, tiled=True)
    attn_pair = second_pair([jnp.concatenate(b, axis=0) for b in (blocks[:4], blocks[4:])])
    attn_chunks = far_blocks(attn_pair, tie(*near_blocks(attn_pair)))
    attn_chunks = [jnp.concatenate(w, axis=0) if isinstance(w, tuple) else w for w in attn_chunks]
    def over_tp(rows):
        send = rows.astype(BF)
        return send.astype(F32) + fetch(send, "t", 1).astype(F32)

    def reduce_rows(own, other):
        return over_tp(own.astype(F32) + swap(other).astype(F32))

    places = (z * 4 + y) * (2 * toks) + jnp.arange(2 * toks, dtype=jnp.int32)
    starts = doc_starts(jnp.where(x == 0, doc_lengths[0], doc_lengths[1]), places)
    positions = (places - starts).astype(F32)
    inverse_freq = jnp.exp(
        jnp.arange(head_dim // 2, dtype=F32) * (-2.0 * math.log(rope_base) / head_dim)
    )
    angles_t = inverse_freq[:, None] * positions[None, :]
    cos_t, sin_t = jnp.cos(angles_t), jnp.sin(angles_t)

    inputs = tokens.astype(F32)
    inv_attn = lax.rsqrt(jnp.mean(inputs * inputs, axis=-1, keepdims=True) + norm_eps)
    second_t, second_cot_t = head_blocks(second_queries), head_blocks(second_cotangent)
    cot_t = turned(pos, out_cotangent, cot_other, whole=True)
    cos_r, sin_r = cos_t.T, sin_t.T
    normed_t, gain_rows, keyval = normed_rows(pos, tokens, tokens_other, attn_chunks, n_kv, at_kv)
    gain_one, gain_two = gain_rows[0:1], gain_rows[1:2]
    kv_own = jnp.where(first, rotate_rows(keyval, cos_r, sin_r), keyval).astype(BF)
    kv_sent = jnp.broadcast_to(kv_own[None], (16,) + kv_own.shape)
    kv_all = lax.all_to_all(kv_sent, ("z", "y"), 0, 0).reshape(-1, head_dim)
    queries_t = project(normed_t, attn_chunks, n_q, 0, F32)
    query_rot = rotate_columns(queries_t.reshape(-1, head_dim, 2 * toks), cos_t, sin_t).astype(BF)
    keys, values, keys_t, values_t = arranged(pos, kv_all, swap(kv_all))
    query_t = jnp.concatenate([query_rot, second_t], axis=0)
    out_t, lse = attend(pos, doc_lengths, query_t, keys, values_t, scale)
    n_first = query_rot.shape[0]
    second_out = head_blocks_back(out_t, n_first)
    attended_t = out_t[:n_first].reshape(-1, 2 * toks).astype(BF)

    branch = reduce_rows(*unproject(pos, [(attn_chunks, at_out, attended_t, False)]))
    resid = inputs + branch
    inv_ffn = lax.rsqrt(jnp.mean(resid * resid, axis=-1, keepdims=True) + norm_eps)
    normed2 = (resid * inv_ffn * gain_two).astype(BF)
    normed2_t = turned(pos, normed2, swap(normed2), whole=True)
    ffn_grads, d_norm2_part, ffn_part = feed_forward(pos, normed2_t, cot_t, ffn_whole)
    ffn_share = lax.psum_scatter(ffn_grads, ("z", "y"), scatter_dimension=0, tiled=True)
    d_normed2 = reduce_rows(*d_norm2_part)

    scaled_two = gain_two * d_normed2
    ffn_gain_part = jnp.sum(d_normed2 * resid * inv_ffn, axis=0)
    d_resid = (
        out_cotangent.astype(F32)
        + inv_ffn * scaled_two
        - resid * inv_ffn**3 * jnp.mean(scaled_two * resid, axis=-1, keepdims=True)
    )
    d_branch = d_resid.astype(BF)

    d_branch_t = turned(pos, d_branch, swap(d_branch))
    d_attended_t = project(d_branch_t, attn_chunks, n_out, at_out, BF)
    d_out_t = jnp.concatenate(
        [d_attended_t.reshape(-1, head_dim, 2 * toks), second_cot_t], axis=0
    )
    d_query_t, kv_mine, kv_give = attend_back(
        pos, doc_lengths, query_t, d_out_t, out_t, lse, keys, keys_t, values, scale, score_scale
    )
    kv_give, d_query_t, *ffn_part = tie(kv_give, d_query_t, *ffn_part)
    ffn_sum = reduce_rows(*ffn_part)
    kv_other = swap(kv_give)
    second_queries_grad = head_blocks_back(d_query_t, n_first)
    d_queries_t = rotate_columns(d_query_t[:n_first], cos_t, -sin_t).reshape(-1, 2 * toks).astype(BF)

    attn_grads = weight_chunks([(normed_t, d_queries_t, True), (d_branch_t, attended_t, True)])
    kv_chip = (kv_mine + kv_other.astype(F32)).astype(BF).reshape(16, 2 * toks, head_dim)
    kv_chip, *attn_grads = tie(kv_chip, *attn_grads)
    kv_parts = lax.all_to_all(kv_chip, ("z", "y"), 0, 0)
    attn_terms = scatter_first(attn_grads)
    near = (1, 3, 5, 7)
    kv_parts, ffn_sum, *got = tie(kv_parts, ffn_sum, *[attn_terms[i] for i in near])
    for i, term in zip(near, got):
        attn_terms[i] = term
    kv_sum = jnp.sum(kv_parts.astype(F32), axis=0)
    result = resid + ffn_sum
    d_keyval = jnp.where(first, rotate_rows(kv_sum, cos_r, -sin_r), kv_sum).astype(BF)
    d_norm_part = unproject(
        pos, [(attn_chunks, 0, d_queries_t, False), (attn_chunks, at_kv, d_keyval, True)]
    )
    d_norm_other = swap(d_norm_part[1])
    d_normed = over_tp(d_norm_part[0].astype(F32) + d_norm_other.astype(F32))
    kv_grads = key_gradients(
        pos, normed_t, d_keyval, tokens, d_norm_part[0], d_norm_other, ffn_gain_part[None]
    )
    kv_got = lax.all_to_all(kv_grads.reshape(32, 2, rows, -1), ("x", "z", "y"), 0, 0)
    kv_got, *attn_terms = tie(kv_got, *attn_terms)
    ffn_got = fetch(ffn_share[64:], "x", 1)
    attn_share, attn_give, ffn_got = scatter_second(attn_terms, ffn_got)
    ffn_sums = ffn_share[:64].astype(F32) + ffn_got.astype(F32)
    kv_share = jnp.sum(kv_got.astype(F32), axis=0)
    scaled_one = gain_one * d_normed
    tokens_grad = (
        d_resid
        + inv_attn * scaled_one
        - inputs * inv_attn**3 * jnp.mean(scaled_one * inputs, axis=-1, keepdims=True)
    )

    gate_grad, up_grad, down_grad_t = unpacked(
        pos,
        ffn_sums[:32],
        swap(ffn_sums[32:]),
        [[(b + i * w, w) for b, unit, w in tile_columns(n_ffn)] for i in range(3)],
    )
    q_grad, out_grad_t = unpacked(pos, attn_share, swap(attn_give), [[(0, n_q)], [(n_q, n_out)]])
    kv_mine, kv_give = (jnp.where(first, kv_share[i], kv_share[1 - i]) for i in (0, 1))
    kv_other = swap(kv_give)
    kv_gain = jnp.concatenate(
        [
            in_order(first, kv_mine[:, :n_kv], kv_other[:, :n_kv], 1),
            kv_mine[:, n_kv:] + kv_other[:, n_kv:],
        ],
        axis=1,
    )
    kv_gain = kv_gain + fetch(kv_gain, "t", 1)
    return (
        result,
        second_out,
        tokens_grad,
        kv_gain[:, 2 * n_kv],
        q_grad,
        kv_gain[:, : 2 * n_kv],
        out_grad_t.T,
        kv_gain[:, 2 * n_kv + 1],
        gate_grad,
        up_grad,
        down_grad_t.T,
        second_queries_grad,
    )


def solution(mesh):
    fine = Mesh(mesh.devices.reshape(2, 4, 4, 2, 2), ("x", "z", "y", "c", "t"))
    seq = ("x", "z", "y", "c")
    rows, both, turned_both = P(seq, None), P(seq, "t"), P("t", seq)
    in_specs = (
        rows, P(), P(seq), both, rows, turned_both, P(seq), both, both, turned_both, both, rows, both,
    )
    out_specs = (
        rows, both, rows, P(seq), both, rows, turned_both, P(seq), both, both, turned_both, both,
    )
    return jax.shard_map(
        on_device, mesh=fine, in_specs=in_specs, out_specs=out_specs, check_vma=False
    )
```

```python
import functools
import math

import jax
import jax.numpy as jnp
from jax import lax
from jax.experimental import pallas as pl
from jax.experimental.pallas import tpu as pltpu
from jax.sharding import Mesh, PartitionSpec as P

norm_eps = 1e-05
rope_base = 10000.0
masked_fill = -1e30
KEY_BLOCK = 1024
BF = jnp.bfloat16
F32 = jnp.float32
MB = 1024 * 1024


def fetch(block, axis, offset):
    n = lax.axis_size(axis)
    return lax.ppermute(block, axis, [((i + offset) % n, i) for i in range(n)])


def hand(block, axis, offset):
    return fetch(block, axis, -offset)


def in_order(first, mine, other, axis):
    return jnp.where(
        first,
        jnp.concatenate([mine, other], axis=axis),
        jnp.concatenate([other, mine], axis=axis),
    )


X, Z, Y, CORE = 0, 1, 2, 3


def near_blocks(pair):
    return [fetch(block, axis, d) for block, axis in pair for d in (1, 3)]


def far_blocks(pair, near):
    out = []
    for i, (block, axis) in enumerate(pair):
        after, before = near[2 * i : 2 * i + 2]
        half = block.shape[0] // 2
        far = (fetch(after[:half], axis, 1), fetch(before[half:], axis, 3))
        out.append([block, after, far, before])
    return out[0] + out[1]


def across_x(mine, other):
    rows = mine.shape[0]
    got = fetch(jnp.concatenate([mine, other], axis=0), "x", 1)
    return [
        jnp.concatenate([mine, got[:rows]], axis=0),
        jnp.concatenate([other, got[rows:]], axis=0),
    ]


def first_blocks(pieces):
    return [
        [piece] + [fetch(piece, axis, d) for d in (1, 2, 3)] for piece, axis in zip(pieces, ("z", "y"))
    ]


def second_pair(halves):
    return [(halves[0], "y"), (halves[1], "z")]


def place_in_chunks(pos_ref, x, z, y, dh):
    dx = lax.rem(x - pos_ref[X] + 2, 2)
    dz = lax.rem(z - pos_ref[Z] + 4, 4)
    dy = lax.rem(y - pos_ref[Y] + 4, 4)
    own = dh == 0
    return dh * 4 + jnp.where(own, dy, dz), jnp.where(own, dz, dy) * 2 + dx


def group_place(pos_ref, group):
    h, y, z, x = group % 2, group // 2 % 4, group // 8 % 4, group // 32
    return place_in_chunks(pos_ref, x, z, y, lax.rem(h + pos_ref[CORE], 2))


def whole_place(pos_ref, group):
    h, y, z, x = group % 2, group // 2 % 4, group // 8 % 4, group // 32
    dx = lax.rem(x - pos_ref[X] + 2, 2)
    return (z * 4 + y) * 4 + dx * 2 + lax.rem(h + pos_ref[CORE], 2)


SMEM_SPEC = pl.BlockSpec(memory_space=pltpu.SMEM)
VMEM_SPEC = pl.BlockSpec(memory_space=pltpu.VMEM)
ANY_SPEC = pl.BlockSpec(memory_space=pl.ANY)
SMALL = pl.CostEstimate(flops=1024, bytes_accessed=1024, transcendentals=0)


def call(kernel, name, in_specs, out_specs, out_shape, scratch=(), limit=24, grid=None, **more):
    return pl.pallas_call(
        kernel,
        grid=grid or (1,),
        in_specs=in_specs,
        out_specs=out_specs,
        out_shape=out_shape,
        scratch_shapes=scratch,
        compiler_params=pltpu.CompilerParams(vmem_limit_bytes=limit * MB),
        cost_estimate=SMALL,
        name=name,
        **more,
    )


def tie(*arrays):
    return list(lax.optimization_barrier(arrays))


def both_cores(pos_ref, own, other):
    first = pos_ref[CORE] == 0
    return jnp.concatenate(
        [jnp.where(first, own, other), jnp.where(first, other, own)], axis=0
    )


def turn(pos_ref, act_ref, out_ref, place=group_place):
    for block in range(16):
        part = act_ref[:, block * 128 : (block + 1) * 128].T
        for k in range(4):
            out_ref[place(pos_ref, block * 4 + k)] = part[k * 32 : (k + 1) * 32]


def turned(pos, own, other, whole=False):
    toks, feats = own.shape
    shape = (64, 32, 2 * toks) if whole else (8, 8, 32, 2 * toks)

    def kernel(pos_ref, own_ref, other_ref, out_ref, act):
        act[...] = both_cores(pos_ref, own_ref[...], other_ref[...])
        turn(pos_ref, act, out_ref, whole_place if whole else group_place)

    out = call(
        kernel,
        "turned",
        [SMEM_SPEC, VMEM_SPEC, VMEM_SPEC],
        VMEM_SPEC,
        jax.ShapeDtypeStruct(shape, own.dtype),
        [pltpu.VMEM((2 * toks, feats), own.dtype)],
    )(pos, own, other)
    return out.reshape((2048, 2 * toks) if whole else (8, 256, 2 * toks))


def normed_rows(pos, own, other, chunks, width, at):
    toks, feats = own.shape

    def kernel(pos_ref, own_ref, other_ref, *refs):
        sides, gains, (out_ref, gain_ref, side_ref, wide, act) = refs[:8], refs[8:16], refs[16:]
        for k in range(8):
            wide[k] = gains[k][...].astype(F32).reshape(8, 32, 128)
        for block in range(feats // 128):
            groups = [wide[group_place(pos_ref, block * 4 + k)] for k in range(4)]
            gain_ref[:, block * 128 : (block + 1) * 128] = jnp.concatenate(groups, axis=0).T[:8]
        rows = both_cores(pos_ref, own_ref[...], other_ref[...]).astype(F32)
        inverse = lax.rsqrt(jnp.mean(rows * rows, axis=-1, keepdims=True) + norm_eps)
        act[...] = (rows * inverse * gain_ref[0:1, :]).astype(BF)
        turn(pos_ref, act, out_ref)
        total = jnp.zeros((2 * toks, width), F32)
        for k in range(8):
            turned_rows = out_ref[k].reshape(256, 2 * toks)
            total = total + jnp.dot(turned_rows.T, sides[k][...], preferred_element_type=F32)
        side_ref[...] = total

    specs = [pl.BlockSpec((256, w), lambda i, b=b: (0, b)) for w, b in ((width, at), (128, at + 1))]
    out, gains, side = call(
        kernel,
        "normed_rows",
        [SMEM_SPEC] + [VMEM_SPEC] * 2 + [specs[0]] * 8 + [specs[1]] * 8,
        [VMEM_SPEC] * 3,
        [
            jax.ShapeDtypeStruct((8, 8, 32, 2 * toks), BF),
            jax.ShapeDtypeStruct((8, feats), F32),
            jax.ShapeDtypeStruct((2 * toks, width), F32),
        ],
        [pltpu.VMEM((8, 8, 32, 128), F32), pltpu.VMEM((2 * toks, feats), BF)],
    )(pos, own, other, *chunks, *chunks)
    return out.reshape(8, 256, 2 * toks), gains, side


def turn_back(pos_ref, wide_ref, own_ref, other_ref, place=group_place):
    first = pos_ref[CORE] == 0
    half = wide_ref.shape[-1] // 2
    for block in range(16):
        groups = [wide_ref[place(pos_ref, block * 4 + k)] for k in range(4)]
        rows = jnp.concatenate(groups, axis=0).T.astype(own_ref.dtype)
        at = slice(block * 128, (block + 1) * 128)
        own_ref[:, at] = jnp.where(first, rows[:half], rows[half:])
        other_ref[:, at] = jnp.where(first, rows[half:], rows[:half])


def project(act, chunks, width, at, kind):
    toks = act.shape[-1]

    def kernel(act_ref, *refs):
        weights, out = refs[:8], refs[8]
        total = jnp.zeros((toks, width), F32)
        for k in range(8):
            total = total + jnp.dot(
                act_ref[k].T, weights[k][...], preferred_element_type=F32
            )
        out[...] = total.T.astype(kind)

    return call(
        kernel,
        "project",
        [VMEM_SPEC] + [pl.BlockSpec((256, width), lambda i: (0, at))] * 8,
        VMEM_SPEC,
        jax.ShapeDtypeStruct((width, toks), kind),
    )(act, *chunks)


def unproject(pos, sides):
    count = len(sides)
    toks = sides[0][2].shape[0 if sides[0][3] else 1]
    operands, specs, starts = [], [], []
    for chunks, at, side, flipped in sides:
        width = side.shape[1 if flipped else 0]
        starts.append(len(operands))
        if isinstance(chunks, list):
            operands += chunks
            specs += [pl.BlockSpec((256, width), lambda i, at=at: (0, at))] * 8
        else:
            operands.append(chunks)
            specs.append(VMEM_SPEC)

    def kernel(pos_ref, *refs):
        rights, weights = refs[:count], refs[count : count + len(operands)]
        own_ref, other_ref, wide = refs[count + len(operands) :]
        for k in range(8):
            total = None
            for i, (chunks, at, side, flipped) in enumerate(sides):
                begin = starts[i]
                left = weights[begin + k][...] if isinstance(chunks, list) else weights[begin][k]
                dims = (((1,), (1 if flipped else 0,)), ((), ()))
                part = lax.dot_general(left, rights[i][...], dims, preferred_element_type=F32)
                total = part if total is None else total + part
            wide[k] = total.reshape(8, 32, toks)
        turn_back(pos_ref, wide, own_ref, other_ref)

    return call(
        kernel,
        "unproject",
        [SMEM_SPEC] + [VMEM_SPEC] * count + specs,
        [VMEM_SPEC] * 2,
        [jax.ShapeDtypeStruct((toks // 2, 2048), BF)] * 2,
        [pltpu.VMEM((8, 8, 32, toks), F32)],
    )(pos, *[side[2] for side in sides], *operands)


TILE = 128


def tile_columns(hidden):
    return [(3 * at, at, min(TILE, hidden - at)) for at in range(0, hidden, TILE)]


def feed_forward(pos, normed2, cot, weights):
    toks = normed2.shape[1]
    width = weights.shape[1]
    hidden_units = width // 3
    tiles = tile_columns(hidden_units)

    def kernel(pos_ref, normed_ref, cot_ref, w_ref, grad_ref, *refs):
        d_norm_refs, ffn_refs = refs[:2], refs[2:4]
        normed_rows, cot_rows, pair_weights, down_weights, pair_side, hidden_side, wide = refs[4:]
        j = pl.program_id(0)

        @pl.when(j == 0)
        def _():
            for k in range(8):
                at = slice(k * 256, (k + 1) * 256)
                normed_rows[:, at] = normed_ref[at, :].T
                cot_rows[:, at] = cot_ref[at, :].T

        def tile_step(t, begin):
            pre = jnp.dot(normed_rows[...], w_ref[:, : 2 * t], preferred_element_type=F32)
            d_hidden = jnp.dot(
                cot_rows[...], w_ref[:, 2 * t : 3 * t], preferred_element_type=F32
            )
            gate, up = pre[:, :t], pre[:, t:]
            gate_sig = jax.nn.sigmoid(gate)
            gate_act = gate * gate_sig
            hidden = (gate_act * up).astype(BF)
            d_gate = (d_hidden * up * gate_sig * (1.0 + gate * (1.0 - gate_sig))).astype(BF)
            d_up = (d_hidden * gate_act).astype(BF)
            d_pair = jnp.concatenate([d_gate, d_up], axis=1)
            grad_ref[:, : 2 * t] = jnp.dot(
                normed_ref[...], d_pair, preferred_element_type=F32
            ).astype(BF)
            grad_ref[:, 2 * t : 3 * t] = jnp.dot(
                cot_ref[...], hidden, preferred_element_type=F32
            ).astype(BF)
            pair_at, down_at = pl.ds(2 * begin, 2 * t), pl.ds(begin, t)
            pair_side[:, pair_at] = d_pair
            hidden_side[:, down_at] = hidden
            pair_weights[:, pair_at] = w_ref[:, : 2 * t]
            down_weights[:, down_at] = w_ref[:, 2 * t : 3 * t]

        last = tiles[-1]

        @pl.when(j < len(tiles) - 1)
        def _():
            tile_step(TILE, pl.multiple_of(j * TILE, TILE))

        @pl.when(j == len(tiles) - 1)
        def _():
            tile_step(last[2], last[1])
            dims = (((1,), (1,)), ((), ()))
            for out_refs, left, right in (
                (d_norm_refs, pair_weights, pair_side),
                (ffn_refs, down_weights, hidden_side),
            ):
                wide[...] = lax.dot_general(
                    left[...], right[...], dims, preferred_element_type=F32
                ).reshape(64, 32, toks)
                turn_back(pos_ref, wide, *out_refs, whole_place)

    whole = pl.BlockSpec((2048, toks), lambda j: (0, 0))
    tile = pl.BlockSpec((2048, 3 * TILE), lambda j: (0, j))
    rows = pl.BlockSpec((toks // 2, 2048), lambda j: (0, 0))
    outs = call(
        kernel,
        "feed_forward",
        [SMEM_SPEC, whole, whole, tile],
        [tile] + [rows] * 4,
        [jax.ShapeDtypeStruct((2048, width), BF)]
        + [jax.ShapeDtypeStruct((toks // 2, 2048), BF)] * 4,
        [
            pltpu.VMEM((toks, 2048), BF),
            pltpu.VMEM((toks, 2048), BF),
            pltpu.VMEM((2048, 2 * hidden_units), BF),
            pltpu.VMEM((2048, hidden_units), BF),
            pltpu.VMEM((toks, 2 * hidden_units), BF),
            pltpu.VMEM((toks, hidden_units), BF),
            pltpu.VMEM((64, 32, toks), F32),
        ],
        limit=60,
        grid=(len(tiles),),
    )(pos, normed2, cot, weights)
    return outs[0], outs[1:3], outs[3:5]


SEND_ORDER = (1, 5, 3, 7, 2, 6, 0, 4)


def weight_chunks(terms):
    widths = [r.shape[0] if f else r.shape[1] for l, r, f in terms]
    total = sum(widths)
    operands = [l for l, r, f in terms] + [r for l, r, f in terms]
    count = len(operands)

    def kernel(*refs):
        ins, outs = refs[:count], refs[count : count + 8]
        slots, sem = refs[-2:]
        copies = []
        for step, chunk in enumerate(SEND_ORDER):
            slot = step % 2
            if step >= 2:
                copies[step - 2].wait()
            begin = 0
            for i, (left, right, flipped) in enumerate(terms):
                dims = (((1,), (1 if flipped else 0,)), ((), ()))
                product = lax.dot_general(
                    ins[i][chunk], ins[len(terms) + i][...], dims, preferred_element_type=F32
                )
                slots[slot, :, begin : begin + widths[i]] = product.astype(BF)
                begin += widths[i]
            copies.append(pltpu.make_async_copy(slots.at[slot], outs[chunk], sem.at[slot]))
            copies[step].start()
        copies[-2].wait()
        copies[-1].wait()

    return call(
        kernel,
        "weight_chunks",
        [VMEM_SPEC] * count,
        [ANY_SPEC] * 8,
        [jax.ShapeDtypeStruct((256, total), BF)] * 8,
        [pltpu.VMEM((2, 256, total), BF), pltpu.SemaphoreType.DMA((2,))],
    )(*operands)


def summed(parts):
    total = parts[0].astype(F32)
    for part in parts[1:]:
        total = total + part.astype(F32)
    return total


def scatter_first(chunks):
    first = []
    for h, axis in ((0, "y"), (1, "z")):
        first += [chunks[4 * h]] + [hand(chunks[4 * h + d], axis, d) for d in (1, 2, 3)]
    return first


def scatter_second(first, beside):
    second = []
    for terms, axis in ((first[:4], "z"), (first[4:], "y")):
        parts = [summed([t[d * 64 : (d + 1) * 64] for t in terms]).astype(BF) for d in range(4)]
        second.append([parts[0]] + [hand(parts[d], axis, d) for d in (1, 2, 3)])
    shares = [summed(terms) for terms in second]
    give = jnp.concatenate([share[32:].astype(BF) for share in shares], axis=0)
    give, beside = tie(give, beside)
    got = fetch(give, "x", 1).astype(F32)
    return shares[0][:32] + got[:32], shares[1][:32] + got[32:], beside


def prepared(pos, q, out_t, kv, gate, up, down_t, gains):
    rows = q.shape[0]
    hidden = gate.shape[1] // 2
    attn_width = (q.shape[1] + out_t.shape[1] + kv.shape[1]) // 2 + 128

    def kernel(pos_ref, q_ref, out_t_ref, kv_ref, gate_ref, up_ref, down_ref, *refs):
        gain_refs, (attn_mine, attn_give, ffn_mine, ffn_give) = refs[:2], refs[2:]
        first = pos_ref[CORE] == 0

        def put(mine_ref, give_ref, to, source, at, width):
            half = source.shape[1] // 2
            one, two = source[:, at : at + width], source[:, half + at : half + at + width]
            mine_ref[:, to : to + width] = jnp.where(first, one, two)
            give_ref[:, to : to + width] = jnp.where(first, two, one)

        begin = 0
        for ref in (q_ref, out_t_ref, kv_ref):
            width = ref.shape[1] // 2
            put(attn_mine, attn_give, begin, ref, 0, width)
            begin += width
        same = lax.broadcasted_iota(jnp.int32, (rows, rows), 0) == lax.broadcasted_iota(
            jnp.int32, (rows, rows), 1
        )
        lane = lax.broadcasted_iota(jnp.int32, (rows, 128), 1)
        block = jnp.zeros((rows, 128), F32)
        for i, ref in enumerate(gain_refs):
            column = jnp.sum(jnp.where(same, ref[...].astype(F32), 0.0), axis=1, keepdims=True)
            block = jnp.where(lane == i, column, block)
        attn_mine[:, begin:] = block.astype(BF)
        attn_give[:, begin:] = block.astype(BF)
        for begin, unit, width in tile_columns(hidden):
            for i, ref in enumerate((gate_ref, up_ref, down_ref)):
                put(ffn_mine, ffn_give, begin + i * width, ref, unit, width)

    return call(
        kernel,
        "prepared",
        [SMEM_SPEC] + [VMEM_SPEC] * 8,
        [VMEM_SPEC] * 4,
        [jax.ShapeDtypeStruct((rows, attn_width), BF)] * 2
        + [jax.ShapeDtypeStruct((rows, 3 * hidden), BF)] * 2,
        limit=60,
    )(pos, q, out_t, kv, gate, up, down_t, *[g.reshape(1, -1) for g in gains])


def unpacked(pos, mine, other, layout):
    rows = mine.shape[0]
    halves = [sum(w for b, w in pieces) for pieces in layout]

    def kernel(pos_ref, mine_ref, other_ref, *outs):
        first = pos_ref[CORE] == 0
        for out, half, pieces in zip(outs, halves, layout):
            to = 0
            for begin, width in pieces:
                one, two = mine_ref[:, begin : begin + width], other_ref[:, begin : begin + width]
                out[:, to : to + width] = jnp.where(first, one, two)
                out[:, half + to : half + to + width] = jnp.where(first, two, one)
                to += width

    return call(
        kernel,
        "unpacked",
        [SMEM_SPEC] + [VMEM_SPEC] * 2,
        [VMEM_SPEC] * len(layout),
        [jax.ShapeDtypeStruct((rows, 2 * half), F32) for half in halves],
    )(pos, mine, other)


def arranged(pos, mine, other):
    count, head_dim = mine.shape
    block = 1024

    def kernel(pos_ref, mine_ref, other_ref, k_ref, v_ref, kt_ref, vt_ref):
        first = pos_ref[CORE] == 0
        one, two = mine_ref[...], other_ref[...]
        keys, values = jnp.where(first, one, two), jnp.where(first, two, one)
        k_ref[...] = keys
        v_ref[...] = values
        kt_ref[...] = keys.T
        vt_ref[...] = values.T

    rows = pl.BlockSpec((block, head_dim), lambda i: (i, 0))
    columns = pl.BlockSpec((head_dim, block), lambda i: (0, i))
    natural = jax.ShapeDtypeStruct((count, head_dim), BF)
    across = jax.ShapeDtypeStruct((head_dim, count), BF)
    return call(
        kernel,
        "arranged",
        [SMEM_SPEC, rows, rows],
        [rows, rows, columns, columns],
        [natural, natural, across, across],
        grid=(count // block,),
    )(pos, mine, other)


def key_gradients(pos, act, d_keyval, tokens, d_own, d_other, ffn_gain):
    toks, width = d_keyval.shape

    def kernel(pos_ref, act_ref, side_ref, tokens_ref, own_ref, other_ref, ffn_ref, out_ref, wide):
        for k in range(8):
            product = jnp.dot(act_ref[k], side_ref[...], preferred_element_type=F32)
            wide[k] = product.reshape(8, 32, width)
        rows = tokens_ref[...].astype(F32)
        inverse = lax.rsqrt(jnp.mean(rows * rows, axis=-1, keepdims=True) + norm_eps)
        d_normed = own_ref[...].astype(F32) + other_ref[...].astype(F32)
        attn_gain = jnp.sum(d_normed * rows * inverse, axis=0, keepdims=True)
        gains = jnp.concatenate(
            [attn_gain, 0.5 * ffn_ref[...], jnp.zeros((126, rows.shape[1]), F32)], axis=0
        )
        for block in range(16):
            groups = [wide[group_place(pos_ref, block * 4 + k)] for k in range(4)]
            at = slice(block * 128, (block + 1) * 128)
            out_ref[at, :width] = jnp.concatenate(groups, axis=0).astype(BF)
            out_ref[at, width:] = gains[:, at].T.astype(BF)

    return call(
        kernel,
        "key_gradients",
        [SMEM_SPEC] + [VMEM_SPEC] * 6,
        VMEM_SPEC,
        jax.ShapeDtypeStruct((2048, width + 128), BF),
        [pltpu.VMEM((8, 8, 32, width), F32)],
    )(pos, act, d_keyval, tokens, d_own, d_other, ffn_gain)


def allowed_keys(begin, count, places, starts):
    shape = (count, places.shape[1])
    key_place = begin + lax.broadcasted_iota(jnp.int32, shape, 0)
    return (key_place <= places) & (key_place >= starts)


def row_places(pos_ref, docs_ref, own, rows, key_block=KEY_BLOCK):
    half = rows // 2
    base = (pos_ref[Z] * 4 + pos_ref[Y]) * rows + jnp.where(own, pos_ref[CORE] * half, 0)
    lane = lax.broadcasted_iota(jnp.int32, (1, rows), 1)
    places = base + jnp.where(own, lax.rem(lane, half), lane)
    end = start = jnp.int32(0)
    starts = jnp.zeros((1, rows), jnp.int32)
    for j in range(docs_ref.shape[1]):
        length = docs_ref[pos_ref[X], j]
        end = end + length
        start = start + jnp.where(base >= end, length, 0)
        starts = starts + jnp.where(places >= end, length, 0)
    last = base + jnp.where(own, half, rows) - 1
    return places, starts, lax.div(start, key_block), lax.div(last, key_block) + 1


def attend_kernel(
    pos_ref, docs_ref, qt_ref, k_ref, vt_ref, ot_ref, lse_ref, *, first_set, scale, key_block
):
    units, head_dim, rows = qt_ref.shape
    own = pl.program_id(0) * units >= first_set
    places, starts, low, high = row_places(pos_ref, docs_ref, own, rows, key_block)

    def step(j, carry):
        begin = pl.multiple_of(j * key_block, key_block)
        keys = k_ref[pl.ds(begin, key_block), :]
        values = vt_ref[:, pl.ds(begin, key_block)]
        allowed = allowed_keys(begin, key_block, places, starts)
        out = []
        for u in range(units):
            top, mass, acc = carry[u]
            scores = jnp.dot(keys, qt_ref[u], preferred_element_type=F32)
            scores = jnp.where(allowed, scores, masked_fill)
            new_top = jnp.maximum(top, jnp.max(scores, axis=0, keepdims=True))
            weights = jnp.exp2((scores - new_top) * scale)
            shrink = jnp.exp2((top - new_top) * scale)
            mass = mass * shrink + jnp.sum(weights, axis=0, keepdims=True)
            acc = acc * shrink + jnp.dot(
                values, weights.astype(BF), preferred_element_type=F32
            )
            out.append((new_top, mass, acc))
        return tuple(out)

    start = (
        jnp.full((1, rows), masked_fill, F32),
        jnp.zeros((1, rows), F32),
        jnp.zeros((head_dim, rows), F32),
    )
    done = lax.fori_loop(low, high, step, (start,) * units)
    for u in range(units):
        top, mass, acc = done[u]
        ot_ref[u] = acc / mass
        lse_ref[u] = top * scale + jnp.log2(mass)


def attend(pos, docs, qt, keys, values_t, scale):
    units = 1
    blocks, head_dim, rows = qt.shape
    count = keys.shape[0]
    first_set = blocks // 2
    block = pl.BlockSpec((units, head_dim, rows), lambda i, p, d: (i, 0, 0))
    return pl.pallas_call(
        functools.partial(
            attend_kernel, first_set=first_set, scale=scale, key_block=2 * KEY_BLOCK
        ),
        grid_spec=pltpu.PrefetchScalarGridSpec(
            num_scalar_prefetch=2,
            grid=(blocks // units,),
            in_specs=[
                block,
                pl.BlockSpec((count, head_dim), lambda i, p, d: (0, 0)),
                pl.BlockSpec((head_dim, count), lambda i, p, d: (0, 0)),
            ],
            out_specs=[block, pl.BlockSpec((units, 1, rows), lambda i, p, d: (i, 0, 0))],
        ),
        out_shape=[
            jax.ShapeDtypeStruct((blocks, head_dim, rows), F32),
            jax.ShapeDtypeStruct((blocks, 1, rows), F32),
        ],
        compiler_params=pltpu.CompilerParams(vmem_limit_bytes=32 * MB),
        cost_estimate=SMALL,
        name="attend",
    )(pos, docs, qt, keys, values_t)


def attend_back_kernel(
    pos_ref, docs_ref, qt_ref, dot_ref, ot_ref, lse_ref, k_ref, kt_ref, v_ref,
    dqt_ref, mine_ref, give_ref, dk_ref, dv_ref, *, first_set, scale, score_scale,
):
    units, head_dim, rows = qt_ref.shape

    @pl.when(pl.program_id(0) == 0)
    def _():
        dk_ref[...] = jnp.zeros_like(dk_ref)
        dv_ref[...] = jnp.zeros_like(dv_ref)

    own = pl.program_id(0) * units >= first_set
    places, starts, low, high = row_places(pos_ref, docs_ref, own, rows)
    queries = [qt_ref[u].T for u in range(units)]
    d_outs = [dot_ref[u].T for u in range(units)]
    deltas = [
        jnp.sum(dot_ref[u].astype(F32) * ot_ref[u], axis=0, keepdims=True) for u in range(units)
    ]

    def step(j, carry):
        begin = pl.multiple_of(j * KEY_BLOCK, KEY_BLOCK)
        part = pl.ds(begin, KEY_BLOCK)
        allowed = allowed_keys(begin, KEY_BLOCK, places, starts)
        out = []
        d_keys = d_values = None
        for u in range(units):
            scores = jnp.dot(k_ref[part, :], qt_ref[u], preferred_element_type=F32)
            d_probs = jnp.dot(v_ref[part, :], dot_ref[u], preferred_element_type=F32)
            probs = jnp.where(allowed, jnp.exp2(scores * scale - lse_ref[u]), 0.0)
            d_scores = (probs * (d_probs - deltas[u])).astype(BF)
            for_keys = jnp.dot(d_scores, queries[u], preferred_element_type=F32)
            for_values = jnp.dot(probs.astype(BF), d_outs[u], preferred_element_type=F32)
            d_keys = for_keys if u == 0 else d_keys + for_keys
            d_values = for_values if u == 0 else d_values + for_values
            out.append(
                carry[u] + jnp.dot(kt_ref[:, part], d_scores, preferred_element_type=F32)
            )
        dk_ref[part, :] += d_keys
        dv_ref[part, :] += d_values
        return tuple(out)

    start = jnp.zeros((head_dim, rows), F32)
    done = lax.fori_loop(low, high, step, (start,) * units)
    for u in range(units):
        dqt_ref[u] = done[u] * score_scale

    @pl.when(pl.program_id(0) == pl.num_programs(0) - 1)
    def _():
        first = pos_ref[CORE] == 0
        d_keys, d_values = dk_ref[...] * score_scale, dv_ref[...]
        mine_ref[...] = jnp.where(first, d_keys, d_values)
        give_ref[...] = jnp.where(first, d_values, d_keys).astype(BF)


def attend_back(pos, docs, qt, d_out_t, out_t, lse, keys, keys_t, values, scale, score_scale):
    units = 2
    blocks, head_dim, rows = qt.shape
    count = keys.shape[0]
    first_set = blocks // 2
    block = pl.BlockSpec((units, head_dim, rows), lambda i, p, d: (i, 0, 0))
    whole = pl.BlockSpec((count, head_dim), lambda i, p, d: (0, 0))
    return pl.pallas_call(
        functools.partial(
            attend_back_kernel, first_set=first_set, scale=scale, score_scale=score_scale
        ),
        grid_spec=pltpu.PrefetchScalarGridSpec(
            num_scalar_prefetch=2,
            grid=(blocks // units,),
            in_specs=[
                block,
                block,
                block,
                pl.BlockSpec((units, 1, rows), lambda i, p, d: (i, 0, 0)),
                whole,
                pl.BlockSpec((head_dim, count), lambda i, p, d: (0, 0)),
                whole,
            ],
            out_specs=[block, whole, whole],
            scratch_shapes=[pltpu.VMEM((count, head_dim), F32)] * 2,
        ),
        out_shape=[
            jax.ShapeDtypeStruct((blocks, head_dim, rows), F32),
            jax.ShapeDtypeStruct((count, head_dim), F32),
            jax.ShapeDtypeStruct((count, head_dim), BF),
        ],
        compiler_params=pltpu.CompilerParams(vmem_limit_bytes=44 * MB),
        cost_estimate=SMALL,
        name="attend_back",
    )(pos, docs, qt, d_out_t, out_t, lse, keys, keys_t, values)


def doc_starts(lengths, places):
    ends = jnp.cumsum(lengths)
    passed = (places[:, None] >= ends[None, :]).astype(jnp.int32)
    return jnp.sum(passed * lengths[None, :], axis=1)


def rotate_rows(values, cosine, sine):
    half = values.shape[-1] // 2
    one, two = values[..., :half], values[..., half:]
    return jnp.concatenate([one * cosine - two * sine, two * cosine + one * sine], axis=-1)


def rotate_columns(values, cosine, sine):
    half = values.shape[1] // 2
    one, two = values[:, :half], values[:, half:]
    return jnp.concatenate([one * cosine - two * sine, two * cosine + one * sine], axis=1)


def head_blocks(array):
    toks, width = array.shape
    count = width // 256

    def kernel(array_ref, out_ref):
        for b in range(count):
            for i in range(2):
                at = (2 * b + i) * 128
                out_ref[b, :, i * toks : (i + 1) * toks] = array_ref[:, at : at + 128].T

    shape = jax.ShapeDtypeStruct((count, 128, 2 * toks), array.dtype)
    return call(kernel, "head_blocks", [VMEM_SPEC], VMEM_SPEC, shape)(array)


def head_blocks_back(blocks, begin):
    total, head_dim, wide = blocks.shape
    count, toks = total - begin, wide // 2

    def kernel(blocks_ref, out_ref):
        for b in range(count):
            for i in range(2):
                at = (2 * b + i) * 128
                out_ref[:, at : at + 128] = blocks_ref[b, :, i * toks : (i + 1) * toks].T

    shape = jax.ShapeDtypeStruct((toks, count * 256), blocks.dtype)
    spec = pl.BlockSpec((count, head_dim, wide), lambda i: (begin // count, 0, 0))
    return call(kernel, "head_blocks_back", [spec], VMEM_SPEC, shape)(blocks)


def on_device(
    tokens, doc_lengths, attn_gain, q_weight, kv_weight, out_weight, ffn_gain,
    gate_weight, up_weight, down_weight, second_queries, out_cotangent, second_cotangent,
):
    x, z, y, c = (lax.axis_index(a) for a in ("x", "z", "y", "c"))
    first = c == 0
    pos = jnp.stack([x, z, y, c]).astype(jnp.int32)
    toks, width = tokens.shape
    head_dim = kv_weight.shape[1] // 2
    score_scale = head_dim ** (-0.5)
    scale = score_scale * math.log2(math.e)
    rows = q_weight.shape[0]

    def swap(own):
        return fetch(own, "c", 1)

    n_q, n_kv = q_weight.shape[1] // 2, head_dim
    n_out, n_ffn = out_weight.shape[0] // 2, down_weight.shape[0] // 2
    n_attn = n_q + n_out
    at_out, at_kv = n_q // n_out, n_attn // n_kv
    attn_mine, attn_give, ffn_mine, ffn_give = prepared(
        pos, q_weight, out_weight.T, kv_weight, gate_weight, up_weight, down_weight.T,
        (attn_gain, ffn_gain),
    )
    attn_other, ffn_other, tokens_other, cot_other = tie(
        swap(attn_give), swap(ffn_give), swap(tokens), swap(out_cotangent)
    )
    attn_rows = across_x(attn_mine, attn_other)
    ffn_both = jnp.concatenate([ffn_mine, ffn_other], axis=0)
    blocks = first_blocks(attn_rows)
    ffn_got, *blocks = tie(fetch(ffn_both, "x", 1), *blocks[0], *blocks[1])
    ffn_rows = jnp.concatenate([ffn_both, ffn_got], axis=0)
    ffn_whole = lax.all_gather(ffn_rows, ("z", "y"), axis=0, tiled=True)
    attn_pair = second_pair([jnp.concatenate(b, axis=0) for b in (blocks[:4], blocks[4:])])
    attn_chunks = far_blocks(attn_pair, tie(*near_blocks(attn_pair)))
    attn_chunks = [jnp.concatenate(w, axis=0) if isinstance(w, tuple) else w for w in attn_chunks]
    def over_tp(rows):
        send = rows.astype(BF)
        return send.astype(F32) + fetch(send, "t", 1).astype(F32)

    def reduce_rows(own, other):
        return over_tp(own.astype(F32) + swap(other).astype(F32))

    places = (z * 4 + y) * (2 * toks) + jnp.arange(2 * toks, dtype=jnp.int32)
    starts = doc_starts(jnp.where(x == 0, doc_lengths[0], doc_lengths[1]), places)
    positions = (places - starts).astype(F32)
    inverse_freq = jnp.exp(
        jnp.arange(head_dim // 2, dtype=F32) * (-2.0 * math.log(rope_base) / head_dim)
    )
    angles_t = inverse_freq[:, None] * positions[None, :]
    cos_t, sin_t = jnp.cos(angles_t), jnp.sin(angles_t)

    inputs = tokens.astype(F32)
    inv_attn = lax.rsqrt(jnp.mean(inputs * inputs, axis=-1, keepdims=True) + norm_eps)
    second_t, second_cot_t = head_blocks(second_queries), head_blocks(second_cotangent)
    cot_t = turned(pos, out_cotangent, cot_other, whole=True)
    cos_r, sin_r = cos_t.T, sin_t.T
    normed_t, gain_rows, keyval = normed_rows(pos, tokens, tokens_other, attn_chunks, n_kv, at_kv)
    gain_one, gain_two = gain_rows[0:1], gain_rows[1:2]
    kv_own = jnp.where(first, rotate_rows(keyval, cos_r, sin_r), keyval).astype(BF)
    kv_sent = jnp.broadcast_to(kv_own[None], (16,) + kv_own.shape)
    kv_all = lax.all_to_all(kv_sent, ("z", "y"), 0, 0).reshape(-1, head_dim)
    queries_t = project(normed_t, attn_chunks, n_q, 0, F32)
    query_rot = rotate_columns(queries_t.reshape(-1, head_dim, 2 * toks), cos_t, sin_t).astype(BF)
    keys, values, keys_t, values_t = arranged(pos, kv_all, swap(kv_all))
    query_t = jnp.concatenate([query_rot, second_t], axis=0)
    out_t, lse = attend(pos, doc_lengths, query_t, keys, values_t, scale)
    n_first = query_rot.shape[0]
    second_out = head_blocks_back(out_t, n_first)
    attended_t = out_t[:n_first].reshape(-1, 2 * toks).astype(BF)

    branch = reduce_rows(*unproject(pos, [(attn_chunks, at_out, attended_t, False)]))
    resid = inputs + branch
    inv_ffn = lax.rsqrt(jnp.mean(resid * resid, axis=-1, keepdims=True) + norm_eps)
    normed2 = (resid * inv_ffn * gain_two).astype(BF)
    normed2_t = turned(pos, normed2, swap(normed2), whole=True)
    ffn_grads, d_norm2_part, ffn_part = feed_forward(pos, normed2_t, cot_t, ffn_whole)
    ffn_share = lax.psum_scatter(ffn_grads, ("z", "y"), scatter_dimension=0, tiled=True)
    d_normed2 = reduce_rows(*d_norm2_part)

    scaled_two = gain_two * d_normed2
    ffn_gain_part = jnp.sum(d_normed2 * resid * inv_ffn, axis=0)
    d_resid = (
        out_cotangent.astype(F32)
        + inv_ffn * scaled_two
        - resid * inv_ffn**3 * jnp.mean(scaled_two * resid, axis=-1, keepdims=True)
    )
    d_branch = d_resid.astype(BF)

    d_branch_t = turned(pos, d_branch, swap(d_branch))
    d_attended_t = project(d_branch_t, attn_chunks, n_out, at_out, BF)
    d_out_t = jnp.concatenate(
        [d_attended_t.reshape(-1, head_dim, 2 * toks), second_cot_t], axis=0
    )
    d_query_t, kv_mine, kv_give = attend_back(
        pos, doc_lengths, query_t, d_out_t, out_t, lse, keys, keys_t, values, scale, score_scale
    )
    kv_give, d_query_t, *ffn_part = tie(kv_give, d_query_t, *ffn_part)
    ffn_sum = reduce_rows(*ffn_part)
    kv_other = swap(kv_give)
    second_queries_grad = head_blocks_back(d_query_t, n_first)
    d_queries_t = rotate_columns(d_query_t[:n_first], cos_t, -sin_t).reshape(-1, 2 * toks).astype(BF)

    attn_grads = weight_chunks([(normed_t, d_queries_t, True), (d_branch_t, attended_t, True)])
    kv_chip = (kv_mine + kv_other.astype(F32)).astype(BF).reshape(16, 2 * toks, head_dim)
    kv_chip, *attn_grads = tie(kv_chip, *attn_grads)
    kv_parts = lax.all_to_all(kv_chip, ("z", "y"), 0, 0)
    attn_terms = scatter_first(attn_grads)
    near = (1, 3, 5, 7)
    kv_parts, ffn_sum, *got = tie(kv_parts, ffn_sum, *[attn_terms[i] for i in near])
    for i, term in zip(near, got):
        attn_terms[i] = term
    kv_sum = jnp.sum(kv_parts.astype(F32), axis=0)
    result = resid + ffn_sum
    d_keyval = jnp.where(first, rotate_rows(kv_sum, cos_r, -sin_r), kv_sum).astype(BF)
    d_norm_part = unproject(
        pos, [(attn_chunks, 0, d_queries_t, False), (attn_chunks, at_kv, d_keyval, True)]
    )
    d_norm_other = swap(d_norm_part[1])
    d_normed = over_tp(d_norm_part[0].astype(F32) + d_norm_other.astype(F32))
    kv_grads = key_gradients(
        pos, normed_t, d_keyval, tokens, d_norm_part[0], d_norm_other, ffn_gain_part[None]
    )
    kv_got = lax.all_to_all(kv_grads.reshape(32, 2, rows, -1), ("x", "z", "y"), 0, 0)
    kv_got, *attn_terms = tie(kv_got, *attn_terms)
    ffn_got = fetch(ffn_share[64:], "x", 1)
    attn_share, attn_give, ffn_got = scatter_second(attn_terms, ffn_got)
    ffn_sums = ffn_share[:64].astype(F32) + ffn_got.astype(F32)
    kv_share = jnp.sum(kv_got.astype(F32), axis=0)
    scaled_one = gain_one * d_normed
    tokens_grad = (
        d_resid
        + inv_attn * scaled_one
        - inputs * inv_attn**3 * jnp.mean(scaled_one * inputs, axis=-1, keepdims=True)
    )

    gate_grad, up_grad, down_grad_t = unpacked(
        pos,
        ffn_sums[:32],
        swap(ffn_sums[32:]),
        [[(b + i * w, w) for b, unit, w in tile_columns(n_ffn)] for i in range(3)],
    )
    q_grad, out_grad_t = unpacked(pos, attn_share, swap(attn_give), [[(0, n_q)], [(n_q, n_out)]])
    kv_mine, kv_give = (jnp.where(first, kv_share[i], kv_share[1 - i]) for i in (0, 1))
    kv_other = swap(kv_give)
    kv_gain = jnp.concatenate(
        [
            in_order(first, kv_mine[:, :n_kv], kv_other[:, :n_kv], 1),
            kv_mine[:, n_kv:] + kv_other[:, n_kv:],
        ],
        axis=1,
    )
    kv_gain = kv_gain + fetch(kv_gain, "t", 1)
    return (
        result,
        second_out,
        tokens_grad,
        kv_gain[:, 2 * n_kv],
        q_grad,
        kv_gain[:, : 2 * n_kv],
        out_grad_t.T,
        kv_gain[:, 2 * n_kv + 1],
        gate_grad,
        up_grad,
        down_grad_t.T,
        second_queries_grad,
    )


def solution(mesh):
    fine = Mesh(mesh.devices.reshape(2, 4, 4, 2, 2), ("x", "z", "y", "c", "t"))
    seq = ("x", "z", "y", "c")
    rows, both, turned_both = P(seq, None), P(seq, "t"), P("t", seq)
    in_specs = (
        rows, P(), P(seq), both, rows, turned_both, P(seq), both, both, turned_both, both, rows, both,
    )
    out_specs = (
        rows, both, rows, P(seq), both, rows, turned_both, P(seq), both, both, turned_both, both,
    )
    return jax.shard_map(
        on_device, mesh=fine, in_specs=in_specs, out_specs=out_specs, check_vma=False
    )
```
